512 devices in a mesh: chan: 128 (over x, y_lo, z), slab: 4 (over y_hi, core).
Axes of the slice: x: 4, y: 4 (y_hi: 2, y_lo: 2; y = y_hi * 2 + y_lo), z: 16, core: 2. Of those that a mesh axis runs over, the one named last changes fastest.
Arguments:
- volume_now: float32 [1024, 4, 16, 512], P('chan', 'slab'), may hold values from 0.05 to 22
- extrapolated: float32 [1024, 4, 16, 512], P('chan', 'slab'), may hold values from -5 to 24
- dual_grad: float32 [3, 1024, 4, 16, 512], P(None, 'chan', 'slab'), may hold values from -3 to 3
- dual_data: float32 [1024, 4, 4096], P('chan', 'slab'), may hold values from -6 to 6
- measured: float32 [1024, 4, 4096], P('chan', 'slab'), may hold values from -6 to 18
- projector: bfloat16 [64, 128, 128], replicated, may hold values from -0.375 to 0.375
- tile_rows: int32 [64], replicated, may hold values from 0 to 31
- tile_cols: int32 [64], replicated, may hold values from 0 to 63
- dual_step: float32 [1], replicated, may hold values from 0.3 to 0.6
- primal_step: float32 [1], replicated, may hold values from 0.2 to 0.5
- reg_weight: float32 [1], replicated, may hold values from 1.2 to 2.4
Outputs:
- updated: float32 [1024, 4, 16, 512], P('chan', 'slab')
- dual_grad_new: float32 [3, 1024, 4, 16, 512], P(None, 'chan', 'slab')
- dual_data_new: float32 [1024, 4, 4096], P('chan', 'slab')
- totals: float32 [2], replicated
The draws below stay inside these ranges and needn't reach their ends.
Inputs may be any that keep to these rules, and one draw needn't show every extreme that they name: `tile_rows`: ray block of each tile; several tiles may share a block. `tile_cols`: pixel block of each tile, blocks counted along the row-by-row pixel order.
All inputs are finite; a program needn't handle non-finite values.
Results may differ from the reference program's by a relative error of at most 0.002.
Values sent between devices are 32-bit elements; how exact they have to be, the bound alone decides.
No kernel may reach another device: no remote copies, remote signals or barrier semaphores. Data moves between devices by JAX's collectives and lax.ppermute only.
A program may use at most 64 MiB of HBM per device.

```python
import math
import jax
import jax.numpy as jnp
from jax import lax

CHANNELS = 1024
SLICES = 4
NR = 16
NC = 512
PIX = 8192
TILE = 128
COL_BLOCKS = 64
ROW_BLOCKS = 32
RAYS = 4096
TILES = 64
SWEEPS = 6


def level_field():
    channel = 1.0 + jnp.arange(CHANNELS, dtype=jnp.float32) / max(CHANNELS - 1, 1)
    depth = 1.0 + jnp.arange(SLICES, dtype=jnp.float32) / max(SLICES - 1, 1)
    height = 1.0 + 2.0 * jnp.arange(NR, dtype=jnp.float32) / max(NR - 1, 1)
    return channel[:, None, None, None] * depth[None, :, None, None] * height[None, None, :, None]


def draw_volume_now(key, part):
    noise = jax.random.uniform(jax.random.fold_in(key, 11), (CHANNELS, SLICES, NR, NC), jnp.float32, 0.2, 1.8)
    return level_field() * noise


def draw_extrapolated(key, part):
    noise = jax.random.uniform(jax.random.fold_in(key, 13), (CHANNELS, SLICES, NR, NC), jnp.float32, -0.4, 2.0)
    return level_field() * noise


def draw_measured(key, part):
    channel = 1.0 + jnp.arange(CHANNELS, dtype=jnp.float32) / max(CHANNELS - 1, 1)
    depth = 1.0 + jnp.arange(SLICES, dtype=jnp.float32) / max(SLICES - 1, 1)
    level = channel[:, None, None] * depth[None, :, None]
    noise = jax.random.uniform(jax.random.fold_in(key, 17), (CHANNELS, SLICES, RAYS), jnp.float32, -1.0, 3.0)
    return 1.5 * level * noise


def with_ends(values, own_key, least, top_value):
    longest = values.shape.index(max(values.shape))
    spots = []
    for shift in (0, 1):
        where = [jax.random.randint(jax.random.fold_in(own_key, axis), (), 0, length) for axis, length in enumerate(values.shape)]
        where[longest] = (where[longest] + shift) % values.shape[longest]
        spots.append(tuple(where))
    return values.at[spots[0]].set(least).at[spots[1]].set(top_value)


def steps_of(stream_key, extent, shards, least, top_value):
    loudness = 1.0
    for dim, shards_of in shards:
        heights = jax.random.uniform(jax.random.fold_in(jax.random.fold_in(stream_key, 6), dim), (shards_of,), jnp.float32, least / len(shards), top_value / len(shards))
        loudness = loudness * jnp.repeat(jnp.exp(heights), extent[dim] // shards_of).reshape((-1,) + (1,) * (len(extent) - 1 - dim))
    return loudness


def gaussian(key, shape, spread, limit, split=(), held_as=jnp.bfloat16):
    values = spread * jax.random.normal(key, shape, jnp.float32)
    if split:
        values = values * steps_of(key, shape, split, -0.22, 0.18)
    return jnp.clip(values, -limit, limit).astype(held_as)


def setup_inputs(seed: int = 0) -> dict:
    seeds = jax.random.split(jax.random.key(seed), 12)
    return {
        "volume_now": draw_volume_now(jax.random.fold_in(seeds[11], 71), 0),
        "extrapolated": draw_extrapolated(jax.random.fold_in(seeds[11], 71), 0),
        "dual_grad": gaussian(seeds[2], (3, CHANNELS, SLICES, NR, NC), 0.5, 3.0, ((1, 128), (2, 4)), jnp.float32),
        "dual_data": gaussian(seeds[3], (CHANNELS, SLICES, RAYS), 1.0, 6.0, ((0, 128), (1, 4)), jnp.float32),
        "measured": draw_measured(jax.random.fold_in(seeds[11], 71), 0),
        "projector": gaussian(seeds[5], (TILES, TILE, TILE), (TILE * TILES // ROW_BLOCKS) ** -0.5, 0.375),
        "tile_rows": with_ends(jax.random.randint(seeds[6], (TILES,), 0, ROW_BLOCKS), jax.random.fold_in(seeds[6], 1), 0, ROW_BLOCKS - 1).astype(jnp.int32),
        "tile_cols": with_ends(jax.random.randint(seeds[7], (TILES,), 0, COL_BLOCKS), jax.random.fold_in(seeds[7], 1), 0, COL_BLOCKS - 1).astype(jnp.int32),
        "dual_step": jnp.clip(jnp.exp(jax.random.uniform(seeds[8], (1,), jnp.float32, math.log(0.3), math.log(0.6))), 0.3, 0.6),
        "primal_step": jnp.clip(jnp.exp(jax.random.uniform(seeds[9], (1,), jnp.float32, math.log(0.2), math.log(0.5))), 0.2, 0.5),
        "reg_weight": jnp.clip(jnp.exp(jax.random.uniform(seeds[10], (1,), jnp.float32, math.log(1.2), math.log(2.4))), 1.2, 2.4),
    }


index_pairs = ((0, 0), (1, 1), (2, 2), (0, 1), (0, 2), (1, 2))
sweep_order = ((0, 1), (0, 2), (1, 2))

def rotate_columns(matrix, first_idx, second_idx, cosine, sine_value):
    result = [list(row) for row in matrix]
    for row_idx in range(3):
        left_val = matrix[row_idx][first_idx]
        right_val = matrix[row_idx][second_idx]
        result[row_idx][first_idx] = cosine * left_val - sine_value * right_val
        result[row_idx][second_idx] = sine_value * left_val + cosine * right_val
    return result

def rotate_rows(matrix, first_idx, second_idx, cosine, sine_value):
    result = [list(row) for row in matrix]
    for col_idx in range(3):
        upper_val = matrix[first_idx][col_idx]
        lower_val = matrix[second_idx][col_idx]
        result[first_idx][col_idx] = cosine * upper_val - sine_value * lower_val
        result[second_idx][col_idx] = sine_value * upper_val + cosine * lower_val
    return result

def unpack(entry_list):
    return [[entry_list[0], entry_list[3], entry_list[4]], [entry_list[3], entry_list[1], entry_list[5]], [entry_list[4], entry_list[5], entry_list[2]]]

def spectral_factor(matrix, radius):
    vectors = [[1.0 if row_idx == col_idx else 0.0 for col_idx in range(3)] for row_idx in range(3)]
    for sweep_idx in range(SWEEPS):
        for first_idx, second_idx in sweep_order:
            angle_half = 0.5 * jnp.arctan2(2.0 * matrix[first_idx][second_idx], matrix[second_idx][second_idx] - matrix[first_idx][first_idx])
            cosine = jnp.cos(angle_half)
            sine_value = jnp.sin(angle_half)
            matrix = rotate_rows(rotate_columns(matrix, first_idx, second_idx, cosine, sine_value), first_idx, second_idx, cosine, sine_value)
            vectors = rotate_columns(vectors, first_idx, second_idx, cosine, sine_value)
    root_values = [jnp.sqrt(jnp.maximum(matrix[diag_idx][diag_idx], 0.0)) for diag_idx in range(3)]
    scales = [radius / jnp.maximum(root_values[diag_idx], radius) for diag_idx in range(3)]
    factor = [[vectors[row_idx][0] * scales[0] * vectors[col_idx][0] + vectors[row_idx][1] * scales[1] * vectors[col_idx][1] + vectors[row_idx][2] * scales[2] * vectors[col_idx][2] for col_idx in range(3)] for row_idx in range(3)]
    excess = (jnp.maximum(root_values[0] - radius, 0.0) + jnp.maximum(root_values[1] - radius, 0.0) + jnp.maximum(root_values[2] - radius, 0.0)) / radius
    return (factor, excess)

def apply_factor(candidate, matrix):
    return jnp.stack([candidate[0] * matrix[0][col_idx] + candidate[1] * matrix[1][col_idx] + candidate[2] * matrix[2][col_idx] for col_idx in range(3)])

def forward_difference(volume, along_axis):
    length = volume.shape[along_axis]
    later = lax.slice_in_dim(volume, 1, length, axis=along_axis)
    kept_part = lax.slice_in_dim(volume, 0, length - 1, axis=along_axis)
    zero_layer = jnp.zeros_like(lax.slice_in_dim(volume, 0, 1, axis=along_axis))
    return jnp.concatenate([later - kept_part, zero_layer], axis=along_axis)

def backward_difference(component, along_axis):
    length = component.shape[along_axis]
    kept_part = lax.slice_in_dim(component, 0, length - 1, axis=along_axis)
    zero_layer = jnp.zeros_like(lax.slice_in_dim(component, 0, 1, axis=along_axis))
    masked = jnp.concatenate([kept_part, zero_layer], axis=along_axis)
    earlier = jnp.concatenate([zero_layer, kept_part], axis=along_axis)
    return masked - earlier

def project_forward(rounded, projector, tile_rows, tile_cols):
    channels, slices, pixels = rounded.shape
    tile_edge = projector.shape[1]
    blocks = rounded.reshape(channels * slices, pixels // tile_edge, tile_edge)
    picked = jnp.take(blocks, tile_cols, axis=1)
    products = jnp.einsum('tij,btj->bti', projector.astype(jnp.float32), picked.astype(jnp.float32), precision=lax.Precision.HIGHEST)
    selector = (tile_rows[:, None] == jnp.arange(ROW_BLOCKS, dtype=jnp.int32)[None, :]).astype(jnp.float32)
    sinogram = jnp.einsum('tr,bti->bri', selector, products, precision=lax.Precision.HIGHEST)
    return sinogram.reshape(channels, slices, ROW_BLOCKS * tile_edge)

def project_back(data_low, projector, tile_rows, tile_cols):
    channels, slices, rays = data_low.shape
    tile_edge = projector.shape[1]
    blocks = data_low.reshape(channels * slices, rays // tile_edge, tile_edge)
    picked = jnp.take(blocks, tile_rows, axis=1)
    products = jnp.einsum('tij,bti->btj', projector.astype(jnp.float32), picked.astype(jnp.float32), precision=lax.Precision.HIGHEST)
    selector = (tile_cols[:, None] == jnp.arange(COL_BLOCKS, dtype=jnp.int32)[None, :]).astype(jnp.float32)
    volume = jnp.einsum('tc,btj->bcj', selector, products, precision=lax.Precision.HIGHEST)
    return volume.reshape(channels, slices, COL_BLOCKS * tile_edge)

def reference(volume_now, extrapolated, dual_grad, dual_data, measured, projector, tile_rows, tile_cols, dual_step, primal_step, reg_weight):
    dual_rate = dual_step[0]
    primal_rate = primal_step[0]
    rounded = lax.optimization_barrier(extrapolated.reshape(CHANNELS, SLICES, PIX).astype(jnp.bfloat16))
    projected = project_forward(rounded, projector, tile_rows, tile_cols)
    residual = projected - measured
    data_new = (dual_data + dual_rate * residual) / (1.0 + dual_rate)
    gradient = jnp.stack([forward_difference(extrapolated, 2), forward_difference(extrapolated, 3), forward_difference(extrapolated, 1)])
    candidate = dual_grad + dual_rate * gradient
    gram = [lax.optimization_barrier(jnp.sum(candidate[first_idx] * candidate[second_idx], axis=0)) for first_idx, second_idx in index_pairs]
    radius = reg_weight[0] * math.sqrt(CHANNELS)
    factor, excess = spectral_factor(unpack(gram), radius)
    grad_new = apply_factor(candidate, factor)
    divergence = backward_difference(grad_new[0], 2) + backward_difference(grad_new[1], 3) + backward_difference(grad_new[2], 1)
    data_low = lax.optimization_barrier(data_new.astype(jnp.bfloat16))
    back_proj = project_back(data_low, projector, tile_rows, tile_cols).reshape(volume_now.shape)
    updated = jnp.maximum(volume_now - primal_rate * (back_proj - divergence), 0.0)
    totals = jnp.stack([jnp.mean(residual * residual), jnp.mean(excess)])
    return (updated, grad_new, data_new, totals)
```

```python
import math

import jax
import jax.numpy as jnp
from jax import lax
from jax.experimental import pallas as pl
from jax.experimental.pallas import tpu as pltpu
from jax.sharding import Mesh
from jax.sharding import PartitionSpec as P

SWEEPS = 6
CHAN = ("x", "y", "zfar", "znear")
SHARE = ("x", "y", "znear")
FAR = "zfar"
LANES = 128

index_pairs = ((0, 0), (1, 1), (2, 2), (0, 1), (0, 2), (1, 2))
entry_of = {pair: k for k, pair in enumerate(index_pairs)}
sweep_order = ((0, 1), (0, 2), (1, 2))

VMEM = pl.BlockSpec(memory_space=pltpu.VMEM)
SMEM = pl.BlockSpec(memory_space=pltpu.SMEM)


def from_behind(block, axis, distance):
    devices = range(lax.axis_size(axis))
    route = [(i - distance, i) for i in devices if i - distance in devices]
    return lax.ppermute(block, axis, route)


def gram_kernel(rate_ref, keep_ref, x_ref, next_ref, dual_ref, cand_ref, out_ref):
    channels, rows, cols = x_ref.shape
    tiles = cols // LANES
    per_row = len(index_pairs) * tiles
    rate = rate_ref[0]
    keep = keep_ref[0]
    row_id = lax.broadcasted_iota(jnp.int32, (rows, LANES), 0)
    lane_id = lax.broadcasted_iota(jnp.int32, (rows, LANES), 1)
    inner_row = row_id < rows - 1
    edge_lane = lane_id == LANES - 1
    for j in range(tiles):
        here = pl.ds(j * LANES, LANES)
        sums = [jnp.zeros((rows, LANES), jnp.float32) for _ in index_pairs]
        for c in range(channels):
            x = x_ref[c, :, here]
            below = pltpu.roll(x, rows - 1, 0)
            right = pltpu.roll(x, LANES - 1, 1)
            if j + 1 < tiles:
                after = pltpu.roll(x_ref[c, :, pl.ds((j + 1) * LANES, LANES)], LANES - 1, 1)
            else:
                after = x
            steps = (
                jnp.where(inner_row, below - x, 0.0),
                jnp.where(edge_lane, after, right) - x,
                (next_ref[c, :, here] - x) * keep,
            )
            cand = [dual_ref[a, c, :, here] + rate * steps[a] for a in range(3)]
            for a in range(3):
                cand_ref[a, c, :, here] = cand[a]
            sums = [s + cand[a] * cand[b] for s, (a, b) in zip(sums, index_pairs)]
        for k, s in enumerate(sums):
            out_ref[pl.ds(k * tiles + j, rows, stride=per_row), :] = s


def pass_on_kernel(parts_ref, misfit_ref, out_ref):
    peers, per_row, _ = parts_ref.shape
    total = parts_ref[0]
    for p in range(1, peers):
        total = total + parts_ref[p]
    misfit = misfit_ref[...]
    for p in range(out_ref.shape[0]):
        out_ref[p, :per_row, :] = total
        out_ref[p, per_row:, :] = misfit


def rotate(entry, vectors, p, q):
    k = 3 - p - q
    pq, kp, kq = (entry_of[tuple(sorted(s))] for s in ((p, q), (k, p), (k, q)))
    across, twice = entry[q] - entry[p], 2.0 * entry[pq]
    square = across * across + twice * twice
    still = square == 0.0
    inverse = lax.rsqrt(jnp.where(still, 1.0, square))
    length = square * inverse
    half = jnp.where(still, 1.0, 0.5 + 0.5 * jnp.abs(across) * inverse)
    root = lax.rsqrt(half)
    large, small = half * root, 0.5 * jnp.abs(twice) * inverse * root
    ahead = across >= 0.0
    cosine = jnp.where(ahead, large, small)
    sine = jnp.where(ahead, small, large)
    sine = jnp.where(twice < 0.0, -sine, sine)
    middle = entry[p] + entry[q]
    entry, vectors = list(entry), [list(row) for row in vectors]
    entry[p], entry[q] = 0.5 * (middle - length), 0.5 * (middle + length)
    entry[pq] = jnp.where(still, entry[pq], 0.0)
    entry[kp], entry[kq] = (
        cosine * entry[kp] - sine * entry[kq],
        sine * entry[kp] + cosine * entry[kq],
    )
    for row in vectors:
        row[p], row[q] = cosine * row[p] - sine * row[q], sine * row[p] + cosine * row[q]
    return entry, vectors


def factor_kernel(radius_ref, parts_ref, out_ref):
    peers, held, _ = parts_ref.shape
    tiles = out_ref.shape[1] // 8
    entries = len(index_pairs)

    def summed(start, size):
        total = parts_ref[0, pl.ds(start, size), :]
        for p in range(1, peers):
            total = total + parts_ref[p, pl.ds(start, size), :]
        return total

    radius = radius_ref[0]
    entry = [summed(k * tiles, tiles) for k in range(entries)]
    one, zero = jnp.ones_like(entry[0]), jnp.zeros_like(entry[0])
    vectors = [[one if r == c else zero for c in range(3)] for r in range(3)]
    for _ in range(SWEEPS):
        for p, q in sweep_order:
            entry, vectors = rotate(entry, vectors, p, q)
    roots = [jnp.sqrt(jnp.maximum(entry[d], 0.0)) for d in range(3)]
    scales = [radius / jnp.maximum(root, radius) for root in roots]
    excess = sum(jnp.maximum(root - radius, 0.0) for root in roots) / radius
    misfit = sum(summed(k, tiles) for k in range(entries * tiles, held, tiles))
    rows = [
        sum(vectors[a][d] * scales[d] * vectors[b][d] for d in range(3)) for a, b in index_pairs
    ] + [excess, misfit]
    for p in range(out_ref.shape[0]):
        for k, row in enumerate(rows):
            out_ref[p, pl.ds(k * tiles, tiles), :] = row


def apply_kernel(factor_ref, cand_ref, new_ref, send_ref, sums_ref):
    _, channels, rows, cols = cand_ref.shape
    tiles = cols // LANES
    entries = len(index_pairs)
    per_row = factor_ref.shape[0] // rows

    def image(k, j):
        return factor_ref[pl.ds(k * tiles + j, rows, stride=per_row), :]

    for k in range(2):
        sums_ref[k] = sum(image(entries + k, j) for j in range(tiles))
    for j in range(tiles):
        here = pl.ds(j * LANES, LANES)
        factor = [image(k, j) for k in range(entries)]
        for c in range(channels):
            cand = [cand_ref[a, c, :, here] for a in range(3)]
            for a in (2, 1, 0):
                new = sum(cand[b] * factor[entry_of[tuple(sorted((b, a)))]] for b in range(3))
                new_ref[a, c, :, here] = new
                if a == 2:
                    send_ref[c, :, here] = new


def backward_difference(component, along_axis):
    length = component.shape[along_axis]
    kept_part = lax.slice_in_dim(component, 0, length - 1, axis=along_axis)
    zero_layer = jnp.zeros_like(lax.slice_in_dim(component, 0, 1, axis=along_axis))
    masked = jnp.concatenate([kept_part, zero_layer], axis=along_axis)
    earlier = jnp.concatenate([zero_layer, kept_part], axis=along_axis)
    return masked - earlier


def picked_blocks(blocks, where, count):
    chosen = (where[:, None] == jnp.arange(count, dtype=jnp.int32)[None, :]).astype(jnp.bfloat16)
    return jnp.einsum("tc,bcj->tbj", chosen, blocks, preferred_element_type=jnp.float32).astype(
        jnp.bfloat16
    )


def gathered_products(products, where, count):
    chosen = (where[:, None] == jnp.arange(count, dtype=jnp.int32)[None, :]).astype(jnp.float32)
    return jnp.einsum("tc,tbj->bcj", chosen, products, precision=lax.Precision.HIGHEST)


def on_device(
    volume_now,
    extrapolated,
    dual_grad,
    dual_data,
    measured,
    projector,
    tile_rows,
    tile_cols,
    dual_step,
    primal_step,
    reg_weight,
):
    f32 = jnp.float32
    dual_rate = dual_step[0]
    primal_rate = primal_step[0]
    channels, slices, row_count, col_count = volume_now.shape
    pixels = row_count * col_count
    rays = dual_data.shape[2]
    edge = projector.shape[1]
    share_count, far_count = lax.axis_size(SHARE), lax.axis_size(FAR)
    slab_count = lax.axis_size("slab")
    total_channels = channels * share_count * far_count
    tiles = col_count // LANES
    held = len(index_pairs) * tiles
    last_slice = lax.axis_index("slab") == slab_count - 1
    images = (channels, row_count, col_count)

    following = from_behind(extrapolated, "slab", -1)
    keep = jnp.where(last_slice, 0.0, 1.0).reshape(1)
    candidate, partial_gram = pl.pallas_call(
        gram_kernel,
        out_shape=(
            jax.ShapeDtypeStruct((3, *images), f32),
            jax.ShapeDtypeStruct((row_count * held, LANES), f32),
        ),
        in_specs=[SMEM, SMEM, VMEM, VMEM, VMEM],
        out_specs=(VMEM, VMEM),
        name="gram",
    )(
        dual_step,
        keep,
        extrapolated.reshape(images),
        following.reshape(images),
        dual_grad.reshape(3, *images),
    )
    gram_parts = lax.all_to_all(
        partial_gram.reshape(share_count, held, LANES), SHARE, 0, 0, tiled=True
    )

    rounded = extrapolated.reshape(channels, pixels // edge, edge).astype(jnp.bfloat16)
    picked = picked_blocks(rounded, tile_cols, pixels // edge)
    products = jnp.einsum("tij,tbj->tbi", projector, picked, preferred_element_type=f32)
    projected = gathered_products(products, tile_rows, rays // edge)
    residual = projected - measured.reshape(projected.shape)
    data_new = (dual_data.reshape(projected.shape) + dual_rate * residual) / (1.0 + dual_rate)
    misfit_part = jnp.sum((residual * residual).reshape(-1, 8, LANES), axis=0)

    to_far = pl.pallas_call(
        pass_on_kernel,
        out_shape=jax.ShapeDtypeStruct((far_count, held + 8, LANES), f32),
        in_specs=[VMEM, VMEM],
        out_specs=VMEM,
        name="pass_on",
    )(gram_parts, misfit_part)
    far_parts = lax.all_to_all(to_far, FAR, 0, 0, tiled=True)

    data_low = data_new.astype(jnp.bfloat16)
    picked_back = picked_blocks(data_low, tile_rows, rays // edge)
    products_back = jnp.einsum("tij,tbi->tbj", projector, picked_back, preferred_element_type=f32)
    back_proj = gathered_products(products_back, tile_cols, pixels // edge).reshape(
        volume_now.shape
    )

    radius = reg_weight * math.sqrt(total_channels)
    to_share = pl.pallas_call(
        factor_kernel,
        out_shape=jax.ShapeDtypeStruct((share_count, 8 * tiles, LANES), f32),
        in_specs=[SMEM, VMEM],
        out_specs=VMEM,
        name="factor",
    )(radius, far_parts)
    factor_rows = lax.all_to_all(to_share, SHARE, 0, 0, tiled=True)

    grad_new, to_next, sums = pl.pallas_call(
        apply_kernel,
        out_shape=(
            jax.ShapeDtypeStruct((3, *images), f32),
            jax.ShapeDtypeStruct(images, f32),
            jax.ShapeDtypeStruct((2, row_count, LANES), f32),
        ),
        in_specs=[VMEM, VMEM],
        out_specs=(VMEM, VMEM, VMEM),
        name="apply",
    )(factor_rows.reshape(share_count * 8 * tiles, LANES), candidate)
    prior_layer = from_behind(to_next, "slab", 1)

    sums = jnp.broadcast_to(sums.sum(axis=(1, 2))[None, :, None], (slab_count, 2, LANES))
    combined = lax.all_to_all(sums, "slab", 0, 0, tiled=True)[:, :, 0].sum(axis=0)

    masked = jnp.where(last_slice, 0.0, to_next)
    ready = volume_now.reshape(images) - primal_rate * (
        back_proj.reshape(images)
        - (backward_difference(grad_new[0], 1) + backward_difference(grad_new[1], 2) + masked)
    )
    updated = jnp.maximum(ready - primal_rate * prior_layer, 0.0)
    totals = jnp.stack(
        [
            combined[1] / (total_channels * slab_count * slices * rays),
            combined[0] / (slab_count * slices * pixels),
        ]
    )
    return (
        updated.reshape(volume_now.shape),
        grad_new.reshape(dual_grad.shape),
        data_new.reshape(dual_data.shape),
        totals,
    )


def solution(mesh):
    torus = Mesh(
        mesh.devices.reshape(4, 2, 8, 2, mesh.shape["slab"]), ("x", "y", "zfar", "znear", "slab")
    )
    placed = (
        P(CHAN, "slab", None, None),
        P(CHAN, "slab", None, None),
        P(None, CHAN, "slab", None, None),
        P(CHAN, "slab", None),
        P(CHAN, "slab", None),
        P(),
        P(),
        P(),
        P(),
        P(),
        P(),
    )
    return jax.shard_map(
        on_device,
        mesh=torus,
        in_specs=placed,
        out_specs=(
            P(CHAN, "slab", None, None),
            P(None, CHAN, "slab", None, None),
            P(CHAN, "slab", None),
            P(),
        ),
        check_vma=False,
    )
```

```python
import functools
import math

import jax
import jax.numpy as jnp
from jax import lax
from jax.experimental import pallas as pl
from jax.experimental.pallas import tpu as pltpu
from jax.sharding import Mesh
from jax.sharding import PartitionSpec as P

SWEEPS = 6
CHAN = ("x", "y", "zfar", "znear")
SHARE = ("x", "y", "znear")
FAR = "zfar"
LANES = 128

index_pairs = ((0, 0), (1, 1), (2, 2), (0, 1), (0, 2), (1, 2))
entry_of = {pair: k for k, pair in enumerate(index_pairs)}
sweep_order = ((0, 1), (0, 2), (1, 2))
own_pairs = ((0, 0), (1, 1), (0, 1))

VMEM = pl.BlockSpec(memory_space=pltpu.VMEM)
SMEM = pl.BlockSpec(memory_space=pltpu.SMEM)


def near(array):
    return pltpu.with_memory_space_constraint(array, pltpu.VMEM)


def kept_near(shape):
    return pltpu.VMEM(shape, jnp.float32)


def from_behind(block, axis, distance):
    devices = range(lax.axis_size(axis))
    route = [(i - distance, i) for i in devices if i - distance in devices]
    return lax.ppermute(block, axis, route)


def own_kernel(rate_ref, x_ref, dual_ref, cand_ref, sums_ref):
    channels, rows, cols = x_ref.shape
    tiles = cols // LANES
    rate = rate_ref[0]
    inner_row = lax.broadcasted_iota(jnp.int32, (rows, LANES), 0) < rows - 1
    edge_lane = lax.broadcasted_iota(jnp.int32, (rows, LANES), 1) == LANES - 1
    for j in range(tiles):
        here = pl.ds(j * LANES, LANES)
        sums = [jnp.zeros((rows, LANES), jnp.float32) for _ in own_pairs]
        for c in range(channels):
            x = x_ref[c, :, here]
            below = pltpu.roll(x, rows - 1, 0)
            right = pltpu.roll(x, LANES - 1, 1)
            if j + 1 < tiles:
                after = pltpu.roll(x_ref[c, :, pl.ds((j + 1) * LANES, LANES)], LANES - 1, 1)
            else:
                after = x
            steps = (jnp.where(inner_row, below - x, 0.0), jnp.where(edge_lane, after, right) - x)
            cand = [dual_ref[a, c, :, here] + rate * steps[a] for a in range(2)]
            for a in range(2):
                cand_ref[a, c, :, here] = cand[a]
            sums = [s + cand[a] * cand[b] for s, (a, b) in zip(sums, own_pairs)]
        for k, s in enumerate(sums):
            sums_ref[k, :, here] = s


def gram_kernel(rate_ref, keep_ref, x_ref, next_ref, dual_ref, own_ref, sums_ref, cand_ref, out_ref):
    channels, rows, cols = x_ref.shape
    tiles = cols // LANES
    per_row = len(index_pairs) * tiles
    rate = rate_ref[0]
    keep = keep_ref[0]
    for j in range(tiles):
        here = pl.ds(j * LANES, LANES)
        sums = {pair: sums_ref[k, :, here] for k, pair in enumerate(own_pairs)}
        for b in range(3):
            sums[b, 2] = jnp.zeros((rows, LANES), jnp.float32)
        for c in range(channels):
            step = (next_ref[c, :, here] - x_ref[c, :, here]) * keep
            cand = dual_ref[2, c, :, here] + rate * step
            cand_ref[c, :, here] = cand
            for b in range(2):
                sums[b, 2] = sums[b, 2] + own_ref[b, c, :, here] * cand
            sums[2, 2] = sums[2, 2] + cand * cand
        for k, pair in enumerate(index_pairs):
            out_ref[pl.ds(k * tiles + j, rows, stride=per_row), :] = sums[pair]


def pass_on_kernel(parts_ref, misfit_ref, out_ref):
    peers, per_row, _ = parts_ref.shape
    total = parts_ref[0]
    for p in range(1, peers):
        total = total + parts_ref[p]
    misfit = misfit_ref[...]
    for p in range(out_ref.shape[0]):
        out_ref[p, :per_row, :] = total
        out_ref[p, per_row:, :] = misfit


def rotate(entry, vectors, p, q):
    k = 3 - p - q
    pq, kp, kq = (entry_of[tuple(sorted(s))] for s in ((p, q), (k, p), (k, q)))
    across, twice = entry[q] - entry[p], 2.0 * entry[pq]
    square = across * across + twice * twice
    still = square == 0.0
    inverse = lax.rsqrt(jnp.where(still, 1.0, square))
    length = square * inverse
    half = jnp.where(still, 1.0, 0.5 + 0.5 * jnp.abs(across) * inverse)
    root = lax.rsqrt(half)
    large, small = half * root, 0.5 * jnp.abs(twice) * inverse * root
    ahead = across >= 0.0
    cosine = jnp.where(ahead, large, small)
    sine = jnp.where(ahead, small, large)
    sine = jnp.where(twice < 0.0, -sine, sine)
    middle = entry[p] + entry[q]
    entry, vectors = list(entry), [list(row) for row in vectors]
    entry[p], entry[q] = 0.5 * (middle - length), 0.5 * (middle + length)
    entry[pq] = jnp.where(still, entry[pq], 0.0)
    entry[kp], entry[kq] = (
        cosine * entry[kp] - sine * entry[kq],
        sine * entry[kp] + cosine * entry[kq],
    )
    for row in vectors:
        row[p], row[q] = cosine * row[p] - sine * row[q], sine * row[p] + cosine * row[q]
    return entry, vectors


def factor_kernel(radius_ref, parts_ref, out_ref, sums_ref):
    peers, held, _ = parts_ref.shape
    entries = len(index_pairs)
    tiles = out_ref.shape[1] // entries

    def summed(start, size):
        total = parts_ref[0, pl.ds(start, size), :]
        for p in range(1, peers):
            total = total + parts_ref[p, pl.ds(start, size), :]
        return total

    radius = radius_ref[0]
    entry = [summed(k * tiles, tiles) for k in range(entries)]
    one, zero = jnp.ones_like(entry[0]), jnp.zeros_like(entry[0])
    vectors = [[one if r == c else zero for c in range(3)] for r in range(3)]
    for _ in range(SWEEPS):
        for p, q in sweep_order:
            entry, vectors = rotate(entry, vectors, p, q)
    roots = [jnp.sqrt(jnp.maximum(entry[d], 0.0)) for d in range(3)]
    scales = [radius / jnp.maximum(root, radius) for root in roots]
    excess = sum(jnp.maximum(root - radius, 0.0) for root in roots) / radius
    rows = [
        sum(vectors[a][d] * scales[d] * vectors[b][d] for d in range(3)) for a, b in index_pairs
    ]
    for p in range(out_ref.shape[0]):
        for k, row in enumerate(rows):
            out_ref[p, pl.ds(k * tiles, tiles), :] = row
    misfit = jnp.sum(summed(entries * tiles, held - entries * tiles), axis=0, keepdims=True)
    excess = jnp.sum(excess, axis=0, keepdims=True)
    for p in range(sums_ref.shape[0]):
        sums_ref[p, pl.ds(0, 1), :] = misfit
        sums_ref[p, pl.ds(1, 1), :] = excess


def factor_image(factor_ref, rows, tiles):
    per_row = factor_ref.shape[0] // rows

    def image(a, b, j):
        k = entry_of[tuple(sorted((a, b)))]
        return factor_ref[pl.ds(k * tiles + j, rows, stride=per_row), :]

    return image


def slice_kernel(factor_ref, own_ref, cand_ref, new_ref):
    channels, rows, cols = cand_ref.shape
    tiles = cols // LANES
    image = factor_image(factor_ref, rows, tiles)
    for j in range(tiles):
        here = pl.ds(j * LANES, LANES)
        factor = [image(b, 2, j) for b in range(3)]
        for c in range(channels):
            new_ref[c, :, here] = (
                own_ref[0, c, :, here] * factor[0]
                + own_ref[1, c, :, here] * factor[1]
                + cand_ref[c, :, here] * factor[2]
            )


def rest_kernel(
    rate_ref, keep_ref, factor_ref, own_ref, cand_ref, slice_ref, volume_ref, back_ref, new_ref, ready_ref
):
    channels, rows, cols = cand_ref.shape
    tiles = cols // LANES
    rate = rate_ref[0]
    keep = keep_ref[0]
    image = factor_image(factor_ref, rows, tiles)
    row_id = lax.broadcasted_iota(jnp.int32, (rows, LANES), 0)
    lane_id = lax.broadcasted_iota(jnp.int32, (rows, LANES), 1)
    before = [None] * channels
    for j in range(tiles):
        here = pl.ds(j * LANES, LANES)
        factor = [[image(b, a, j) for b in range(3)] for a in range(2)]
        for c in range(channels):
            cand = [own_ref[0, c, :, here], own_ref[1, c, :, here], cand_ref[c, :, here]]
            new = [sum(cand[b] * factor[a][b] for b in range(3)) for a in range(2)]
            along = slice_ref[c, :, here]
            for a in range(2):
                new_ref[a, c, :, here] = new[a]
            new_ref[2, c, :, here] = along
            kept = jnp.where(row_id < rows - 1, new[0], 0.0)
            spread = kept - jnp.where(row_id > 0, pltpu.roll(new[0], 1, 0), 0.0)
            left = pltpu.roll(new[1], 1, 1)
            earlier = jnp.where(lane_id > 0, left, 0.0 if j == 0 else before[c])
            before[c] = left
            kept = new[1] if j + 1 < tiles else jnp.where(lane_id < LANES - 1, new[1], 0.0)
            spread = spread + (kept - earlier) + keep * along
            ready_ref[c, :, here] = volume_ref[c, :, here] - rate * (back_ref[c, :, here] - spread)


def finish_kernel(counts, rate_ref, ready_ref, prior_ref, sums_ref, updated_ref, totals_ref):
    rate = rate_ref[0]
    for c in range(ready_ref.shape[0]):
        updated_ref[c] = jnp.maximum(ready_ref[c] - rate * prior_ref[c], 0.0)
    total = sums_ref[0]
    for p in range(1, sums_ref.shape[0]):
        total = total + sums_ref[p]
    for k, count in enumerate(counts):
        totals_ref[k] = jnp.sum(total[k : k + 1]) / count


def picked_blocks(blocks, where, count):
    chosen = (where[:, None] == jnp.arange(count, dtype=jnp.int32)[None, :]).astype(jnp.bfloat16)
    return jnp.einsum("tc,bcj->tbj", chosen, blocks, preferred_element_type=jnp.float32).astype(
        jnp.bfloat16
    )


def gathered_products(products, where, count):
    chosen = (where[:, None] == jnp.arange(count, dtype=jnp.int32)[None, :]).astype(jnp.float32)
    return jnp.einsum("tc,tbj->bcj", chosen, products, precision=lax.Precision.HIGHEST)


def on_device(
    volume_now,
    extrapolated,
    dual_grad,
    dual_data,
    measured,
    projector,
    tile_rows,
    tile_cols,
    dual_step,
    primal_step,
    reg_weight,
):
    f32 = jnp.float32
    dual_rate = dual_step[0]
    channels, slices, row_count, col_count = volume_now.shape
    pixels = row_count * col_count
    rays = dual_data.shape[2]
    edge = projector.shape[1]
    share_count, far_count = lax.axis_size(SHARE), lax.axis_size(FAR)
    slab_count = lax.axis_size("slab")
    total_channels = channels * share_count * far_count
    tiles = col_count // LANES
    held = len(index_pairs) * tiles
    last_slice = lax.axis_index("slab") == slab_count - 1
    images = (channels, row_count, col_count)

    keep = jnp.where(last_slice, 0.0, 1.0).reshape(1)
    image_form = jax.ShapeDtypeStruct(images, f32)
    x_near, dual_near = near(extrapolated.reshape(images)), near(dual_grad.reshape(3, *images))

    following = from_behind(extrapolated, "slab", -1)
    own, own_sums = pl.pallas_call(
        own_kernel,
        out_shape=(kept_near((2, *images)), kept_near((len(own_pairs), row_count, col_count))),
        in_specs=[SMEM, VMEM, VMEM],
        out_specs=(VMEM, VMEM),
        name="own",
    )(dual_step, x_near, dual_near)
    cand, partial_gram = pl.pallas_call(
        gram_kernel,
        out_shape=(kept_near(images), jax.ShapeDtypeStruct((row_count * held, LANES), f32)),
        in_specs=[SMEM, SMEM, VMEM, VMEM, VMEM, VMEM, VMEM],
        out_specs=(VMEM, VMEM),
        name="gram",
    )(
        dual_step,
        keep,
        x_near,
        near(following.reshape(images)),
        dual_near,
        near(own),
        near(own_sums),
    )
    gram_parts = lax.all_to_all(
        partial_gram.reshape(share_count, held, LANES), SHARE, 0, 0, tiled=True
    )

    rounded = extrapolated.reshape(channels, pixels // edge, edge).astype(jnp.bfloat16)
    picked = picked_blocks(rounded, tile_cols, pixels // edge)
    products = jnp.einsum("tij,tbj->tbi", projector, picked, preferred_element_type=f32)
    projected = gathered_products(products, tile_rows, rays // edge)
    residual = projected - measured.reshape(projected.shape)
    data_new = (dual_data.reshape(projected.shape) + dual_rate * residual) / (1.0 + dual_rate)
    misfit_part = jnp.sum((residual * residual).reshape(-1, 8, LANES), axis=0)

    to_far = pl.pallas_call(
        pass_on_kernel,
        out_shape=jax.ShapeDtypeStruct((far_count, held + 8, LANES), f32),
        in_specs=[VMEM, VMEM],
        out_specs=VMEM,
        name="pass_on",
    )(near(gram_parts), near(misfit_part))
    far_parts = lax.all_to_all(to_far, FAR, 0, 0, tiled=True)

    data_low = data_new.astype(jnp.bfloat16)
    picked_back = picked_blocks(data_low, tile_rows, rays // edge)
    products_back = jnp.einsum("tij,tbi->tbj", projector, picked_back, preferred_element_type=f32)
    back_proj = gathered_products(products_back, tile_cols, pixels // edge).reshape(
        volume_now.shape
    )

    radius = reg_weight * math.sqrt(total_channels)
    to_share, sums = pl.pallas_call(
        factor_kernel,
        out_shape=(
            jax.ShapeDtypeStruct((share_count, held, LANES), f32),
            jax.ShapeDtypeStruct((share_count * slab_count, 2, LANES), f32),
        ),
        in_specs=[SMEM, VMEM],
        out_specs=(VMEM, VMEM),
        name="factor",
    )(radius, near(far_parts))
    factor_rows = lax.all_to_all(to_share, SHARE, 0, 0, tiled=True)
    all_sums = lax.all_to_all(sums, (*SHARE, "slab"), 0, 0, tiled=True)
    factor_near = near(factor_rows.reshape(share_count * held, LANES))

    new_slice = pl.pallas_call(
        slice_kernel,
        out_shape=kept_near(images),
        in_specs=[VMEM, VMEM, VMEM],
        out_specs=VMEM,
        name="slice",
    )(factor_near, near(own), near(cand))
    prior_layer = from_behind(new_slice, "slab", 1)
    grad_new, ready = pl.pallas_call(
        rest_kernel,
        out_shape=(jax.ShapeDtypeStruct((3, *images), f32), kept_near(images)),
        in_specs=[SMEM, SMEM] + [VMEM] * 6,
        out_specs=(VMEM, VMEM),
        name="rest",
    )(
        primal_step,
        keep,
        factor_near,
        near(own),
        near(cand),
        near(new_slice),
        near(volume_now.reshape(images)),
        near(back_proj.reshape(images)),
    )
    counts = (total_channels * slab_count * slices * rays, slab_count * slices * pixels)
    updated, totals = pl.pallas_call(
        functools.partial(finish_kernel, counts),
        out_shape=(image_form, jax.ShapeDtypeStruct((2,), f32)),
        in_specs=[SMEM, VMEM, VMEM, VMEM],
        out_specs=(VMEM, SMEM),
        name="finish",
    )(primal_step, near(ready), near(prior_layer), near(all_sums))
    return (
        updated.reshape(volume_now.shape),
        grad_new.reshape(dual_grad.shape),
        data_new.reshape(dual_data.shape),
        totals,
    )


def solution(mesh):
    torus = Mesh(
        mesh.devices.reshape(4, 2, 8, 2, mesh.shape["slab"]), ("x", "y", "zfar", "znear", "slab")
    )
    placed = (
        P(CHAN, "slab", None, None),
        P(CHAN, "slab", None, None),
        P(None, CHAN, "slab", None, None),
        P(CHAN, "slab", None),
        P(CHAN, "slab", None),
        P(),
        P(),
        P(),
        P(),
        P(),
        P(),
    )
    return jax.shard_map(
        on_device,
        mesh=torus,
        in_specs=placed,
        out_specs=(
            P(CHAN, "slab", None, None),
            P(None, CHAN, "slab", None, None),
            P(CHAN, "slab", None),
            P(),
        ),
        check_vma=False,
    )
```

```python
import functools
import math

import jax
import jax.numpy as jnp
from jax import lax
from jax.experimental import pallas as pl
from jax.experimental.pallas import tpu as pltpu
from jax.sharding import Mesh
from jax.sharding import PartitionSpec as P

SWEEPS = 6
CHAN = ("x", "y", "zfar", "znear")
SHARE = ("x", "y", "znear")
FAR = "zfar"
LANES = 128

index_pairs = ((0, 0), (1, 1), (2, 2), (0, 1), (0, 2), (1, 2))
entry_of = {pair: k for k, pair in enumerate(index_pairs)}
sweep_order = ((0, 1), (0, 2), (1, 2))
own_pairs = ((0, 0), (1, 1), (0, 1))

VMEM = pl.BlockSpec(memory_space=pltpu.VMEM)
SMEM = pl.BlockSpec(memory_space=pltpu.SMEM)
ANY = pl.BlockSpec(memory_space=pl.ANY)


def near(array):
    return pltpu.with_memory_space_constraint(array, pltpu.VMEM)


def kept_near(shape):
    return pltpu.VMEM(shape, jnp.float32)


def from_behind(block, axis, distance):
    devices = range(lax.axis_size(axis))
    route = [(i - distance, i) for i in devices if i - distance in devices]
    return lax.ppermute(block, axis, route)


def own_kernel(rate_ref, x_far, dual_far, x_ref, cand_ref, sums_ref, arrived):
    channels, rows, cols = x_ref.shape
    tiles = cols // LANES
    parts = arrived.shape[1]
    size = channels // parts
    copies = []
    for part in range(parts):
        some = pl.ds(part * size, size)
        copies.append(
            (
                pltpu.make_async_copy(x_far.at[some], x_ref.at[some], arrived.at[0, part]),
                pltpu.make_async_copy(
                    dual_far.at[:, some], cand_ref.at[:, some], arrived.at[1, part]
                ),
            )
        )
        for copy in copies[-1]:
            copy.start()
    rate = rate_ref[0]
    inner_row = lax.broadcasted_iota(jnp.int32, (rows, LANES), 0) < rows - 1
    edge_lane = lax.broadcasted_iota(jnp.int32, (rows, LANES), 1) == LANES - 1
    for part in range(parts):
        for copy in copies[part]:
            copy.wait()
        for j in range(tiles):
            here = pl.ds(j * LANES, LANES)
            if part:
                sums = [sums_ref[k, :, here] for k in range(len(own_pairs))]
            else:
                sums = [jnp.zeros((rows, LANES), jnp.float32) for _ in own_pairs]
            for c in range(part * size, part * size + size):
                x = x_ref[c, :, here]
                below = pltpu.roll(x, rows - 1, 0)
                right = pltpu.roll(x, LANES - 1, 1)
                if j + 1 < tiles:
                    after = pltpu.roll(x_ref[c, :, pl.ds((j + 1) * LANES, LANES)], LANES - 1, 1)
                else:
                    after = x
                steps = (
                    jnp.where(inner_row, below - x, 0.0),
                    jnp.where(edge_lane, after, right) - x,
                )
                cand = [cand_ref[a, c, :, here] + rate * steps[a] for a in range(2)]
                for a in range(2):
                    cand_ref[a, c, :, here] = cand[a]
                sums = [s + cand[a] * cand[b] for s, (a, b) in zip(sums, own_pairs)]
            for k, s in enumerate(sums):
                sums_ref[k, :, here] = s


def gram_kernel(
    rate_ref, keep_ref, next_ref, sums_ref, x_ref, dual_ref, x_same, cand_ref, out_ref
):
    channels, rows, cols = x_ref.shape
    tiles = cols // LANES
    per_row = len(index_pairs) * tiles
    rate = rate_ref[0]
    keep = keep_ref[0]
    for j in range(tiles):
        here = pl.ds(j * LANES, LANES)
        sums = {pair: sums_ref[k, :, here] for k, pair in enumerate(own_pairs)}
        for b in range(3):
            sums[b, 2] = jnp.zeros((rows, LANES), jnp.float32)
        for c in range(channels):
            step = (next_ref[c, :, here] - x_ref[c, :, here]) * keep
            cand = dual_ref[2, c, :, here] + rate * step
            for b in range(2):
                sums[b, 2] = sums[b, 2] + dual_ref[b, c, :, here] * cand
            sums[2, 2] = sums[2, 2] + cand * cand
            cand_ref[2, c, :, here] = cand
        for k, pair in enumerate(index_pairs):
            out_ref[pl.ds(k * tiles + j, rows, stride=per_row), :] = sums[pair]


def pass_on_kernel(parts_ref, misfit_ref, data_ref, out_ref, data_same):
    peers, per_row, _ = parts_ref.shape
    total = parts_ref[0]
    for p in range(1, peers):
        total = total + parts_ref[p]
    misfit = misfit_ref[...]
    for p in range(out_ref.shape[0]):
        out_ref[p, :per_row, :] = total
        out_ref[p, per_row:, :] = misfit


def rotate(entry, vectors, p, q):
    k = 3 - p - q
    pq, kp, kq = (entry_of[tuple(sorted(s))] for s in ((p, q), (k, p), (k, q)))
    across, twice = entry[q] - entry[p], 2.0 * entry[pq]
    square = across * across + twice * twice
    still = square == 0.0
    inverse = lax.rsqrt(jnp.where(still, 1.0, square))
    length = square * inverse
    half = jnp.where(still, 1.0, 0.5 + 0.5 * jnp.abs(across) * inverse)
    root = lax.rsqrt(half)
    large, small = half * root, 0.5 * jnp.abs(twice) * inverse * root
    ahead = across >= 0.0
    cosine = jnp.where(ahead, large, small)
    sine = jnp.where(ahead, small, large)
    sine = jnp.where(twice < 0.0, -sine, sine)
    middle = entry[p] + entry[q]
    entry, vectors = list(entry), [list(row) for row in vectors]
    entry[p], entry[q] = 0.5 * (middle - length), 0.5 * (middle + length)
    entry[pq] = jnp.where(still, entry[pq], 0.0)
    entry[kp], entry[kq] = (
        cosine * entry[kp] - sine * entry[kq],
        sine * entry[kp] + cosine * entry[kq],
    )
    for row in vectors:
        row[p], row[q] = cosine * row[p] - sine * row[q], sine * row[p] + cosine * row[q]
    return entry, vectors


def factor_kernel(radius_ref, parts_ref, back_ref, out_ref, back_same):
    peers, held, _ = parts_ref.shape
    entries = len(index_pairs)
    tiles = out_ref.shape[1] // (entries + 2)

    def summed(start, size):
        total = parts_ref[0, pl.ds(start, size), :]
        for p in range(1, peers):
            total = total + parts_ref[p, pl.ds(start, size), :]
        return total

    radius = radius_ref[0]
    entry = [summed(k * tiles, tiles) for k in range(entries)]
    one, zero = jnp.ones_like(entry[0]), jnp.zeros_like(entry[0])
    vectors = [[one if r == c else zero for c in range(3)] for r in range(3)]
    for _ in range(SWEEPS):
        for p, q in sweep_order:
            entry, vectors = rotate(entry, vectors, p, q)
    roots = [jnp.sqrt(jnp.maximum(entry[d], 0.0)) for d in range(3)]
    scales = [radius / jnp.maximum(root, radius) for root in roots]
    excess = sum(jnp.maximum(root - radius, 0.0) for root in roots) / radius
    misfit = sum(summed(k, tiles) for k in range(entries * tiles, held, tiles))
    rows = [
        sum(vectors[a][d] * scales[d] * vectors[b][d] for d in range(3)) for a, b in index_pairs
    ] + [misfit, excess]
    for p in range(out_ref.shape[0]):
        for k, row in enumerate(rows):
            out_ref[p, pl.ds(k * tiles, tiles), :] = row


def factor_image(factor_ref, rows, tiles):
    per_row = factor_ref.shape[0] // rows

    def image(k, j):
        return factor_ref[pl.ds(k * tiles + j, rows, stride=per_row), :]

    return image


def entry_at(a, b):
    return entry_of[tuple(sorted((a, b)))]


def slice_kernel(factor_ref, cand_ref, new_ref):
    _, channels, rows, cols = cand_ref.shape
    tiles = cols // LANES
    image = factor_image(factor_ref, rows, tiles)
    for j in range(tiles):
        here = pl.ds(j * LANES, LANES)
        factor = [image(entry_at(b, 2), j) for b in range(3)]
        for c in range(channels):
            new_ref[c, :, here] = sum(cand_ref[b, c, :, here] * factor[b] for b in range(3))


def rest_kernel(
    rate_ref,
    keep_ref,
    factor_ref,
    cand_ref,
    slice_ref,
    volume_ref,
    back_ref,
    new_ref,
    ready_ref,
    sums_ref,
):
    _, channels, rows, cols = cand_ref.shape
    tiles = cols // LANES
    rate = rate_ref[0]
    keep = keep_ref[0]
    image = factor_image(factor_ref, rows, tiles)
    for k in range(2):
        total = sum(image(len(index_pairs) + k, j) for j in range(tiles))
        total = jnp.sum(total, axis=0, keepdims=True)
        for p in range(sums_ref.shape[0]):
            sums_ref[p, pl.ds(k, 1), :] = total
    row_id = lax.broadcasted_iota(jnp.int32, (rows, LANES), 0)
    lane_id = lax.broadcasted_iota(jnp.int32, (rows, LANES), 1)
    before = [None] * channels
    for j in range(tiles):
        here = pl.ds(j * LANES, LANES)
        factor = [[image(entry_at(b, a), j) for b in range(3)] for a in range(2)]
        for c in range(channels):
            cand = [cand_ref[b, c, :, here] for b in range(3)]
            new = [sum(cand[b] * factor[a][b] for b in range(3)) for a in range(2)]
            along = slice_ref[c, :, here]
            for a in range(2):
                new_ref[a, c, :, here] = new[a]
            new_ref[2, c, :, here] = along
            kept = jnp.where(row_id < rows - 1, new[0], 0.0)
            spread = kept - jnp.where(row_id > 0, pltpu.roll(new[0], 1, 0), 0.0)
            left = pltpu.roll(new[1], 1, 1)
            earlier = jnp.where(lane_id > 0, left, 0.0 if j == 0 else before[c])
            before[c] = left
            kept = new[1] if j + 1 < tiles else jnp.where(lane_id < LANES - 1, new[1], 0.0)
            spread = spread + (kept - earlier) + keep * along
            ready_ref[c, :, here] = volume_ref[c, :, here] - rate * (back_ref[c, :, here] - spread)


def finish_kernel(counts, rate_ref, ready_ref, prior_ref, sums_ref, updated_ref, totals_ref):
    rate = rate_ref[0]
    for c in range(ready_ref.shape[0]):
        updated_ref[c] = jnp.maximum(ready_ref[c] - rate * prior_ref[c], 0.0)
    total = sums_ref[0]
    for p in range(1, sums_ref.shape[0]):
        total = total + sums_ref[p]
    for k, count in enumerate(counts):
        totals_ref[k] = jnp.sum(total[k : k + 1]) / count


def picked_blocks(blocks, where, count):
    chosen = (where[:, None] == jnp.arange(count, dtype=jnp.int32)[None, :]).astype(jnp.bfloat16)
    return jnp.einsum("tc,bcj->tbj", chosen, blocks, preferred_element_type=jnp.float32).astype(
        jnp.bfloat16
    )


def gathered_products(products, where, count):
    chosen = (where[:, None] == jnp.arange(count, dtype=jnp.int32)[None, :]).astype(jnp.float32)
    return jnp.einsum("tc,tbj->bcj", chosen, products, precision=lax.Precision.HIGHEST)


def on_device(
    volume_now,
    extrapolated,
    dual_grad,
    dual_data,
    measured,
    projector,
    tile_rows,
    tile_cols,
    dual_step,
    primal_step,
    reg_weight,
):
    f32 = jnp.float32
    dual_rate = dual_step[0]
    channels, slices, row_count, col_count = volume_now.shape
    pixels = row_count * col_count
    rays = dual_data.shape[2]
    edge = projector.shape[1]
    share_count, far_count = lax.axis_size(SHARE), lax.axis_size(FAR)
    slab_count = lax.axis_size("slab")
    total_channels = channels * share_count * far_count
    tiles = col_count // LANES
    held = len(index_pairs) * tiles
    last_slice = lax.axis_index("slab") == slab_count - 1
    images = (channels, row_count, col_count)

    keep = jnp.where(last_slice, 0.0, 1.0).reshape(1)
    image_form = jax.ShapeDtypeStruct(images, f32)

    following = from_behind(extrapolated, "slab", -1)
    x_near, duals, own_sums = pl.pallas_call(
        own_kernel,
        out_shape=(
            kept_near(images),
            kept_near((3, *images)),
            kept_near((len(own_pairs), row_count, col_count)),
        ),
        in_specs=[SMEM, ANY, ANY],
        out_specs=(VMEM, VMEM, VMEM),
        scratch_shapes=[pltpu.SemaphoreType.DMA((2, 4))],
        name="own",
    )(dual_step, extrapolated.reshape(images), dual_grad.reshape(3, *images))
    x_near, candidate, partial_gram = pl.pallas_call(
        gram_kernel,
        out_shape=(
            kept_near(images),
            kept_near((3, *images)),
            jax.ShapeDtypeStruct((row_count * held, LANES), f32),
        ),
        in_specs=[SMEM, SMEM, VMEM, VMEM, VMEM, VMEM],
        out_specs=(VMEM, VMEM, VMEM),
        input_output_aliases={4: 0, 5: 1},
        name="gram",
    )(
        dual_step,
        keep,
        near(following.reshape(images)),
        near(own_sums),
        near(x_near),
        near(duals),
    )
    gram_parts = lax.all_to_all(
        partial_gram.reshape(share_count, held, LANES), SHARE, 0, 0, tiled=True
    )

    rounded = x_near.reshape(channels, pixels // edge, edge).astype(jnp.bfloat16)
    picked = picked_blocks(rounded, tile_cols, pixels // edge)
    products = jnp.einsum("tij,tbj->tbi", projector, picked, preferred_element_type=f32)
    projected = gathered_products(products, tile_rows, rays // edge)
    residual = projected - measured.reshape(projected.shape)
    data_new = (dual_data.reshape(projected.shape) + dual_rate * residual) / (1.0 + dual_rate)
    misfit_part = jnp.sum((residual * residual).reshape(-1, 8, LANES), axis=0)

    to_far, data_new = pl.pallas_call(
        pass_on_kernel,
        out_shape=(
            jax.ShapeDtypeStruct((far_count, held + 8, LANES), f32),
            kept_near(data_new.shape),
        ),
        in_specs=[VMEM, VMEM, VMEM],
        out_specs=(VMEM, VMEM),
        input_output_aliases={2: 1},
        name="pass_on",
    )(near(gram_parts), near(misfit_part), near(data_new))
    far_parts = lax.all_to_all(to_far, FAR, 0, 0, tiled=True)

    data_low = data_new.astype(jnp.bfloat16)
    picked_back = picked_blocks(data_low, tile_rows, rays // edge)
    products_back = jnp.einsum("tij,tbi->tbj", projector, picked_back, preferred_element_type=f32)
    back_proj = gathered_products(products_back, tile_cols, pixels // edge).reshape(
        volume_now.shape
    )

    radius = reg_weight * math.sqrt(total_channels)
    to_share, back_proj = pl.pallas_call(
        factor_kernel,
        out_shape=(
            jax.ShapeDtypeStruct((share_count, held + 2 * tiles, LANES), f32),
            kept_near(images),
        ),
        in_specs=[SMEM, VMEM, VMEM],
        out_specs=(VMEM, VMEM),
        input_output_aliases={2: 1},
        name="factor",
    )(radius, near(far_parts), near(back_proj.reshape(images)))
    factor_rows = lax.all_to_all(to_share, SHARE, 0, 0, tiled=True)
    factor_near = near(factor_rows.reshape(-1, LANES))

    new_slice = pl.pallas_call(
        slice_kernel,
        out_shape=kept_near(images),
        in_specs=[VMEM, VMEM],
        out_specs=VMEM,
        name="slice",
    )(factor_near, near(candidate))
    prior_layer = from_behind(new_slice, "slab", 1)
    grad_new, ready, sums = pl.pallas_call(
        rest_kernel,
        out_shape=(
            jax.ShapeDtypeStruct((3, *images), f32),
            kept_near(images),
            jax.ShapeDtypeStruct((slab_count, 2, LANES), f32),
        ),
        in_specs=[SMEM, SMEM] + [VMEM] * 5,
        out_specs=(VMEM, VMEM, VMEM),
        name="rest",
    )(
        primal_step,
        keep,
        factor_near,
        near(candidate),
        near(new_slice),
        near(volume_now.reshape(images)),
        near(back_proj),
    )
    all_sums = lax.all_to_all(sums, "slab", 0, 0, tiled=True)
    counts = (total_channels * slab_count * slices * rays, slab_count * slices * pixels)
    updated, totals = pl.pallas_call(
        functools.partial(finish_kernel, counts),
        out_shape=(image_form, jax.ShapeDtypeStruct((2,), f32)),
        in_specs=[SMEM, VMEM, VMEM, VMEM],
        out_specs=(VMEM, SMEM),
        name="finish",
    )(primal_step, near(ready), near(prior_layer), near(all_sums))
    return (
        updated.reshape(volume_now.shape),
        grad_new.reshape(dual_grad.shape),
        data_new.reshape(dual_data.shape),
        totals,
    )


def solution(mesh):
    torus = Mesh(
        mesh.devices.reshape(4, 2, 8, 2, mesh.shape["slab"]), ("x", "y", "zfar", "znear", "slab")
    )
    placed = (
        P(CHAN, "slab", None, None),
        P(CHAN, "slab", None, None),
        P(None, CHAN, "slab", None, None),
        P(CHAN, "slab", None),
        P(CHAN, "slab", None),
        P(),
        P(),
        P(),
        P(),
        P(),
        P(),
    )
    return jax.shard_map(
        on_device,
        mesh=torus,
        in_specs=placed,
        out_specs=(
            P(CHAN, "slab", None, None),
            P(None, CHAN, "slab", None, None),
            P(CHAN, "slab", None),
            P(),
        ),
        check_vma=False,
    )
```

```python
import functools
import math

import jax
import jax.numpy as jnp
from jax import lax
from jax.experimental import pallas as pl
from jax.experimental.pallas import tpu as pltpu
from jax.sharding import Mesh
from jax.sharding import PartitionSpec as P

SWEEPS = 6
CHAN = ("x", "y", "zfar", "znear")
SHARE = ("x", "y", "znear")
FAR = "zfar"
LANES = 128

index_pairs = ((0, 0), (1, 1), (2, 2), (0, 1), (0, 2), (1, 2))
entry_of = {pair: k for k, pair in enumerate(index_pairs)}
sweep_order = ((0, 1), (0, 2), (1, 2))
own_pairs = ((0, 0), (1, 1), (0, 1))

VMEM = pl.BlockSpec(memory_space=pltpu.VMEM)
SMEM = pl.BlockSpec(memory_space=pltpu.SMEM)
ANY = pl.BlockSpec(memory_space=pl.ANY)
SCRATCH = pltpu.CompilerParams(vmem_limit_bytes=6 * 2**20)


def near(array):
    return pltpu.with_memory_space_constraint(array, pltpu.VMEM)


def left_far(array):
    return pltpu.with_memory_space_constraint(array, pltpu.HBM)


def kept_near(shape):
    return pltpu.VMEM(shape, jnp.float32)


def from_behind(block, axis, distance):
    devices = range(lax.axis_size(axis))
    route = [(i - distance, i) for i in devices if i - distance in devices]
    return lax.ppermute(block, axis, route)


def own_kernel(rate_ref, x_far, dual_far, *refs):
    count = (len(refs) - 5) // 2
    others_far, (x_ref, cand_ref, sums_ref), others = refs[:count], refs[count : count + 3], refs[count + 3 : -2]
    arrived, others_in = refs[-2:]
    channels, rows, cols = x_ref.shape
    tiles = cols // LANES
    parts = arrived.shape[1]
    size = channels // parts
    copies = []
    for part in range(parts):
        some = pl.ds(part * size, size)
        copies.append(
            (
                pltpu.make_async_copy(x_far.at[some], x_ref.at[some], arrived.at[0, part]),
                pltpu.make_async_copy(
                    dual_far.at[:, some], cand_ref.at[:, some], arrived.at[1, part]
                ),
            )
        )
        for copy in copies[-1]:
            copy.start()
    other_copies = [
        pltpu.make_async_copy(far, here, others_in.at[k])
        for k, (far, here) in enumerate(zip(others_far, others))
    ]
    for copy in other_copies:
        copy.start()
    rate = rate_ref[0]
    inner_row = lax.broadcasted_iota(jnp.int32, (rows, LANES), 0) < rows - 1
    edge_lane = lax.broadcasted_iota(jnp.int32, (rows, LANES), 1) == LANES - 1
    for part in range(parts):
        for copy in copies[part]:
            copy.wait()
        for j in range(tiles):
            here = pl.ds(j * LANES, LANES)
            if part:
                sums = [sums_ref[k, :, here] for k in range(len(own_pairs))]
            else:
                sums = [jnp.zeros((rows, LANES), jnp.float32) for _ in own_pairs]
            for c in range(part * size, part * size + size):
                x = x_ref[c, :, here]
                below = pltpu.roll(x, rows - 1, 0)
                right = pltpu.roll(x, LANES - 1, 1)
                if j + 1 < tiles:
                    after = pltpu.roll(x_ref[c, :, pl.ds((j + 1) * LANES, LANES)], LANES - 1, 1)
                else:
                    after = x
                steps = (
                    jnp.where(inner_row, below - x, 0.0),
                    jnp.where(edge_lane, after, right) - x,
                )
                cand = [cand_ref[a, c, :, here] + rate * steps[a] for a in range(2)]
                for a in range(2):
                    cand_ref[a, c, :, here] = cand[a]
                sums = [s + cand[a] * cand[b] for s, (a, b) in zip(sums, own_pairs)]
            for k, s in enumerate(sums):
                sums_ref[k, :, here] = s
    for copy in other_copies:
        copy.wait()


def gram_kernel(
    rate_ref, keep_ref, next_ref, sums_ref, x_ref, dual_ref, x_same, cand_ref, out_ref
):
    channels, rows, cols = x_ref.shape
    tiles = cols // LANES
    per_row = len(index_pairs) * tiles
    rate = rate_ref[0]
    keep = keep_ref[0]
    for j in range(tiles):
        here = pl.ds(j * LANES, LANES)
        sums = {pair: sums_ref[k, :, here] for k, pair in enumerate(own_pairs)}
        for b in range(3):
            sums[b, 2] = jnp.zeros((rows, LANES), jnp.float32)
        for c in range(channels):
            step = (next_ref[c, :, here] - x_ref[c, :, here]) * keep
            cand = dual_ref[2, c, :, here] + rate * step
            for b in range(2):
                sums[b, 2] = sums[b, 2] + dual_ref[b, c, :, here] * cand
            sums[2, 2] = sums[2, 2] + cand * cand
            cand_ref[2, c, :, here] = cand
        for k, pair in enumerate(index_pairs):
            out_ref[pl.ds(k * tiles + j, rows, stride=per_row), :] = sums[pair]


def pass_on_kernel(parts_ref, misfit_ref, data_ref, out_ref, data_same):
    peers, per_row, _ = parts_ref.shape
    total = parts_ref[0]
    for p in range(1, peers):
        total = total + parts_ref[p]
    misfit = misfit_ref[...]
    for p in range(out_ref.shape[0]):
        out_ref[p, :per_row, :] = total
        out_ref[p, per_row:, :] = misfit


def rotate(entry, vectors, p, q):
    k = 3 - p - q
    pq, kp, kq = (entry_of[tuple(sorted(s))] for s in ((p, q), (k, p), (k, q)))
    across, twice = entry[q] - entry[p], 2.0 * entry[pq]
    square = across * across + twice * twice
    still = square == 0.0
    inverse = lax.rsqrt(jnp.where(still, 1.0, square))
    length = square * inverse
    half = jnp.where(still, 1.0, 0.5 + 0.5 * jnp.abs(across) * inverse)
    root = lax.rsqrt(half)
    large, small = half * root, 0.5 * jnp.abs(twice) * inverse * root
    ahead = across >= 0.0
    cosine = jnp.where(ahead, large, small)
    sine = jnp.where(ahead, small, large)
    sine = jnp.where(twice < 0.0, -sine, sine)
    middle = entry[p] + entry[q]
    entry, vectors = list(entry), [list(row) for row in vectors]
    entry[p], entry[q] = 0.5 * (middle - length), 0.5 * (middle + length)
    entry[pq] = jnp.where(still, entry[pq], 0.0)
    entry[kp], entry[kq] = (
        cosine * entry[kp] - sine * entry[kq],
        sine * entry[kp] + cosine * entry[kq],
    )
    for row in vectors:
        row[p], row[q] = cosine * row[p] - sine * row[q], sine * row[p] + cosine * row[q]
    return entry, vectors


def factor_kernel(radius_ref, parts_ref, back_ref, out_ref, back_same):
    peers, held, _ = parts_ref.shape
    entries = len(index_pairs)
    tiles = out_ref.shape[1] // (entries + 2)

    def summed(start, size):
        total = parts_ref[0, pl.ds(start, size), :]
        for p in range(1, peers):
            total = total + parts_ref[p, pl.ds(start, size), :]
        return total

    radius = radius_ref[0]
    entry = [summed(k * tiles, tiles) for k in range(entries)]
    one, zero = jnp.ones_like(entry[0]), jnp.zeros_like(entry[0])
    vectors = [[one if r == c else zero for c in range(3)] for r in range(3)]
    for _ in range(SWEEPS):
        for p, q in sweep_order:
            entry, vectors = rotate(entry, vectors, p, q)
    roots = [jnp.sqrt(jnp.maximum(entry[d], 0.0)) for d in range(3)]
    scales = [radius / jnp.maximum(root, radius) for root in roots]
    excess = sum(jnp.maximum(root - radius, 0.0) for root in roots) / radius
    misfit = sum(summed(k, tiles) for k in range(entries * tiles, held, tiles))
    rows = [
        sum(vectors[a][d] * scales[d] * vectors[b][d] for d in range(3)) for a, b in index_pairs
    ] + [misfit, excess]
    for p in range(out_ref.shape[0]):
        for k, row in enumerate(rows):
            out_ref[p, pl.ds(k * tiles, tiles), :] = row


def factor_image(factor_ref, rows, tiles):
    per_row = factor_ref.shape[0] // rows

    def image(k, j):
        return factor_ref[pl.ds(k * tiles + j, rows, stride=per_row), :]

    return image


def entry_at(a, b):
    return entry_of[tuple(sorted((a, b)))]


def slice_kernel(factor_ref, cand_ref, new_ref):
    _, channels, rows, cols = cand_ref.shape
    tiles = cols // LANES
    image = factor_image(factor_ref, rows, tiles)
    for j in range(tiles):
        here = pl.ds(j * LANES, LANES)
        factor = [image(entry_at(b, 2), j) for b in range(3)]
        for c in range(channels):
            new_ref[c, :, here] = sum(cand_ref[b, c, :, here] * factor[b] for b in range(3))


def sums_kernel(factor_ref, slice_ref, sums_ref):
    slabs, count, _ = sums_ref.shape
    rows = slice_ref.shape[1]
    tiles = slice_ref.shape[2] // LANES
    image = factor_image(factor_ref, rows, tiles)
    for k in range(count):
        total = sum(image(len(index_pairs) + k, j) for j in range(tiles))
        total = jnp.sum(total, axis=0, keepdims=True)
        for p in range(slabs):
            sums_ref[p, pl.ds(k, 1), :] = total


def rest_kernel(
    rate_ref,
    keep_ref,
    factor_ref,
    cand_ref,
    slice_ref,
    volume_ref,
    back_ref,
    new_ref,
    ready_ref,
):
    _, channels, rows, cols = cand_ref.shape
    tiles = cols // LANES
    rate = rate_ref[0]
    keep = keep_ref[0]
    image = factor_image(factor_ref, rows, tiles)
    row_id = lax.broadcasted_iota(jnp.int32, (rows, LANES), 0)
    lane_id = lax.broadcasted_iota(jnp.int32, (rows, LANES), 1)
    before = [None] * channels
    for j in range(tiles):
        here = pl.ds(j * LANES, LANES)
        factor = [[image(entry_at(b, a), j) for b in range(3)] for a in range(2)]
        for c in range(channels):
            cand = [cand_ref[b, c, :, here] for b in range(3)]
            new = [sum(cand[b] * factor[a][b] for b in range(3)) for a in range(2)]
            along = slice_ref[c, :, here]
            for a in range(2):
                new_ref[a, c, :, here] = new[a]
            new_ref[2, c, :, here] = along
            kept = jnp.where(row_id < rows - 1, new[0], 0.0)
            spread = kept - jnp.where(row_id > 0, pltpu.roll(new[0], 1, 0), 0.0)
            left = pltpu.roll(new[1], 1, 1)
            earlier = jnp.where(lane_id > 0, left, 0.0 if j == 0 else before[c])
            before[c] = left
            kept = new[1] if j + 1 < tiles else jnp.where(lane_id < LANES - 1, new[1], 0.0)
            spread = spread + (kept - earlier) + keep * along
            ready_ref[c, :, here] = volume_ref[c, :, here] - rate * (back_ref[c, :, here] - spread)


def finish_kernel(counts, rate_ref, ready_ref, prior_ref, sums_ref, updated_ref, totals_ref):
    rate = rate_ref[0]
    for c in range(ready_ref.shape[0]):
        updated_ref[c] = jnp.maximum(ready_ref[c] - rate * prior_ref[c], 0.0)
    total = sums_ref[0]
    for p in range(1, sums_ref.shape[0]):
        total = total + sums_ref[p]
    for k, count in enumerate(counts):
        totals_ref[k] = jnp.sum(total[k : k + 1]) / count


def picked_blocks(blocks, where, count):
    chosen = (where[:, None] == jnp.arange(count, dtype=jnp.int32)[None, :]).astype(jnp.bfloat16)
    return jnp.einsum("tc,bcj->tbj", chosen, blocks, preferred_element_type=jnp.float32).astype(
        jnp.bfloat16
    )


def gathered_products(products, where, count):
    chosen = (where[:, None] == jnp.arange(count, dtype=jnp.int32)[None, :]).astype(jnp.float32)
    return jnp.einsum("tc,tbj->bcj", chosen, products, precision=lax.Precision.HIGHEST)


def on_device(
    volume_now,
    extrapolated,
    dual_grad,
    dual_data,
    measured,
    projector,
    tile_rows,
    tile_cols,
    dual_step,
    primal_step,
    reg_weight,
):
    f32 = jnp.float32
    dual_rate = dual_step[0]
    channels, slices, row_count, col_count = volume_now.shape
    pixels = row_count * col_count
    rays = dual_data.shape[2]
    edge = projector.shape[1]
    share_count, far_count = lax.axis_size(SHARE), lax.axis_size(FAR)
    slab_count = lax.axis_size("slab")
    total_channels = channels * share_count * far_count
    tiles = col_count // LANES
    held = len(index_pairs) * tiles
    last_slice = lax.axis_index("slab") == slab_count - 1
    images = (channels, row_count, col_count)

    keep = jnp.where(last_slice, 0.0, 1.0).reshape(1)
    image_form = jax.ShapeDtypeStruct(images, f32)

    following = from_behind(extrapolated, "slab", -1)
    sinogram = (channels, rays // edge, edge)
    others = (measured.reshape(sinogram), dual_data.reshape(sinogram), projector)
    x_near, duals, own_sums, measured_near, data_near, projector_near = pl.pallas_call(
        own_kernel,
        out_shape=(
            kept_near(images),
            kept_near((3, *images)),
            kept_near((len(own_pairs), row_count, col_count)),
            *(pltpu.VMEM(other.shape, other.dtype) for other in others),
        ),
        in_specs=[SMEM] + [ANY] * 5,
        out_specs=(VMEM,) * 6,
        scratch_shapes=[pltpu.SemaphoreType.DMA((2, 4)), pltpu.SemaphoreType.DMA((len(others),))],
        compiler_params=SCRATCH,
        name="own",
    )(
        dual_step,
        *map(left_far, (extrapolated.reshape(images), dual_grad.reshape(3, *images), *others)),
    )
    x_near, candidate, partial_gram = pl.pallas_call(
        gram_kernel,
        out_shape=(
            kept_near(images),
            kept_near((3, *images)),
            jax.ShapeDtypeStruct((row_count * held, LANES), f32),
        ),
        in_specs=[SMEM, SMEM, VMEM, VMEM, VMEM, VMEM],
        out_specs=(VMEM, VMEM, VMEM),
        input_output_aliases={4: 0, 5: 1},
        compiler_params=SCRATCH,
        name="gram",
    )(
        dual_step,
        keep,
        near(following.reshape(images)),
        near(own_sums),
        near(x_near),
        near(duals),
    )
    gram_parts = lax.all_to_all(
        partial_gram.reshape(share_count, held, LANES), SHARE, 0, 0, tiled=True
    )

    rounded = x_near.reshape(channels, pixels // edge, edge).astype(jnp.bfloat16)
    picked = picked_blocks(rounded, tile_cols, pixels // edge)
    products = jnp.einsum("tij,tbj->tbi", projector_near, picked, preferred_element_type=f32)
    projected = gathered_products(products, tile_rows, rays // edge)
    residual = projected - measured_near
    data_new = (data_near + dual_rate * residual) / (1.0 + dual_rate)
    misfit_part = jnp.sum((residual * residual).reshape(-1, 8, LANES), axis=0)

    to_far, data_new = pl.pallas_call(
        pass_on_kernel,
        out_shape=(
            jax.ShapeDtypeStruct((far_count, held + 8, LANES), f32),
            kept_near(data_new.shape),
        ),
        in_specs=[VMEM, VMEM, VMEM],
        out_specs=(VMEM, VMEM),
        input_output_aliases={2: 1},
        compiler_params=SCRATCH,
        name="pass_on",
    )(near(gram_parts), near(misfit_part), near(data_new))
    half = far_count // 2
    late_first = [[(half + i) % far_count for i in range(far_count)]]
    far_parts = lax.all_to_all(to_far, FAR, 0, 0, axis_index_groups=late_first, tiled=True)

    data_low = data_new.astype(jnp.bfloat16)
    picked_back = picked_blocks(data_low, tile_rows, rays // edge)
    products_back = jnp.einsum("tij,tbi->tbj", projector_near, picked_back, preferred_element_type=f32)
    back_proj = gathered_products(products_back, tile_cols, pixels // edge).reshape(
        volume_now.shape
    )

    radius = reg_weight * math.sqrt(total_channels)
    to_share, back_proj = pl.pallas_call(
        factor_kernel,
        out_shape=(
            jax.ShapeDtypeStruct((share_count, held + 2 * tiles, LANES), f32),
            kept_near(images),
        ),
        in_specs=[SMEM, VMEM, VMEM],
        out_specs=(VMEM, VMEM),
        input_output_aliases={2: 1},
        compiler_params=SCRATCH,
        name="factor",
    )(radius, near(far_parts), near(back_proj.reshape(images)))
    factor_rows = lax.all_to_all(to_share, SHARE, 0, 0, tiled=True)
    factor_near = near(factor_rows.reshape(-1, LANES))

    new_slice = pl.pallas_call(
        slice_kernel,
        out_shape=kept_near(images),
        in_specs=[VMEM, VMEM],
        out_specs=VMEM,
        compiler_params=SCRATCH,
        name="slice",
    )(factor_near, near(candidate))
    prior_layer = from_behind(new_slice, "slab", 1)
    sums = pl.pallas_call(
        sums_kernel,
        out_shape=jax.ShapeDtypeStruct((slab_count, 2, LANES), f32),
        in_specs=[VMEM, VMEM],
        out_specs=VMEM,
        compiler_params=SCRATCH,
        name="sums",
    )(factor_near, near(new_slice))
    all_sums = lax.all_to_all(sums, "slab", 0, 0, tiled=True)
    grad_new, ready = pl.pallas_call(
        rest_kernel,
        out_shape=(jax.ShapeDtypeStruct((3, *images), f32), kept_near(images)),
        in_specs=[SMEM, SMEM] + [VMEM] * 5,
        out_specs=(VMEM, VMEM),
        compiler_params=SCRATCH,
        name="rest",
    )(
        primal_step,
        keep,
        factor_near,
        near(candidate),
        near(new_slice),
        near(volume_now.reshape(images)),
        near(back_proj),
    )
    counts = (total_channels * slab_count * slices * rays, slab_count * slices * pixels)
    updated, totals = pl.pallas_call(
        functools.partial(finish_kernel, counts),
        out_shape=(image_form, jax.ShapeDtypeStruct((2,), f32)),
        in_specs=[SMEM, VMEM, VMEM, VMEM],
        out_specs=(VMEM, SMEM),
        compiler_params=SCRATCH,
        name="finish",
    )(primal_step, near(ready), near(prior_layer), near(all_sums))
    return (
        updated.reshape(volume_now.shape),
        grad_new.reshape(dual_grad.shape),
        data_new.reshape(dual_data.shape),
        totals,
    )


def solution(mesh):
    torus = Mesh(
        mesh.devices.reshape(4, 2, 8, 2, mesh.shape["slab"]), ("x", "y", "zfar", "znear", "slab")
    )
    placed = (
        P(CHAN, "slab", None, None),
        P(CHAN, "slab", None, None),
        P(None, CHAN, "slab", None, None),
        P(CHAN, "slab", None),
        P(CHAN, "slab", None),
        P(),
        P(),
        P(),
        P(),
        P(),
        P(),
    )
    return jax.shard_map(
        on_device,
        mesh=torus,
        in_specs=placed,
        out_specs=(
            P(CHAN, "slab", None, None),
            P(None, CHAN, "slab", None, None),
            P(CHAN, "slab", None),
            P(),
        ),
        check_vma=False,
    )
```

```python
import functools
import itertools
import math

import jax
import jax.numpy as jnp
from jax import lax
from jax.experimental import pallas as pl
from jax.experimental.pallas import tpu as pltpu
from jax.sharding import Mesh
from jax.sharding import PartitionSpec as P

SWEEPS = 6
CHAN = ("x", "y", "zfar", "znear")
SHARE = ("x", "y", "znear")
FAR = "zfar"
LANES = 128

index_pairs = ((0, 0), (1, 1), (2, 2), (0, 1), (0, 2), (1, 2))
entry_of = {pair: k for k, pair in enumerate(index_pairs)}
sweep_order = ((0, 1), (0, 2), (1, 2))
own_pairs = ((0, 0), (1, 1), (0, 1))

VMEM = pl.BlockSpec(memory_space=pltpu.VMEM)
SMEM = pl.BlockSpec(memory_space=pltpu.SMEM)
ANY = pl.BlockSpec(memory_space=pl.ANY)
SCRATCH = pltpu.CompilerParams(vmem_limit_bytes=6 * 2**20)


def near(array):
    return pltpu.with_memory_space_constraint(array, pltpu.VMEM)


def left_far(array):
    return pltpu.with_memory_space_constraint(array, pltpu.HBM)


def kept_near(shape):
    return pltpu.VMEM(shape, jnp.float32)


def by_distance(axes, first):
    sizes = [lax.axis_size(axis) for axis in axes]
    places = list(itertools.product(*map(range, sizes)))

    def away(place):
        return sum(min((a - b) % n, (b - a) % n) for a, b, n in zip(place, first, sizes))

    order = sorted(range(len(places)), key=lambda i: -away(places[i]))
    order.remove(places.index(first))
    return [places.index(first), *order]


def from_behind(block, axis, distance):
    devices = range(lax.axis_size(axis))
    route = [(i - distance, i) for i in devices if i - distance in devices]
    return lax.ppermute(block, axis, route)


def own_kernel(
    rate_ref,
    x_far,
    dual_far,
    measured_far,
    data_far,
    x_ref,
    cand_ref,
    sums_ref,
    measured_ref,
    data_ref,
    arrived,
    data_arrived,
):
    channels, rows, cols = x_ref.shape
    tiles = cols // LANES
    parts = arrived.shape[1]
    size = channels // parts
    copies = []
    for part in range(parts):
        some = pl.ds(part * size, size)
        copies.append(
            (
                pltpu.make_async_copy(x_far.at[some], x_ref.at[some], arrived.at[0, part]),
                pltpu.make_async_copy(
                    dual_far.at[:, some], cand_ref.at[:, some], arrived.at[1, part]
                ),
            )
        )
        for copy in copies[-1]:
            copy.start()
    data_copies = (
        pltpu.make_async_copy(measured_far, measured_ref, data_arrived.at[0]),
        pltpu.make_async_copy(data_far, data_ref, data_arrived.at[1]),
    )
    for copy in data_copies:
        copy.start()
    rate = rate_ref[0]
    inner_row = lax.broadcasted_iota(jnp.int32, (rows, LANES), 0) < rows - 1
    edge_lane = lax.broadcasted_iota(jnp.int32, (rows, LANES), 1) == LANES - 1
    for part in range(parts):
        for copy in copies[part]:
            copy.wait()
        for j in range(tiles):
            here = pl.ds(j * LANES, LANES)
            if part:
                sums = [sums_ref[k, :, here] for k in range(len(own_pairs))]
            else:
                sums = [jnp.zeros((rows, LANES), jnp.float32) for _ in own_pairs]
            for c in range(part * size, part * size + size):
                x = x_ref[c, :, here]
                below = pltpu.roll(x, rows - 1, 0)
                right = pltpu.roll(x, LANES - 1, 1)
                if j + 1 < tiles:
                    after = pltpu.roll(x_ref[c, :, pl.ds((j + 1) * LANES, LANES)], LANES - 1, 1)
                else:
                    after = x
                steps = (
                    jnp.where(inner_row, below - x, 0.0),
                    jnp.where(edge_lane, after, right) - x,
                )
                cand = [cand_ref[a, c, :, here] + rate * steps[a] for a in range(2)]
                for a in range(2):
                    cand_ref[a, c, :, here] = cand[a]
                sums = [s + cand[a] * cand[b] for s, (a, b) in zip(sums, own_pairs)]
            for k, s in enumerate(sums):
                sums_ref[k, :, here] = s
    for copy in data_copies:
        copy.wait()


def gram_kernel(
    rate_ref,
    keep_ref,
    projector_far,
    next_ref,
    sums_ref,
    x_ref,
    dual_ref,
    x_same,
    cand_ref,
    out_ref,
    projector_ref,
    arrived,
):
    projector_copy = pltpu.make_async_copy(projector_far, projector_ref, arrived)
    projector_copy.start()
    channels, rows, cols = x_ref.shape
    tiles = cols // LANES
    per_row = len(index_pairs) * tiles
    rate = rate_ref[0]
    keep = keep_ref[0]
    for j in range(tiles):
        here = pl.ds(j * LANES, LANES)
        sums = {pair: sums_ref[k, :, here] for k, pair in enumerate(own_pairs)}
        for b in range(3):
            sums[b, 2] = jnp.zeros((rows, LANES), jnp.float32)
        for c in range(channels):
            step = (next_ref[c, :, here] - x_ref[c, :, here]) * keep
            cand = dual_ref[2, c, :, here] + rate * step
            for b in range(2):
                sums[b, 2] = sums[b, 2] + dual_ref[b, c, :, here] * cand
            sums[2, 2] = sums[2, 2] + cand * cand
            cand_ref[2, c, :, here] = cand
        for k, pair in enumerate(index_pairs):
            out_ref[pl.ds(k * tiles + j, rows, stride=per_row), :] = sums[pair]
    projector_copy.wait()


def pass_on_kernel(parts_ref, misfit_ref, data_ref, out_ref, data_same):
    peers, per_row, _ = parts_ref.shape
    total = parts_ref[0]
    for p in range(1, peers):
        total = total + parts_ref[p]
    misfit = misfit_ref[...]
    for p in range(out_ref.shape[0]):
        out_ref[p, :per_row, :] = total
        out_ref[p, per_row:, :] = misfit


def rotate(entry, vectors, p, q):
    k = 3 - p - q
    pq, kp, kq = (entry_of[tuple(sorted(s))] for s in ((p, q), (k, p), (k, q)))
    across, twice = entry[q] - entry[p], 2.0 * entry[pq]
    square = across * across + twice * twice
    still = square == 0.0
    inverse = lax.rsqrt(jnp.where(still, 1.0, square))
    length = square * inverse
    half = jnp.where(still, 1.0, 0.5 + 0.5 * jnp.abs(across) * inverse)
    root = lax.rsqrt(half)
    large, small = half * root, 0.5 * jnp.abs(twice) * inverse * root
    ahead = across >= 0.0
    cosine = jnp.where(ahead, large, small)
    sine = jnp.where(ahead, small, large)
    sine = jnp.where(twice < 0.0, -sine, sine)
    middle = entry[p] + entry[q]
    entry, vectors = list(entry), [list(row) for row in vectors]
    entry[p], entry[q] = 0.5 * (middle - length), 0.5 * (middle + length)
    entry[pq] = jnp.where(still, entry[pq], 0.0)
    entry[kp], entry[kq] = (
        cosine * entry[kp] - sine * entry[kq],
        sine * entry[kp] + cosine * entry[kq],
    )
    for row in vectors:
        row[p], row[q] = cosine * row[p] - sine * row[q], sine * row[p] + cosine * row[q]
    return entry, vectors


def factor_kernel(channels, weight_ref, parts_ref, back_ref, out_ref, back_same):
    peers, held, _ = parts_ref.shape
    entries = len(index_pairs)
    tiles = out_ref.shape[1] // (entries + 2)

    def summed(start, size):
        total = parts_ref[0, pl.ds(start, size), :]
        for p in range(1, peers):
            total = total + parts_ref[p, pl.ds(start, size), :]
        return total

    radius = weight_ref[0] * math.sqrt(channels)
    entry = [summed(k * tiles, tiles) for k in range(entries)]
    one, zero = jnp.ones_like(entry[0]), jnp.zeros_like(entry[0])
    vectors = [[one if r == c else zero for c in range(3)] for r in range(3)]
    for _ in range(SWEEPS):
        for p, q in sweep_order:
            entry, vectors = rotate(entry, vectors, p, q)
    roots = [jnp.sqrt(jnp.maximum(entry[d], 0.0)) for d in range(3)]
    scales = [radius / jnp.maximum(root, radius) for root in roots]
    excess = sum(jnp.maximum(root - radius, 0.0) for root in roots) / radius
    misfit = sum(summed(k, tiles) for k in range(entries * tiles, held, tiles))
    rows = [
        sum(vectors[a][d] * scales[d] * vectors[b][d] for d in range(3)) for a, b in index_pairs
    ] + [misfit, excess]
    for p in range(out_ref.shape[0]):
        for k, row in enumerate(rows):
            out_ref[p, pl.ds(k * tiles, tiles), :] = row


def factor_image(factor_ref, rows, tiles):
    per_row = factor_ref.shape[0] // rows

    def image(k, j):
        return factor_ref[pl.ds(k * tiles + j, rows, stride=per_row), :]

    return image


def entry_at(a, b):
    return entry_of[tuple(sorted((a, b)))]


def slice_kernel(factor_ref, cand_ref, new_ref, sums_ref):
    _, channels, rows, cols = cand_ref.shape
    tiles = cols // LANES
    image = factor_image(factor_ref, rows, tiles)
    for j in range(tiles):
        here = pl.ds(j * LANES, LANES)
        factor = [image(entry_at(b, 2), j) for b in range(3)]
        for c in range(channels):
            new_ref[c, :, here] = sum(cand_ref[b, c, :, here] * factor[b] for b in range(3))
    per_row = factor_ref.shape[0] // rows
    slabs, count, _ = sums_ref.shape
    size = count * tiles
    total = sum(
        factor_ref[pl.ds(r * per_row + per_row - size, size), :] for r in range(rows)
    )
    for k in range(count):
        row = jnp.sum(total[k * tiles : (k + 1) * tiles], axis=0, keepdims=True)
        for p in range(slabs):
            sums_ref[p, pl.ds(k, 1), :] = row


def rest_kernel(
    rate_ref,
    keep_ref,
    factor_ref,
    cand_ref,
    slice_ref,
    volume_ref,
    back_ref,
    data_ref,
    new_ref,
    ready_ref,
    data_out,
):
    _, channels, rows, cols = cand_ref.shape
    tiles = cols // LANES
    rate = rate_ref[0]
    keep = keep_ref[0]
    image = factor_image(factor_ref, rows, tiles)
    data_out[...] = data_ref[...]
    row_id = lax.broadcasted_iota(jnp.int32, (rows, LANES), 0)
    lane_id = lax.broadcasted_iota(jnp.int32, (rows, LANES), 1)
    before = [None] * channels
    for j in range(tiles):
        here = pl.ds(j * LANES, LANES)
        factor = [[image(entry_at(b, a), j) for b in range(3)] for a in range(2)]
        for c in range(channels):
            cand = [cand_ref[b, c, :, here] for b in range(3)]
            new = [sum(cand[b] * factor[a][b] for b in range(3)) for a in range(2)]
            along = slice_ref[c, :, here]
            for a in range(2):
                new_ref[a, c, :, here] = new[a]
            new_ref[2, c, :, here] = along
            kept = jnp.where(row_id < rows - 1, new[0], 0.0)
            spread = kept - jnp.where(row_id > 0, pltpu.roll(new[0], 1, 0), 0.0)
            left = pltpu.roll(new[1], 1, 1)
            earlier = jnp.where(lane_id > 0, left, 0.0 if j == 0 else before[c])
            before[c] = left
            kept = new[1] if j + 1 < tiles else jnp.where(lane_id < LANES - 1, new[1], 0.0)
            spread = spread + (kept - earlier) + keep * along
            ready_ref[c, :, here] = volume_ref[c, :, here] - rate * (back_ref[c, :, here] - spread)


def finish_kernel(counts, rate_ref, ready_ref, prior_ref, sums_ref, updated_ref, totals_ref):
    rate = rate_ref[0]
    for c in range(ready_ref.shape[0]):
        updated_ref[c] = jnp.maximum(ready_ref[c] - rate * prior_ref[c], 0.0)
    total = sums_ref[0]
    for p in range(1, sums_ref.shape[0]):
        total = total + sums_ref[p]
    for k, count in enumerate(counts):
        totals_ref[k] = jnp.sum(total[k : k + 1]) / count


def picked_blocks(blocks, where, count):
    chosen = (where[:, None] == jnp.arange(count, dtype=jnp.int32)[None, :]).astype(jnp.bfloat16)
    return jnp.einsum("tc,bcj->tbj", chosen, blocks, preferred_element_type=jnp.float32).astype(
        jnp.bfloat16
    )


def gathered_products(products, where, count):
    chosen = (where[:, None] == jnp.arange(count, dtype=jnp.int32)[None, :]).astype(jnp.float32)
    return jnp.einsum("tc,tbj->bcj", chosen, products, precision=lax.Precision.HIGHEST)


def on_device(
    volume_now,
    extrapolated,
    dual_grad,
    dual_data,
    measured,
    projector,
    tile_rows,
    tile_cols,
    dual_step,
    primal_step,
    reg_weight,
):
    f32 = jnp.float32
    dual_rate = dual_step[0]
    channels, slices, row_count, col_count = volume_now.shape
    pixels = row_count * col_count
    rays = dual_data.shape[2]
    edge = projector.shape[1]
    share_count, far_count = lax.axis_size(SHARE), lax.axis_size(FAR)
    slab_count = lax.axis_size("slab")
    total_channels = channels * share_count * far_count
    tiles = col_count // LANES
    held = len(index_pairs) * tiles
    last_slice = lax.axis_index("slab") == slab_count - 1
    images = (channels, row_count, col_count)

    keep = jnp.where(last_slice, 0.0, 1.0).reshape(1)
    image_form = jax.ShapeDtypeStruct(images, f32)

    following = from_behind(extrapolated, "slab", -1)
    sinogram = (channels, rays // edge, edge)
    x_near, duals, own_sums, measured_near, data_near = pl.pallas_call(
        own_kernel,
        out_shape=(
            kept_near(images),
            kept_near((3, *images)),
            kept_near((len(own_pairs), row_count, col_count)),
            kept_near(sinogram),
            kept_near(sinogram),
        ),
        in_specs=[SMEM] + [ANY] * 4,
        out_specs=(VMEM,) * 5,
        scratch_shapes=[pltpu.SemaphoreType.DMA((2, 4)), pltpu.SemaphoreType.DMA((2,))],
        compiler_params=SCRATCH,
        name="own",
    )(
        dual_step,
        left_far(extrapolated.reshape(images)),
        left_far(dual_grad.reshape(3, *images)),
        left_far(measured.reshape(sinogram)),
        left_far(dual_data.reshape(sinogram)),
    )
    x_near, candidate, partial_gram, projector_near = pl.pallas_call(
        gram_kernel,
        out_shape=(
            kept_near(images),
            kept_near((3, *images)),
            jax.ShapeDtypeStruct((row_count * held, LANES), f32),
            pltpu.VMEM(projector.shape, projector.dtype),
        ),
        in_specs=[SMEM, SMEM, ANY, VMEM, VMEM, VMEM, VMEM],
        out_specs=(VMEM,) * 4,
        scratch_shapes=[pltpu.SemaphoreType.DMA(())],
        input_output_aliases={5: 0, 6: 1},
        compiler_params=SCRATCH,
        name="gram",
    )(
        dual_step,
        keep,
        left_far(projector),
        near(following.reshape(images)),
        near(own_sums),
        near(x_near),
        near(duals),
    )
    share_order = [by_distance(SHARE, (2, 1, 1))]
    far_order = [by_distance((FAR,), (far_count // 2,))]
    slab_order = [by_distance(("slab",), (1,))]
    gram_parts = lax.all_to_all(
        partial_gram.reshape(share_count, held, LANES),
        SHARE,
        0,
        0,
        axis_index_groups=share_order,
        tiled=True,
    )

    rounded = x_near.reshape(channels, pixels // edge, edge).astype(jnp.bfloat16)
    picked = picked_blocks(rounded, tile_cols, pixels // edge)
    products = jnp.einsum("tij,tbj->tbi", projector_near, picked, preferred_element_type=f32)
    projected = gathered_products(products, tile_rows, rays // edge)
    residual = projected - measured_near
    data_new = (data_near + dual_rate * residual) / (1.0 + dual_rate)
    misfit_part = jnp.sum((residual * residual).reshape(-1, 8, LANES), axis=0)

    to_far, data_new = pl.pallas_call(
        pass_on_kernel,
        out_shape=(
            jax.ShapeDtypeStruct((far_count, held + 8, LANES), f32),
            kept_near(data_new.shape),
        ),
        in_specs=[VMEM, VMEM, VMEM],
        out_specs=(VMEM, VMEM),
        input_output_aliases={2: 1},
        compiler_params=SCRATCH,
        name="pass_on",
    )(near(gram_parts), near(misfit_part), near(data_new))
    far_parts = lax.all_to_all(to_far, FAR, 0, 0, axis_index_groups=far_order, tiled=True)

    data_low = data_new.astype(jnp.bfloat16)
    picked_back = picked_blocks(data_low, tile_rows, rays // edge)
    products_back = jnp.einsum("tij,tbi->tbj", projector_near, picked_back, preferred_element_type=f32)
    back_proj = gathered_products(products_back, tile_cols, pixels // edge).reshape(
        volume_now.shape
    )

    to_share, back_proj = pl.pallas_call(
        functools.partial(factor_kernel, total_channels),
        out_shape=(
            kept_near((share_count, held + 2 * tiles, LANES)),
            kept_near(images),
        ),
        in_specs=[SMEM, VMEM, VMEM],
        out_specs=(VMEM, VMEM),
        input_output_aliases={2: 1},
        compiler_params=SCRATCH,
        name="factor",
    )(reg_weight, near(far_parts), near(back_proj.reshape(images)))
    factor_rows = lax.all_to_all(
        to_share, SHARE, 0, 0, axis_index_groups=share_order, tiled=True
    )
    factor_near = near(factor_rows.reshape(-1, LANES))

    new_slice, sums = pl.pallas_call(
        slice_kernel,
        out_shape=(kept_near(images), jax.ShapeDtypeStruct((slab_count, 2, LANES), f32)),
        in_specs=[VMEM, VMEM],
        out_specs=(VMEM, VMEM),
        compiler_params=SCRATCH,
        name="slice",
    )(factor_near, near(candidate))
    prior_layer = from_behind(new_slice, "slab", 1)
    all_sums = lax.all_to_all(sums, "slab", 0, 0, axis_index_groups=slab_order, tiled=True)
    grad_new, ready, data_out = pl.pallas_call(
        rest_kernel,
        out_shape=(
            jax.ShapeDtypeStruct((3, *images), f32),
            kept_near(images),
            jax.ShapeDtypeStruct(sinogram, f32),
        ),
        in_specs=[SMEM, SMEM] + [VMEM] * 6,
        out_specs=(VMEM, VMEM, VMEM),
        compiler_params=SCRATCH,
        name="rest",
    )(
        primal_step,
        keep,
        factor_near,
        near(candidate),
        near(new_slice),
        near(volume_now.reshape(images)),
        near(back_proj),
        near(data_new),
    )
    counts = (total_channels * slab_count * slices * rays, slab_count * slices * pixels)
    updated, totals = pl.pallas_call(
        functools.partial(finish_kernel, counts),
        out_shape=(image_form, jax.ShapeDtypeStruct((2,), f32)),
        in_specs=[SMEM, VMEM, VMEM, VMEM],
        out_specs=(VMEM, SMEM),
        compiler_params=SCRATCH,
        name="finish",
    )(primal_step, near(ready), near(prior_layer), near(all_sums))
    return (
        updated.reshape(volume_now.shape),
        grad_new.reshape(dual_grad.shape),
        data_out.reshape(dual_data.shape),
        totals,
    )


def solution(mesh):
    torus = Mesh(
        mesh.devices.reshape(4, 2, 8, 2, mesh.shape["slab"]), ("x", "y", "zfar", "znear", "slab")
    )
    placed = (
        P(CHAN, "slab", None, None),
        P(CHAN, "slab", None, None),
        P(None, CHAN, "slab", None, None),
        P(CHAN, "slab", None),
        P(CHAN, "slab", None),
        P(),
        P(),
        P(),
        P(),
        P(),
        P(),
    )
    return jax.shard_map(
        on_device,
        mesh=torus,
        in_specs=placed,
        out_specs=(
            P(CHAN, "slab", None, None),
            P(None, CHAN, "slab", None, None),
            P(CHAN, "slab", None),
            P(),
        ),
        check_vma=False,
    )
```

```python
import functools
import itertools
import math

import jax
import jax.numpy as jnp
from jax import lax
from jax.experimental import pallas as pl
from jax.experimental.pallas import tpu as pltpu
from jax.sharding import Mesh
from jax.sharding import PartitionSpec as P

SWEEPS = 6
CHAN = ("x", "y", "zfar", "znear")
SHARE = ("x", "y", "znear")
FAR = "zfar"
LANES = 128

index_pairs = ((0, 0), (1, 1), (2, 2), (0, 1), (0, 2), (1, 2))
entry_of = {pair: k for k, pair in enumerate(index_pairs)}
sweep_order = ((0, 1), (0, 2), (1, 2))
own_pairs = ((0, 0), (1, 1), (0, 1))

VMEM = pl.BlockSpec(memory_space=pltpu.VMEM)
SMEM = pl.BlockSpec(memory_space=pltpu.SMEM)
ANY = pl.BlockSpec(memory_space=pl.ANY)
SCRATCH = pltpu.CompilerParams(vmem_limit_bytes=6 * 2**20)


def near(array):
    return pltpu.with_memory_space_constraint(array, pltpu.VMEM)


def left_far(array):
    return pltpu.with_memory_space_constraint(array, pltpu.HBM)


def kept_near(shape):
    return pltpu.VMEM(shape, jnp.float32)


def by_distance(axes, first):
    sizes = [lax.axis_size(axis) for axis in axes]
    places = list(itertools.product(*map(range, sizes)))

    def away(place):
        return sum(min((a - b) % n, (b - a) % n) for a, b, n in zip(place, first, sizes))

    order = sorted(range(len(places)), key=lambda i: -away(places[i]))
    order.remove(places.index(first))
    return [places.index(first), *order]


def from_behind(block, axis, distance):
    devices = range(lax.axis_size(axis))
    route = [(i - distance, i) for i in devices if i - distance in devices]
    return lax.ppermute(block, axis, route)


def own_kernel(
    rate_ref,
    x_far,
    dual_far,
    projector_far,
    x_ref,
    cand_ref,
    sums_ref,
    projector_ref,
    arrived,
    projector_arrived,
):
    channels, rows, cols = x_ref.shape
    tiles = cols // LANES
    parts = arrived.shape[1]
    size = channels // parts
    copies = []
    for part in range(parts):
        some = pl.ds(part * size, size)
        copies.append(
            (
                pltpu.make_async_copy(x_far.at[some], x_ref.at[some], arrived.at[0, part]),
                pltpu.make_async_copy(
                    dual_far.at[:, some], cand_ref.at[:, some], arrived.at[1, part]
                ),
            )
        )
        for copy in copies[-1]:
            copy.start()
    projector_copies = []
    pieces = projector_arrived.shape[0]
    size_in = projector_ref.shape[0] // pieces
    for piece in range(pieces):
        some = pl.ds(piece * size_in, size_in)
        projector_copies.append(
            pltpu.make_async_copy(
                projector_far.at[some], projector_ref.at[some], projector_arrived.at[piece]
            )
        )
    for copy in projector_copies:
        copy.start()
    rate = rate_ref[0]
    inner_row = lax.broadcasted_iota(jnp.int32, (rows, LANES), 0) < rows - 1
    edge_lane = lax.broadcasted_iota(jnp.int32, (rows, LANES), 1) == LANES - 1
    for part in range(parts):
        for copy in copies[part]:
            copy.wait()
        for j in range(tiles):
            here = pl.ds(j * LANES, LANES)
            if part:
                sums = [sums_ref[k, :, here] for k in range(len(own_pairs))]
            else:
                sums = [jnp.zeros((rows, LANES), jnp.float32) for _ in own_pairs]
            for c in range(part * size, part * size + size):
                x = x_ref[c, :, here]
                below = pltpu.roll(x, rows - 1, 0)
                right = pltpu.roll(x, LANES - 1, 1)
                if j + 1 < tiles:
                    after = pltpu.roll(x_ref[c, :, pl.ds((j + 1) * LANES, LANES)], LANES - 1, 1)
                else:
                    after = x
                steps = (
                    jnp.where(inner_row, below - x, 0.0),
                    jnp.where(edge_lane, after, right) - x,
                )
                cand = [cand_ref[a, c, :, here] + rate * steps[a] for a in range(2)]
                for a in range(2):
                    cand_ref[a, c, :, here] = cand[a]
                sums = [s + cand[a] * cand[b] for s, (a, b) in zip(sums, own_pairs)]
            for k, s in enumerate(sums):
                sums_ref[k, :, here] = s
    for copy in projector_copies:
        copy.wait()


def gram_kernel(
    rate_ref,
    keep_ref,
    next_ref,
    sums_ref,
    x_ref,
    dual_ref,
    x_same,
    cand_ref,
    out_ref,
):
    channels, rows, cols = x_ref.shape
    tiles = cols // LANES
    per_row = len(index_pairs) * tiles
    rate = rate_ref[0]
    keep = keep_ref[0]
    for j in range(tiles):
        here = pl.ds(j * LANES, LANES)
        sums = {pair: sums_ref[k, :, here] for k, pair in enumerate(own_pairs)}
        for b in range(3):
            sums[b, 2] = jnp.zeros((rows, LANES), jnp.float32)
        for c in range(channels):
            step = (next_ref[c, :, here] - x_ref[c, :, here]) * keep
            cand = dual_ref[2, c, :, here] + rate * step
            for b in range(2):
                sums[b, 2] = sums[b, 2] + dual_ref[b, c, :, here] * cand
            sums[2, 2] = sums[2, 2] + cand * cand
            cand_ref[2, c, :, here] = cand
        for k, pair in enumerate(index_pairs):
            out_ref[pl.ds(k * tiles + j, rows, stride=per_row), :] = sums[pair]


def pass_on_kernel(parts_ref, residual_ref, data_ref, out_ref, data_same):
    peers, per_row, _ = parts_ref.shape
    total = parts_ref[0]
    for p in range(1, peers):
        total = total + parts_ref[p]
    misfit = jnp.zeros((out_ref.shape[1] - per_row, LANES), jnp.float32)
    for c in range(residual_ref.shape[0]):
        for start in range(0, residual_ref.shape[1], misfit.shape[0]):
            some = residual_ref[c, pl.ds(start, misfit.shape[0]), :]
            misfit = misfit + some * some
    for p in range(out_ref.shape[0]):
        out_ref[p, :per_row, :] = total
        out_ref[p, per_row:, :] = misfit


def rotate(entry, vectors, p, q):
    k = 3 - p - q
    pq, kp, kq = (entry_of[tuple(sorted(s))] for s in ((p, q), (k, p), (k, q)))
    across, twice = entry[q] - entry[p], 2.0 * entry[pq]
    square = across * across + twice * twice
    still = square == 0.0
    inverse = lax.rsqrt(jnp.where(still, 1.0, square))
    length = square * inverse
    half = jnp.where(still, 1.0, 0.5 + 0.5 * jnp.abs(across) * inverse)
    root = lax.rsqrt(half)
    large, small = half * root, 0.5 * jnp.abs(twice) * inverse * root
    ahead = across >= 0.0
    cosine = jnp.where(ahead, large, small)
    sine = jnp.where(ahead, small, large)
    sine = jnp.where(twice < 0.0, -sine, sine)
    middle = entry[p] + entry[q]
    entry, vectors = list(entry), [list(row) for row in vectors]
    entry[p], entry[q] = 0.5 * (middle - length), 0.5 * (middle + length)
    entry[pq] = jnp.where(still, entry[pq], 0.0)
    entry[kp], entry[kq] = (
        cosine * entry[kp] - sine * entry[kq],
        sine * entry[kp] + cosine * entry[kq],
    )
    for row in vectors:
        row[p], row[q] = cosine * row[p] - sine * row[q], sine * row[p] + cosine * row[q]
    return entry, vectors


def factor_kernel(channels, weight_ref, parts_ref, back_ref, out_ref, back_same):
    peers, held, _ = parts_ref.shape
    entries = len(index_pairs)
    tiles = out_ref.shape[1] // (entries + 2)

    def summed(start, size):
        total = parts_ref[0, pl.ds(start, size), :]
        for p in range(1, peers):
            total = total + parts_ref[p, pl.ds(start, size), :]
        return total

    radius = weight_ref[0] * math.sqrt(channels)
    entry = [summed(k * tiles, tiles) for k in range(entries)]
    one, zero = jnp.ones_like(entry[0]), jnp.zeros_like(entry[0])
    vectors = [[one if r == c else zero for c in range(3)] for r in range(3)]
    for _ in range(SWEEPS):
        for p, q in sweep_order:
            entry, vectors = rotate(entry, vectors, p, q)
    roots = [jnp.sqrt(jnp.maximum(entry[d], 0.0)) for d in range(3)]
    scales = [radius / jnp.maximum(root, radius) for root in roots]
    excess = sum(jnp.maximum(root - radius, 0.0) for root in roots) / radius
    misfit = sum(summed(k, tiles) for k in range(entries * tiles, held, tiles))
    rows = [
        sum(vectors[a][d] * scales[d] * vectors[b][d] for d in range(3)) for a, b in index_pairs
    ] + [misfit, excess]
    for p in range(out_ref.shape[0]):
        for k, row in enumerate(rows):
            out_ref[p, pl.ds(k * tiles, tiles), :] = row


def factor_image(factor_ref, rows, tiles):
    per_row = factor_ref.shape[0] // rows

    def image(k, j):
        return factor_ref[pl.ds(k * tiles + j, rows, stride=per_row), :]

    return image


def entry_at(a, b):
    return entry_of[tuple(sorted((a, b)))]


def slice_kernel(factor_ref, cand_ref, new_ref, sums_ref):
    _, channels, rows, cols = cand_ref.shape
    tiles = cols // LANES
    image = factor_image(factor_ref, rows, tiles)
    for j in range(tiles):
        here = pl.ds(j * LANES, LANES)
        factor = [image(entry_at(b, 2), j) for b in range(3)]
        for c in range(channels):
            new_ref[c, :, here] = sum(cand_ref[b, c, :, here] * factor[b] for b in range(3))
    per_row = factor_ref.shape[0] // rows
    slabs, count, _ = sums_ref.shape
    size = count * tiles
    total = sum(
        factor_ref[pl.ds(r * per_row + per_row - size, size), :] for r in range(rows)
    )
    for k in range(count):
        row = jnp.sum(total[k * tiles : (k + 1) * tiles], axis=0, keepdims=True)
        for p in range(slabs):
            sums_ref[p, pl.ds(k, 1), :] = row


def rest_kernel(
    rate_ref,
    keep_ref,
    factor_ref,
    cand_ref,
    slice_ref,
    volume_ref,
    back_ref,
    data_ref,
    new_ref,
    ready_ref,
    data_out,
):
    _, channels, rows, cols = cand_ref.shape
    tiles = cols // LANES
    rate = rate_ref[0]
    keep = keep_ref[0]
    image = factor_image(factor_ref, rows, tiles)
    data_out[...] = data_ref[...]
    row_id = lax.broadcasted_iota(jnp.int32, (rows, LANES), 0)
    lane_id = lax.broadcasted_iota(jnp.int32, (rows, LANES), 1)
    before = [None] * channels
    for j in range(tiles):
        here = pl.ds(j * LANES, LANES)
        factor = [[image(entry_at(b, a), j) for b in range(3)] for a in range(2)]
        for c in range(channels):
            cand = [cand_ref[b, c, :, here] for b in range(3)]
            new = [sum(cand[b] * factor[a][b] for b in range(3)) for a in range(2)]
            along = slice_ref[c, :, here]
            for a in range(2):
                new_ref[a, c, :, here] = new[a]
            new_ref[2, c, :, here] = along
            kept = jnp.where(row_id < rows - 1, new[0], 0.0)
            spread = kept - jnp.where(row_id > 0, pltpu.roll(new[0], 1, 0), 0.0)
            left = pltpu.roll(new[1], 1, 1)
            earlier = jnp.where(lane_id > 0, left, 0.0 if j == 0 else before[c])
            before[c] = left
            kept = new[1] if j + 1 < tiles else jnp.where(lane_id < LANES - 1, new[1], 0.0)
            spread = spread + (kept - earlier) + keep * along
            ready_ref[c, :, here] = volume_ref[c, :, here] - rate * (back_ref[c, :, here] - spread)


def finish_kernel(counts, rate_ref, ready_ref, prior_ref, sums_ref, updated_ref, totals_ref):
    rate = rate_ref[0]
    for c in range(ready_ref.shape[0]):
        updated_ref[c] = jnp.maximum(ready_ref[c] - rate * prior_ref[c], 0.0)
    total = sums_ref[0]
    for p in range(1, sums_ref.shape[0]):
        total = total + sums_ref[p]
    for k, count in enumerate(counts):
        totals_ref[k] = jnp.sum(total[k : k + 1]) / count


def picked_blocks(blocks, where, count):
    chosen = (where[:, None] == jnp.arange(count, dtype=jnp.int32)[None, :]).astype(jnp.bfloat16)
    return jnp.einsum("tc,bcj->tbj", chosen, blocks, preferred_element_type=jnp.float32).astype(
        jnp.bfloat16
    )


def gathered_products(products, where, count):
    chosen = (where[:, None] == jnp.arange(count, dtype=jnp.int32)[None, :]).astype(jnp.float32)
    return jnp.einsum("tc,tbj->bcj", chosen, products, precision=lax.Precision.HIGHEST)


def on_device(
    volume_now,
    extrapolated,
    dual_grad,
    dual_data,
    measured,
    projector,
    tile_rows,
    tile_cols,
    dual_step,
    primal_step,
    reg_weight,
):
    f32 = jnp.float32
    dual_rate = dual_step[0]
    channels, slices, row_count, col_count = volume_now.shape
    pixels = row_count * col_count
    rays = dual_data.shape[2]
    edge = projector.shape[1]
    share_count, far_count = lax.axis_size(SHARE), lax.axis_size(FAR)
    slab_count = lax.axis_size("slab")
    total_channels = channels * share_count * far_count
    tiles = col_count // LANES
    held = len(index_pairs) * tiles
    last_slice = lax.axis_index("slab") == slab_count - 1
    images = (channels, row_count, col_count)

    keep = jnp.where(last_slice, 0.0, 1.0).reshape(1)
    image_form = jax.ShapeDtypeStruct(images, f32)

    following = from_behind(extrapolated, "slab", -1)
    sinogram = (channels, rays // edge, edge)
    x_near, duals, own_sums, projector_near = pl.pallas_call(
        own_kernel,
        out_shape=(
            kept_near(images),
            kept_near((3, *images)),
            kept_near((len(own_pairs), row_count, col_count)),
            pltpu.VMEM(projector.shape, projector.dtype),
        ),
        in_specs=[SMEM] + [ANY] * 3,
        out_specs=(VMEM,) * 4,
        scratch_shapes=[pltpu.SemaphoreType.DMA(n) for n in ((2, 4), (8,))],
        compiler_params=SCRATCH,
        name="own",
    )(
        dual_step,
        left_far(extrapolated.reshape(images)),
        left_far(dual_grad.reshape(3, *images)),
        left_far(projector),
    )
    x_near, candidate, partial_gram = pl.pallas_call(
        gram_kernel,
        out_shape=(
            kept_near(images),
            kept_near((3, *images)),
            jax.ShapeDtypeStruct((row_count * held, LANES), f32),
        ),
        in_specs=[SMEM, SMEM, VMEM, VMEM, VMEM, VMEM],
        out_specs=(VMEM,) * 3,
        input_output_aliases={4: 0, 5: 1},
        compiler_params=SCRATCH,
        name="gram",
    )(
        dual_step,
        keep,
        near(following.reshape(images)),
        near(own_sums),
        near(x_near),
        near(duals),
    )
    share_order = [by_distance(SHARE, (2, 1, 1))]
    far_order = [by_distance((FAR,), (far_count // 2,))]
    gram_parts = lax.all_to_all(
        partial_gram.reshape(share_count, held, LANES),
        SHARE,
        0,
        0,
        axis_index_groups=share_order,
        tiled=True,
    )

    rounded = x_near.reshape(channels, pixels // edge, edge).astype(jnp.bfloat16)
    picked = picked_blocks(rounded, tile_cols, pixels // edge)
    products = jnp.einsum("tij,tbj->tbi", projector_near, picked, preferred_element_type=f32)
    projected = gathered_products(products, tile_rows, rays // edge)
    residual = projected - measured.reshape(sinogram)
    data_new = (dual_data.reshape(sinogram) + dual_rate * residual) / (1.0 + dual_rate)

    to_far, data_new = pl.pallas_call(
        pass_on_kernel,
        out_shape=(
            jax.ShapeDtypeStruct((far_count, held + 8, LANES), f32),
            kept_near(data_new.shape),
        ),
        in_specs=[VMEM, VMEM, VMEM],
        out_specs=(VMEM, VMEM),
        input_output_aliases={2: 1},
        compiler_params=SCRATCH,
        name="pass_on",
    )(near(gram_parts), near(residual), near(data_new))
    far_parts = lax.all_to_all(to_far, FAR, 0, 0, axis_index_groups=far_order, tiled=True)

    data_low = data_new.astype(jnp.bfloat16)
    picked_back = picked_blocks(data_low, tile_rows, rays // edge)
    products_back = jnp.einsum("tij,tbi->tbj", projector_near, picked_back, preferred_element_type=f32)
    back_proj = gathered_products(products_back, tile_cols, pixels // edge).reshape(
        volume_now.shape
    )

    to_share, back_proj = pl.pallas_call(
        functools.partial(factor_kernel, total_channels),
        out_shape=(
            kept_near((share_count, held + 2 * tiles, LANES)),
            kept_near(images),
        ),
        in_specs=[SMEM, VMEM, VMEM],
        out_specs=(VMEM, VMEM),
        input_output_aliases={2: 1},
        compiler_params=SCRATCH,
        name="factor",
    )(reg_weight, near(far_parts), near(back_proj.reshape(images)))
    factor_rows = lax.all_to_all(
        to_share, SHARE, 0, 0, axis_index_groups=share_order, tiled=True
    )
    factor_near = near(factor_rows.reshape(-1, LANES))

    new_slice, sums = pl.pallas_call(
        slice_kernel,
        out_shape=(kept_near(images), jax.ShapeDtypeStruct((slab_count, 2, LANES), f32)),
        in_specs=[VMEM, VMEM],
        out_specs=(VMEM, VMEM),
        compiler_params=SCRATCH,
        name="slice",
    )(factor_near, near(candidate))
    prior_layer = from_behind(new_slice, "slab", 1)
    all_sums = lax.all_to_all(sums, "slab", 0, 0, tiled=True)
    grad_new, ready, data_out = pl.pallas_call(
        rest_kernel,
        out_shape=(
            jax.ShapeDtypeStruct((3, *images), f32),
            kept_near(images),
            jax.ShapeDtypeStruct(sinogram, f32),
        ),
        in_specs=[SMEM, SMEM] + [VMEM] * 6,
        out_specs=(VMEM, VMEM, VMEM),
        compiler_params=SCRATCH,
        name="rest",
    )(
        primal_step,
        keep,
        factor_near,
        near(candidate),
        near(new_slice),
        near(volume_now.reshape(images)),
        near(back_proj),
        near(data_new),
    )
    counts = (total_channels * slab_count * slices * rays, slab_count * slices * pixels)
    updated, totals = pl.pallas_call(
        functools.partial(finish_kernel, counts),
        out_shape=(image_form, jax.ShapeDtypeStruct((2,), f32)),
        in_specs=[SMEM, VMEM, VMEM, VMEM],
        out_specs=(VMEM, SMEM),
        compiler_params=SCRATCH,
        name="finish",
    )(primal_step, near(ready), near(prior_layer), near(all_sums))
    return (
        updated.reshape(volume_now.shape),
        grad_new.reshape(dual_grad.shape),
        data_out.reshape(dual_data.shape),
        totals,
    )


def solution(mesh):
    torus = Mesh(
        mesh.devices.reshape(4, 2, 8, 2, mesh.shape["slab"]), ("x", "y", "zfar", "znear", "slab")
    )
    placed = (
        P(CHAN, "slab", None, None),
        P(CHAN, "slab", None, None),
        P(None, CHAN, "slab", None, None),
        P(CHAN, "slab", None),
        P(CHAN, "slab", None),
        P(),
        P(),
        P(),
        P(),
        P(),
        P(),
    )
    return jax.shard_map(
        on_device,
        mesh=torus,
        in_specs=placed,
        out_specs=(
            P(CHAN, "slab", None, None),
            P(None, CHAN, "slab", None, None),
            P(CHAN, "slab", None),
            P(),
        ),
        check_vma=False,
    )
```

```python
import functools
import itertools
import math

import jax
import jax.numpy as jnp
from jax import lax
from jax.experimental import pallas as pl
from jax.experimental.pallas import tpu as pltpu
from jax.sharding import Mesh
from jax.sharding import PartitionSpec as P

SWEEPS = 6
CHAN = ("x", "y", "zfar", "znear")
SHARE = ("x", "y", "znear")
FAR = "zfar"
LANES = 128

index_pairs = ((0, 0), (1, 1), (2, 2), (0, 1), (0, 2), (1, 2))
entry_of = {pair: k for k, pair in enumerate(index_pairs)}
sweep_order = ((0, 1), (0, 2), (1, 2))
own_pairs = ((0, 0), (1, 1), (0, 1))

VMEM = pl.BlockSpec(memory_space=pltpu.VMEM)
SMEM = pl.BlockSpec(memory_space=pltpu.SMEM)
ANY = pl.BlockSpec(memory_space=pl.ANY)
SCRATCH = pltpu.CompilerParams(vmem_limit_bytes=6 * 2**20)


def near(array):
    return pltpu.with_memory_space_constraint(array, pltpu.VMEM)


def left_far(array):
    return pltpu.with_memory_space_constraint(array, pltpu.HBM)


def kept_near(shape):
    return pltpu.VMEM(shape, jnp.float32)


def by_distance(axes, first):
    sizes = [lax.axis_size(axis) for axis in axes]
    places = list(itertools.product(*map(range, sizes)))

    def away(place):
        return sum(min((a - b) % n, (b - a) % n) for a, b, n in zip(place, first, sizes))

    order = sorted(range(len(places)), key=lambda i: -away(places[i]))
    order.remove(places.index(first))
    return [places.index(first), *order]


def from_behind(block, axis, distance):
    devices = range(lax.axis_size(axis))
    route = [(i - distance, i) for i in devices if i - distance in devices]
    return lax.ppermute(block, axis, route)


def own_kernel(
    rate_ref,
    x_far,
    dual_far,
    projector_far,
    x_ref,
    cand_ref,
    sums_ref,
    projector_ref,
    arrived,
    projector_arrived,
):
    channels, rows, cols = x_ref.shape
    tiles = cols // LANES
    parts = arrived.shape[1]
    size = channels // parts
    copies = []
    for part in range(parts):
        some = pl.ds(part * size, size)
        copies.append(
            (
                pltpu.make_async_copy(x_far.at[some], x_ref.at[some], arrived.at[0, part]),
                pltpu.make_async_copy(
                    dual_far.at[:, some], cand_ref.at[:, some], arrived.at[1, part]
                ),
            )
        )
        for copy in copies[-1]:
            copy.start()
    projector_copies = []
    pieces = projector_arrived.shape[0]
    size_in = projector_ref.shape[0] // pieces
    for piece in range(pieces):
        some = pl.ds(piece * size_in, size_in)
        projector_copies.append(
            pltpu.make_async_copy(
                projector_far.at[some], projector_ref.at[some], projector_arrived.at[piece]
            )
        )
    for copy in projector_copies:
        copy.start()
    rate = rate_ref[0]
    inner_row = lax.broadcasted_iota(jnp.int32, (rows, LANES), 0) < rows - 1
    edge_lane = lax.broadcasted_iota(jnp.int32, (rows, LANES), 1) == LANES - 1
    for part in range(parts):
        for copy in copies[part]:
            copy.wait()
        for j in range(tiles):
            here = pl.ds(j * LANES, LANES)
            if part:
                sums = [sums_ref[k, :, here] for k in range(len(own_pairs))]
            else:
                sums = [jnp.zeros((rows, LANES), jnp.float32) for _ in own_pairs]
            for c in range(part * size, part * size + size):
                x = x_ref[c, :, here]
                below = pltpu.roll(x, rows - 1, 0)
                right = pltpu.roll(x, LANES - 1, 1)
                if j + 1 < tiles:
                    after = pltpu.roll(x_ref[c, :, pl.ds((j + 1) * LANES, LANES)], LANES - 1, 1)
                else:
                    after = x
                steps = (
                    jnp.where(inner_row, below - x, 0.0),
                    jnp.where(edge_lane, after, right) - x,
                )
                cand = [cand_ref[a, c, :, here] + rate * steps[a] for a in range(2)]
                for a in range(2):
                    cand_ref[a, c, :, here] = cand[a]
                sums = [s + cand[a] * cand[b] for s, (a, b) in zip(sums, own_pairs)]
            for k, s in enumerate(sums):
                sums_ref[k, :, here] = s
    for copy in projector_copies:
        copy.wait()


def gram_kernel(
    rate_ref,
    keep_ref,
    next_ref,
    sums_ref,
    x_ref,
    dual_ref,
    x_same,
    cand_ref,
    out_ref,
):
    channels, rows, cols = x_ref.shape
    tiles = cols // LANES
    per_row = len(index_pairs) * tiles
    rate = rate_ref[0]
    keep = keep_ref[0]
    for j in range(tiles):
        here = pl.ds(j * LANES, LANES)
        sums = {pair: sums_ref[k, :, here] for k, pair in enumerate(own_pairs)}
        for b in range(3):
            sums[b, 2] = jnp.zeros((rows, LANES), jnp.float32)
        for c in range(channels):
            step = (next_ref[c, :, here] - x_ref[c, :, here]) * keep
            cand = dual_ref[2, c, :, here] + rate * step
            for b in range(2):
                sums[b, 2] = sums[b, 2] + dual_ref[b, c, :, here] * cand
            sums[2, 2] = sums[2, 2] + cand * cand
            cand_ref[2, c, :, here] = cand
        for k, pair in enumerate(index_pairs):
            out_ref[pl.ds(k * tiles + j, rows, stride=per_row), :] = sums[pair]


def pass_on_kernel(weight_ref, parts_ref, residual_ref, back_ref, out_ref, back_same):
    peers, per_row, _ = parts_ref.shape
    total = parts_ref[0]
    for p in range(1, peers):
        total = total + parts_ref[p]
    misfit = jnp.zeros((out_ref.shape[1] - per_row, LANES), jnp.float32)
    for c in range(residual_ref.shape[0]):
        for start in range(0, residual_ref.shape[1], misfit.shape[0]):
            some = residual_ref[c, pl.ds(start, misfit.shape[0]), :]
            misfit = misfit + some * some
    for p in range(out_ref.shape[0]):
        out_ref[p, :per_row, :] = total
        out_ref[p, per_row:, :] = misfit


def rotate(entry, vectors, p, q):
    k = 3 - p - q
    pq, kp, kq = (entry_of[tuple(sorted(s))] for s in ((p, q), (k, p), (k, q)))
    across, twice = entry[q] - entry[p], 2.0 * entry[pq]
    square = across * across + twice * twice
    still = square == 0.0
    inverse = lax.rsqrt(jnp.where(still, 1.0, square))
    length = square * inverse
    half = jnp.where(still, 1.0, 0.5 + 0.5 * jnp.abs(across) * inverse)
    root = lax.rsqrt(half)
    large, small = half * root, 0.5 * jnp.abs(twice) * inverse * root
    ahead = across >= 0.0
    cosine = jnp.where(ahead, large, small)
    sine = jnp.where(ahead, small, large)
    sine = jnp.where(twice < 0.0, -sine, sine)
    middle = entry[p] + entry[q]
    entry, vectors = list(entry), [list(row) for row in vectors]
    entry[p], entry[q] = 0.5 * (middle - length), 0.5 * (middle + length)
    entry[pq] = jnp.where(still, entry[pq], 0.0)
    entry[kp], entry[kq] = (
        cosine * entry[kp] - sine * entry[kq],
        sine * entry[kp] + cosine * entry[kq],
    )
    for row in vectors:
        row[p], row[q] = cosine * row[p] - sine * row[q], sine * row[p] + cosine * row[q]
    return entry, vectors


def factor_kernel(channels, weight_ref, parts_ref, out_ref):
    peers, held, _ = parts_ref.shape
    entries = len(index_pairs)
    tiles = out_ref.shape[1] // (entries + 2)

    def summed(start, size):
        total = parts_ref[0, pl.ds(start, size), :]
        for p in range(1, peers):
            total = total + parts_ref[p, pl.ds(start, size), :]
        return total

    radius = weight_ref[0] * math.sqrt(channels)
    entry = [summed(k * tiles, tiles) for k in range(entries)]
    one, zero = jnp.ones_like(entry[0]), jnp.zeros_like(entry[0])
    vectors = [[one if r == c else zero for c in range(3)] for r in range(3)]
    for _ in range(SWEEPS):
        for p, q in sweep_order:
            entry, vectors = rotate(entry, vectors, p, q)
    roots = [jnp.sqrt(jnp.maximum(entry[d], 0.0)) for d in range(3)]
    scales = [radius / jnp.maximum(root, radius) for root in roots]
    excess = sum(jnp.maximum(root - radius, 0.0) for root in roots) / radius
    misfit = sum(summed(k, tiles) for k in range(entries * tiles, held, tiles))
    rows = [
        sum(vectors[a][d] * scales[d] * vectors[b][d] for d in range(3)) for a, b in index_pairs
    ] + [misfit, excess]
    for p in range(out_ref.shape[0]):
        for k, row in enumerate(rows):
            out_ref[p, pl.ds(k * tiles, tiles), :] = row


def factor_image(factor_ref, rows, tiles):
    per_row = factor_ref.shape[0] // rows

    def image(k, j):
        return factor_ref[pl.ds(k * tiles + j, rows, stride=per_row), :]

    return image


def entry_at(a, b):
    return entry_of[tuple(sorted((a, b)))]


def slice_kernel(factor_ref, cand_ref, new_ref, sums_ref):
    _, channels, rows, cols = cand_ref.shape
    tiles = cols // LANES
    image = factor_image(factor_ref, rows, tiles)
    for j in range(tiles):
        here = pl.ds(j * LANES, LANES)
        factor = [image(entry_at(b, 2), j) for b in range(3)]
        for c in range(channels):
            new_ref[c, :, here] = sum(cand_ref[b, c, :, here] * factor[b] for b in range(3))
    per_row = factor_ref.shape[0] // rows
    slabs, count, _ = sums_ref.shape
    size = count * tiles
    total = sum(
        factor_ref[pl.ds(r * per_row + per_row - size, size), :] for r in range(rows)
    )
    for k in range(count):
        row = jnp.sum(total[k * tiles : (k + 1) * tiles], axis=0, keepdims=True)
        for p in range(slabs):
            sums_ref[p, pl.ds(k, 1), :] = row


def rest_kernel(
    rate_ref,
    keep_ref,
    factor_ref,
    cand_ref,
    slice_ref,
    volume_ref,
    back_ref,
    data_ref,
    new_ref,
    ready_ref,
    data_out,
):
    _, channels, rows, cols = cand_ref.shape
    tiles = cols // LANES
    rate = rate_ref[0]
    keep = keep_ref[0]
    image = factor_image(factor_ref, rows, tiles)
    data_out[...] = data_ref[...]
    row_id = lax.broadcasted_iota(jnp.int32, (rows, LANES), 0)
    lane_id = lax.broadcasted_iota(jnp.int32, (rows, LANES), 1)
    before = [None] * channels
    for j in range(tiles):
        here = pl.ds(j * LANES, LANES)
        factor = [[image(entry_at(b, a), j) for b in range(3)] for a in range(2)]
        for c in range(channels):
            cand = [cand_ref[b, c, :, here] for b in range(3)]
            new = [sum(cand[b] * factor[a][b] for b in range(3)) for a in range(2)]
            along = slice_ref[c, :, here]
            for a in range(2):
                new_ref[a, c, :, here] = new[a]
            new_ref[2, c, :, here] = along
            kept = jnp.where(row_id < rows - 1, new[0], 0.0)
            spread = kept - jnp.where(row_id > 0, pltpu.roll(new[0], 1, 0), 0.0)
            left = pltpu.roll(new[1], 1, 1)
            earlier = jnp.where(lane_id > 0, left, 0.0 if j == 0 else before[c])
            before[c] = left
            kept = new[1] if j + 1 < tiles else jnp.where(lane_id < LANES - 1, new[1], 0.0)
            spread = spread + (kept - earlier) + keep * along
            ready_ref[c, :, here] = volume_ref[c, :, here] - rate * (back_ref[c, :, here] - spread)


def finish_kernel(rate_ref, ready_ref, prior_ref, updated_ref):
    rate = rate_ref[0]
    for c in range(ready_ref.shape[0]):
        updated_ref[c] = jnp.maximum(ready_ref[c] - rate * prior_ref[c], 0.0)


def totals_kernel(counts, sums_ref, updated_far, totals_ref):
    total = sums_ref[0]
    for p in range(1, sums_ref.shape[0]):
        total = total + sums_ref[p]
    for k, count in enumerate(counts):
        totals_ref[k] = jnp.sum(total[k : k + 1]) / count


def picked_blocks(blocks, where, count):
    chosen = (where[:, None] == jnp.arange(count, dtype=jnp.int32)[None, :]).astype(jnp.bfloat16)
    return jnp.einsum("tc,bcj->tbj", chosen, blocks, preferred_element_type=jnp.float32).astype(
        jnp.bfloat16
    )


def gathered_products(products, where, count):
    chosen = (where[:, None] == jnp.arange(count, dtype=jnp.int32)[None, :]).astype(jnp.float32)
    return jnp.einsum("tc,tbj->bcj", chosen, products, precision=lax.Precision.HIGHEST)


def on_device(
    volume_now,
    extrapolated,
    dual_grad,
    dual_data,
    measured,
    projector,
    tile_rows,
    tile_cols,
    dual_step,
    primal_step,
    reg_weight,
):
    f32 = jnp.float32
    dual_rate = dual_step[0]
    channels, slices, row_count, col_count = volume_now.shape
    pixels = row_count * col_count
    rays = dual_data.shape[2]
    edge = projector.shape[1]
    share_count, far_count = lax.axis_size(SHARE), lax.axis_size(FAR)
    slab_count = lax.axis_size("slab")
    total_channels = channels * share_count * far_count
    tiles = col_count // LANES
    held = len(index_pairs) * tiles
    last_slice = lax.axis_index("slab") == slab_count - 1
    images = (channels, row_count, col_count)

    keep = jnp.where(last_slice, 0.0, 1.0).reshape(1)
    image_form = jax.ShapeDtypeStruct(images, f32)

    following = from_behind(extrapolated, "slab", -1)
    sinogram = (channels, rays // edge, edge)
    x_near, duals, own_sums, projector_near = pl.pallas_call(
        own_kernel,
        out_shape=(
            kept_near(images),
            kept_near((3, *images)),
            kept_near((len(own_pairs), row_count, col_count)),
            pltpu.VMEM(projector.shape, projector.dtype),
        ),
        in_specs=[SMEM] + [ANY] * 3,
        out_specs=(VMEM,) * 4,
        scratch_shapes=[pltpu.SemaphoreType.DMA(n) for n in ((2, 4), (8,))],
        compiler_params=SCRATCH,
        name="own",
    )(
        dual_step,
        left_far(extrapolated.reshape(images)),
        left_far(dual_grad.reshape(3, *images)),
        left_far(projector),
    )
    x_near, candidate, partial_gram = pl.pallas_call(
        gram_kernel,
        out_shape=(
            kept_near(images),
            kept_near((3, *images)),
            jax.ShapeDtypeStruct((row_count * held, LANES), f32),
        ),
        in_specs=[SMEM, SMEM, VMEM, VMEM, VMEM, VMEM],
        out_specs=(VMEM,) * 3,
        input_output_aliases={4: 0, 5: 1},
        compiler_params=SCRATCH,
        name="gram",
    )(
        dual_step,
        keep,
        near(following.reshape(images)),
        near(own_sums),
        near(x_near),
        near(duals),
    )
    share_order = [by_distance(SHARE, (2, 1, 1))]
    far_order = [by_distance((FAR,), (far_count // 2 + 1,))]
    gram_parts = lax.all_to_all(
        partial_gram.reshape(share_count, held, LANES),
        SHARE,
        0,
        0,
        axis_index_groups=share_order,
        tiled=True,
    )

    rounded = x_near.reshape(channels, pixels // edge, edge).astype(jnp.bfloat16)
    picked = picked_blocks(rounded, tile_cols, pixels // edge)
    products = jnp.einsum("tij,tbj->tbi", projector_near, picked, preferred_element_type=f32)
    projected = gathered_products(products, tile_rows, rays // edge)
    residual = projected - measured.reshape(sinogram)
    data_new = (dual_data.reshape(sinogram) + dual_rate * residual) / (1.0 + dual_rate)

    data_low = data_new.astype(jnp.bfloat16)
    picked_back = picked_blocks(data_low, tile_rows, rays // edge)
    products_back = jnp.einsum("tij,tbi->tbj", projector_near, picked_back, preferred_element_type=f32)
    back_proj = gathered_products(products_back, tile_cols, pixels // edge).reshape(
        volume_now.shape
    )
    to_far, back_proj = pl.pallas_call(
        pass_on_kernel,
        out_shape=(
            jax.ShapeDtypeStruct((far_count, held + 8, LANES), f32),
            kept_near(images),
        ),
        in_specs=[SMEM, VMEM, VMEM, VMEM],
        out_specs=(VMEM, VMEM),
        input_output_aliases={3: 1},
        compiler_params=SCRATCH,
        name="pass_on",
    )(reg_weight, near(gram_parts), near(residual), near(back_proj.reshape(images)))
    far_parts = lax.all_to_all(to_far, FAR, 0, 0, axis_index_groups=far_order, tiled=True)

    to_share = pl.pallas_call(
        functools.partial(factor_kernel, total_channels),
        out_shape=kept_near((share_count, held + 2 * tiles, LANES)),
        in_specs=[SMEM, VMEM],
        out_specs=VMEM,
        compiler_params=SCRATCH,
        name="factor",
    )(reg_weight, near(far_parts))
    factor_rows = lax.all_to_all(
        to_share, SHARE, 0, 0, axis_index_groups=share_order, tiled=True
    )
    factor_near = near(factor_rows.reshape(-1, LANES))

    new_slice, sums = pl.pallas_call(
        slice_kernel,
        out_shape=(kept_near(images), jax.ShapeDtypeStruct((slab_count, 2, LANES), f32)),
        in_specs=[VMEM, VMEM],
        out_specs=(VMEM, VMEM),
        compiler_params=SCRATCH,
        name="slice",
    )(factor_near, near(candidate))
    prior_layer = from_behind(new_slice, "slab", 1)
    all_sums = lax.all_to_all(sums, "slab", 0, 0, tiled=True)
    grad_new, ready, data_out = pl.pallas_call(
        rest_kernel,
        out_shape=(
            jax.ShapeDtypeStruct((3, *images), f32),
            kept_near(images),
            jax.ShapeDtypeStruct(sinogram, f32),
        ),
        in_specs=[SMEM, SMEM] + [VMEM] * 6,
        out_specs=(VMEM, VMEM, VMEM),
        compiler_params=SCRATCH,
        name="rest",
    )(
        primal_step,
        keep,
        factor_near,
        near(candidate),
        near(new_slice),
        near(volume_now.reshape(images)),
        near(back_proj),
        near(data_new),
    )
    counts = (total_channels * slab_count * slices * rays, slab_count * slices * pixels)
    updated = pl.pallas_call(
        finish_kernel,
        out_shape=image_form,
        in_specs=[SMEM, VMEM, VMEM],
        out_specs=VMEM,
        compiler_params=SCRATCH,
        name="finish",
    )(primal_step, near(ready), near(prior_layer))
    totals = pl.pallas_call(
        functools.partial(totals_kernel, counts),
        out_shape=jax.ShapeDtypeStruct((2,), f32),
        in_specs=[VMEM, ANY],
        out_specs=SMEM,
        compiler_params=SCRATCH,
        name="totals",
    )(near(all_sums), left_far(updated))
    return (
        updated.reshape(volume_now.shape),
        grad_new.reshape(dual_grad.shape),
        data_out.reshape(dual_data.shape),
        totals,
    )


def solution(mesh):
    torus = Mesh(
        mesh.devices.reshape(4, 2, 8, 2, mesh.shape["slab"]), ("x", "y", "zfar", "znear", "slab")
    )
    placed = (
        P(CHAN, "slab", None, None),
        P(CHAN, "slab", None, None),
        P(None, CHAN, "slab", None, None),
        P(CHAN, "slab", None),
        P(CHAN, "slab", None),
        P(),
        P(),
        P(),
        P(),
        P(),
        P(),
    )
    return jax.shard_map(
        on_device,
        mesh=torus,
        in_specs=placed,
        out_specs=(
            P(CHAN, "slab", None, None),
            P(None, CHAN, "slab", None, None),
            P(CHAN, "slab", None),
            P(),
        ),
        check_vma=False,
    )
```

```python
import functools
import itertools
import math

import jax
import jax.numpy as jnp
from jax import lax
from jax.experimental import pallas as pl
from jax.experimental.pallas import tpu as pltpu
from jax.sharding import Mesh
from jax.sharding import PartitionSpec as P

SWEEPS = 6
CHAN = ("x", "y", "zfar", "znear")
SHARE = ("x", "y", "znear")
FAR = "zfar"
LANES = 128

index_pairs = ((0, 0), (1, 1), (2, 2), (0, 1), (0, 2), (1, 2))
entry_of = {pair: k for k, pair in enumerate(index_pairs)}
sweep_order = ((0, 1), (0, 2), (1, 2))
own_pairs = ((0, 0), (1, 1), (0, 1))

VMEM = pl.BlockSpec(memory_space=pltpu.VMEM)
SMEM = pl.BlockSpec(memory_space=pltpu.SMEM)
ANY = pl.BlockSpec(memory_space=pl.ANY)
SCRATCH = pltpu.CompilerParams(vmem_limit_bytes=6 * 2**20)


def near(array):
    return pltpu.with_memory_space_constraint(array, pltpu.VMEM)


def left_far(array):
    return pltpu.with_memory_space_constraint(array, pltpu.HBM)


def kept_near(shape):
    return pltpu.VMEM(shape, jnp.float32)


def by_distance(axes, first):
    sizes = [lax.axis_size(axis) for axis in axes]
    places = list(itertools.product(*map(range, sizes)))

    def away(place):
        return sum(min((a - b) % n, (b - a) % n) for a, b, n in zip(place, first, sizes))

    order = sorted(range(len(places)), key=lambda i: -away(places[i]))
    order.remove(places.index(first))
    return [places.index(first), *order]


def from_behind(block, axis, distance):
    devices = range(lax.axis_size(axis))
    route = [(i - distance, i) for i in devices if i - distance in devices]
    return lax.ppermute(block, axis, route)


def own_kernel(
    rate_ref,
    x_far,
    dual_far,
    projector_far,
    x_ref,
    cand_ref,
    sums_ref,
    projector_ref,
    arrived,
    projector_arrived,
):
    channels, rows, cols = x_ref.shape
    tiles = cols // LANES
    parts = arrived.shape[1]
    size = channels // parts
    copies = []
    for part in range(parts):
        some = pl.ds(part * size, size)
        copies.append(
            (
                pltpu.make_async_copy(x_far.at[some], x_ref.at[some], arrived.at[0, part]),
                pltpu.make_async_copy(
                    dual_far.at[:, some], cand_ref.at[:, some], arrived.at[1, part]
                ),
            )
        )
        for copy in copies[-1]:
            copy.start()
    projector_copies = []
    pieces = projector_arrived.shape[0]
    size_in = projector_ref.shape[0] // pieces
    for piece in range(pieces):
        some = pl.ds(piece * size_in, size_in)
        projector_copies.append(
            pltpu.make_async_copy(
                projector_far.at[some], projector_ref.at[some], projector_arrived.at[piece]
            )
        )
    for copy in projector_copies:
        copy.start()
    rate = rate_ref[0]
    inner_row = lax.broadcasted_iota(jnp.int32, (rows, LANES), 0) < rows - 1
    edge_lane = lax.broadcasted_iota(jnp.int32, (rows, LANES), 1) == LANES - 1
    for part in range(parts):
        for copy in copies[part]:
            copy.wait()
        for j in range(tiles):
            here = pl.ds(j * LANES, LANES)
            if part:
                sums = [sums_ref[k, :, here] for k in range(len(own_pairs))]
            else:
                sums = [jnp.zeros((rows, LANES), jnp.float32) for _ in own_pairs]
            for c in range(part * size, part * size + size):
                x = x_ref[c, :, here]
                below = pltpu.roll(x, rows - 1, 0)
                right = pltpu.roll(x, LANES - 1, 1)
                if j + 1 < tiles:
                    after = pltpu.roll(x_ref[c, :, pl.ds((j + 1) * LANES, LANES)], LANES - 1, 1)
                else:
                    after = x
                steps = (
                    jnp.where(inner_row, below - x, 0.0),
                    jnp.where(edge_lane, after, right) - x,
                )
                cand = [cand_ref[a, c, :, here] + rate * steps[a] for a in range(2)]
                for a in range(2):
                    cand_ref[a, c, :, here] = cand[a]
                sums = [s + cand[a] * cand[b] for s, (a, b) in zip(sums, own_pairs)]
            for k, s in enumerate(sums):
                sums_ref[k, :, here] = s
    for copy in projector_copies:
        copy.wait()


def gram_kernel(
    rate_ref, keep_ref, next_ref, sums_ref, x_ref, dual_ref, x_same, cand_ref, out_far, out_ref, left
):
    channels, rows, cols = x_ref.shape
    tiles = cols // LANES
    per_row = len(index_pairs) * tiles
    rate = rate_ref[0]
    keep = keep_ref[0]
    parts = left.shape[0]
    size = rows // parts
    copies = []
    for part in range(parts):
        these = pl.ds(part * size, size)
        for j in range(tiles):
            here = pl.ds(j * LANES, LANES)
            sums = {pair: sums_ref[k, these, here] for k, pair in enumerate(own_pairs)}
            for b in range(3):
                sums[b, 2] = jnp.zeros((size, LANES), jnp.float32)
            for c in range(channels):
                step = (next_ref[c, these, here] - x_ref[c, these, here]) * keep
                cand = dual_ref[2, c, these, here] + rate * step
                for b in range(2):
                    sums[b, 2] = sums[b, 2] + dual_ref[b, c, these, here] * cand
                sums[2, 2] = sums[2, 2] + cand * cand
                cand_ref[2, c, these, here] = cand
            for k, pair in enumerate(index_pairs):
                start = part * size * per_row + k * tiles + j
                out_ref[pl.ds(start, size, stride=per_row), :] = sums[pair]
        done = pl.ds(part * size * per_row, size * per_row)
        copies.append(pltpu.make_async_copy(out_ref.at[done], out_far.at[done], left.at[part]))
        copies[-1].start()
    for copy in copies:
        copy.wait()


def pass_on_kernel(weight_ref, parts_ref, residual_ref, back_ref, out_ref, back_same):
    peers, per_row, _ = parts_ref.shape
    total = parts_ref[0]
    for p in range(1, peers):
        total = total + parts_ref[p]
    misfit = jnp.zeros((out_ref.shape[1] - per_row, LANES), jnp.float32)
    for c in range(residual_ref.shape[0]):
        for start in range(0, residual_ref.shape[1], misfit.shape[0]):
            some = residual_ref[c, pl.ds(start, misfit.shape[0]), :]
            misfit = misfit + some * some
    for p in range(out_ref.shape[0]):
        out_ref[p, :per_row, :] = total
        out_ref[p, per_row:, :] = misfit


def rotate(entry, vectors, p, q):
    k = 3 - p - q
    pq, kp, kq = (entry_of[tuple(sorted(s))] for s in ((p, q), (k, p), (k, q)))
    across, twice = entry[q] - entry[p], 2.0 * entry[pq]
    square = across * across + twice * twice
    still = square == 0.0
    inverse = lax.rsqrt(jnp.where(still, 1.0, square))
    length = square * inverse
    half = jnp.where(still, 1.0, 0.5 + 0.5 * jnp.abs(across) * inverse)
    root = lax.rsqrt(half)
    large, small = half * root, 0.5 * jnp.abs(twice) * inverse * root
    ahead = across >= 0.0
    cosine = jnp.where(ahead, large, small)
    sine = jnp.where(ahead, small, large)
    sine = jnp.where(twice < 0.0, -sine, sine)
    middle = entry[p] + entry[q]
    entry, vectors = list(entry), [list(row) for row in vectors]
    entry[p], entry[q] = 0.5 * (middle - length), 0.5 * (middle + length)
    entry[pq] = jnp.where(still, entry[pq], 0.0)
    entry[kp], entry[kq] = (
        cosine * entry[kp] - sine * entry[kq],
        sine * entry[kp] + cosine * entry[kq],
    )
    for row in vectors:
        row[p], row[q] = cosine * row[p] - sine * row[q], sine * row[p] + cosine * row[q]
    return entry, vectors


def factor_kernel(channels, weight_ref, parts_ref, out_ref):
    peers, held, _ = parts_ref.shape
    entries = len(index_pairs)
    tiles = out_ref.shape[1] // (entries + 2)

    def summed(start, size):
        total = parts_ref[0, pl.ds(start, size), :]
        for p in range(1, peers):
            total = total + parts_ref[p, pl.ds(start, size), :]
        return total

    radius = weight_ref[0] * math.sqrt(channels)
    entry = [summed(k * tiles, tiles) for k in range(entries)]
    one, zero = jnp.ones_like(entry[0]), jnp.zeros_like(entry[0])
    vectors = [[one if r == c else zero for c in range(3)] for r in range(3)]
    for _ in range(SWEEPS):
        for p, q in sweep_order:
            entry, vectors = rotate(entry, vectors, p, q)
    roots = [jnp.sqrt(jnp.maximum(entry[d], 0.0)) for d in range(3)]
    scales = [radius / jnp.maximum(root, radius) for root in roots]
    excess = sum(jnp.maximum(root - radius, 0.0) for root in roots) / radius
    misfit = sum(summed(k, tiles) for k in range(entries * tiles, held, tiles))
    rows = [
        sum(vectors[a][d] * scales[d] * vectors[b][d] for d in range(3)) for a, b in index_pairs
    ] + [misfit, excess]
    for p in range(out_ref.shape[0]):
        for k, row in enumerate(rows):
            out_ref[p, pl.ds(k * tiles, tiles), :] = row


def factor_image(factor_ref, rows, tiles):
    per_row = factor_ref.shape[0] // rows

    def image(k, j):
        return factor_ref[pl.ds(k * tiles + j, rows, stride=per_row), :]

    return image


def entry_at(a, b):
    return entry_of[tuple(sorted((a, b)))]


def slice_kernel(factor_ref, cand_ref, new_ref, sums_far, sums_ref, left):
    _, channels, rows, cols = cand_ref.shape
    tiles = cols // LANES
    image = factor_image(factor_ref, rows, tiles)
    per_row = factor_ref.shape[0] // rows
    slabs, count, _ = sums_ref.shape
    size = count * tiles
    total = sum(
        factor_ref[pl.ds(r * per_row + per_row - size, size), :] for r in range(rows)
    )
    for k in range(count):
        row = jnp.sum(total[k * tiles : (k + 1) * tiles], axis=0, keepdims=True)
        for p in range(slabs):
            sums_ref[p, pl.ds(k, 1), :] = row
    copy = pltpu.make_async_copy(sums_ref, sums_far, left)
    copy.start()
    for j in range(tiles):
        here = pl.ds(j * LANES, LANES)
        factor = [image(entry_at(b, 2), j) for b in range(3)]
        for c in range(channels):
            new_ref[c, :, here] = sum(cand_ref[b, c, :, here] * factor[b] for b in range(3))
    copy.wait()


def rest_kernel(
    rate_ref,
    keep_ref,
    factor_ref,
    cand_ref,
    slice_ref,
    volume_ref,
    back_ref,
    data_ref,
    new_ref,
    ready_ref,
    data_out,
):
    _, channels, rows, cols = cand_ref.shape
    tiles = cols // LANES
    rate = rate_ref[0]
    keep = keep_ref[0]
    image = factor_image(factor_ref, rows, tiles)
    data_out[...] = data_ref[...]
    row_id = lax.broadcasted_iota(jnp.int32, (rows, LANES), 0)
    lane_id = lax.broadcasted_iota(jnp.int32, (rows, LANES), 1)
    before = [None] * channels
    for j in range(tiles):
        here = pl.ds(j * LANES, LANES)
        factor = [[image(entry_at(b, a), j) for b in range(3)] for a in range(2)]
        for c in range(channels):
            cand = [cand_ref[b, c, :, here] for b in range(3)]
            new = [sum(cand[b] * factor[a][b] for b in range(3)) for a in range(2)]
            along = slice_ref[c, :, here]
            for a in range(2):
                new_ref[a, c, :, here] = new[a]
            new_ref[2, c, :, here] = along
            kept = jnp.where(row_id < rows - 1, new[0], 0.0)
            spread = kept - jnp.where(row_id > 0, pltpu.roll(new[0], 1, 0), 0.0)
            left = pltpu.roll(new[1], 1, 1)
            earlier = jnp.where(lane_id > 0, left, 0.0 if j == 0 else before[c])
            before[c] = left
            kept = new[1] if j + 1 < tiles else jnp.where(lane_id < LANES - 1, new[1], 0.0)
            spread = spread + (kept - earlier) + keep * along
            ready_ref[c, :, here] = volume_ref[c, :, here] - rate * (back_ref[c, :, here] - spread)


def finish_kernel(rate_ref, ready_ref, prior_ref, updated_ref):
    rate = rate_ref[0]
    for c in range(ready_ref.shape[0]):
        updated_ref[c] = jnp.maximum(ready_ref[c] - rate * prior_ref[c], 0.0)


def totals_kernel(counts, sums_ref, updated_far, totals_ref):
    total = sums_ref[0]
    for p in range(1, sums_ref.shape[0]):
        total = total + sums_ref[p]
    across = jnp.sum(total, axis=1, keepdims=True)
    for k, count in enumerate(counts):
        totals_ref[k] = across[k, 0] * (1.0 / count)


def picked_blocks(blocks, where, count):
    chosen = (where[:, None] == jnp.arange(count, dtype=jnp.int32)[None, :]).astype(jnp.bfloat16)
    return jnp.einsum("tc,bcj->tbj", chosen, blocks, preferred_element_type=jnp.float32).astype(
        jnp.bfloat16
    )


def gathered_products(products, where, count):
    chosen = (where[:, None] == jnp.arange(count, dtype=jnp.int32)[None, :]).astype(jnp.float32)
    return jnp.einsum("tc,tbj->bcj", chosen, products, precision=lax.Precision.HIGHEST)


def on_device(
    volume_now,
    extrapolated,
    dual_grad,
    dual_data,
    measured,
    projector,
    tile_rows,
    tile_cols,
    dual_step,
    primal_step,
    reg_weight,
):
    f32 = jnp.float32
    dual_rate = dual_step[0]
    channels, slices, row_count, col_count = volume_now.shape
    pixels = row_count * col_count
    rays = dual_data.shape[2]
    edge = projector.shape[1]
    share_count, far_count = lax.axis_size(SHARE), lax.axis_size(FAR)
    slab_count = lax.axis_size("slab")
    total_channels = channels * share_count * far_count
    tiles = col_count // LANES
    held = len(index_pairs) * tiles
    last_slice = lax.axis_index("slab") == slab_count - 1
    images = (channels, row_count, col_count)

    keep = jnp.where(last_slice, 0.0, 1.0).reshape(1)
    image_form = jax.ShapeDtypeStruct(images, f32)

    following = from_behind(extrapolated, "slab", -1)
    sinogram = (channels, rays // edge, edge)
    x_near, duals, own_sums, projector_near = pl.pallas_call(
        own_kernel,
        out_shape=(
            kept_near(images),
            kept_near((3, *images)),
            kept_near((len(own_pairs), row_count, col_count)),
            pltpu.VMEM(projector.shape, projector.dtype),
        ),
        in_specs=[SMEM] + [ANY] * 3,
        out_specs=(VMEM,) * 4,
        scratch_shapes=[pltpu.SemaphoreType.DMA(n) for n in ((2, 4), (8,))],
        compiler_params=SCRATCH,
        name="own",
    )(
        dual_step,
        left_far(extrapolated.reshape(images)),
        left_far(dual_grad.reshape(3, *images)),
        left_far(projector),
    )
    x_near, candidate, partial_gram = pl.pallas_call(
        gram_kernel,
        out_shape=(
            kept_near(images),
            kept_near((3, *images)),
            pltpu.HBM((row_count * held, LANES), f32),
        ),
        in_specs=[SMEM, SMEM, VMEM, VMEM, VMEM, VMEM],
        out_specs=(VMEM, VMEM, ANY),
        scratch_shapes=[
            pltpu.VMEM((row_count * held, LANES), f32),
            pltpu.SemaphoreType.DMA((2,)),
        ],
        input_output_aliases={4: 0, 5: 1},
        compiler_params=SCRATCH,
        name="gram",
    )(
        dual_step,
        keep,
        near(following.reshape(images)),
        near(own_sums),
        near(x_near),
        near(duals),
    )
    share_order = [by_distance(SHARE, (2, 1, 1))]
    far_order = [by_distance((FAR,), (far_count // 2 + 1,))]
    gram_parts = lax.all_to_all(
        partial_gram.reshape(share_count, held, LANES),
        SHARE,
        0,
        0,
        axis_index_groups=share_order,
        tiled=True,
    )

    rounded = x_near.reshape(channels, pixels // edge, edge).astype(jnp.bfloat16)
    picked = picked_blocks(rounded, tile_cols, pixels // edge)
    products = jnp.einsum("tij,tbj->tbi", projector_near, picked, preferred_element_type=f32)
    projected = gathered_products(products, tile_rows, rays // edge)
    residual = projected - measured.reshape(sinogram)
    data_new = (dual_data.reshape(sinogram) + dual_rate * residual) / (1.0 + dual_rate)

    data_low = data_new.astype(jnp.bfloat16)
    picked_back = picked_blocks(data_low, tile_rows, rays // edge)
    products_back = jnp.einsum("tij,tbi->tbj", projector_near, picked_back, preferred_element_type=f32)
    back_proj = gathered_products(products_back, tile_cols, pixels // edge).reshape(
        volume_now.shape
    )
    to_far, back_proj = pl.pallas_call(
        pass_on_kernel,
        out_shape=(
            jax.ShapeDtypeStruct((far_count, held + 8, LANES), f32),
            kept_near(images),
        ),
        in_specs=[SMEM, VMEM, VMEM, VMEM],
        out_specs=(VMEM, VMEM),
        input_output_aliases={3: 1},
        compiler_params=SCRATCH,
        name="pass_on",
    )(reg_weight, near(gram_parts), near(residual), near(back_proj.reshape(images)))
    far_parts = lax.all_to_all(to_far, FAR, 0, 0, axis_index_groups=far_order, tiled=True)

    to_share = pl.pallas_call(
        functools.partial(factor_kernel, total_channels),
        out_shape=kept_near((share_count, held + 2 * tiles, LANES)),
        in_specs=[SMEM, VMEM],
        out_specs=VMEM,
        compiler_params=SCRATCH,
        name="factor",
    )(reg_weight, near(far_parts))
    factor_rows = lax.all_to_all(
        to_share, SHARE, 0, 0, axis_index_groups=share_order, tiled=True
    )
    factor_near = near(factor_rows.reshape(-1, LANES))

    new_slice, sums = pl.pallas_call(
        slice_kernel,
        out_shape=(kept_near(images), pltpu.HBM((slab_count, 2, LANES), f32)),
        in_specs=[VMEM, VMEM],
        out_specs=(VMEM, ANY),
        scratch_shapes=[
            pltpu.VMEM((slab_count, 2, LANES), f32),
            pltpu.SemaphoreType.DMA(()),
        ],
        compiler_params=SCRATCH,
        name="slice",
    )(factor_near, near(candidate))
    prior_layer = from_behind(new_slice, "slab", 1)
    slab_order = [[0, *range(slab_count // 2, slab_count), *range(1, slab_count // 2)]]
    all_sums = lax.all_to_all(sums, "slab", 0, 0, axis_index_groups=slab_order, tiled=True)
    grad_new, ready, data_out = pl.pallas_call(
        rest_kernel,
        out_shape=(
            jax.ShapeDtypeStruct((3, *images), f32),
            kept_near(images),
            jax.ShapeDtypeStruct(sinogram, f32),
        ),
        in_specs=[SMEM, SMEM] + [VMEM] * 6,
        out_specs=(VMEM, VMEM, VMEM),
        compiler_params=SCRATCH,
        name="rest",
    )(
        primal_step,
        keep,
        factor_near,
        near(candidate),
        near(new_slice),
        near(volume_now.reshape(images)),
        near(back_proj),
        near(data_new),
    )
    counts = (total_channels * slab_count * slices * rays, slab_count * slices * pixels)
    updated = pl.pallas_call(
        finish_kernel,
        out_shape=image_form,
        in_specs=[SMEM, VMEM, VMEM],
        out_specs=VMEM,
        compiler_params=SCRATCH,
        name="finish",
    )(primal_step, near(ready), near(prior_layer))
    totals = pl.pallas_call(
        functools.partial(totals_kernel, counts),
        out_shape=jax.ShapeDtypeStruct((2,), f32),
        in_specs=[VMEM, ANY],
        out_specs=SMEM,
        compiler_params=SCRATCH,
        name="totals",
    )(near(all_sums), left_far(updated))
    return (
        updated.reshape(volume_now.shape),
        grad_new.reshape(dual_grad.shape),
        data_out.reshape(dual_data.shape),
        totals,
    )


def solution(mesh):
    torus = Mesh(
        mesh.devices.reshape(4, 2, 8, 2, mesh.shape["slab"]), ("x", "y", "zfar", "znear", "slab")
    )
    placed = (
        P(CHAN, "slab", None, None),
        P(CHAN, "slab", None, None),
        P(None, CHAN, "slab", None, None),
        P(CHAN, "slab", None),
        P(CHAN, "slab", None),
        P(),
        P(),
        P(),
        P(),
        P(),
        P(),
    )
    return jax.shard_map(
        on_device,
        mesh=torus,
        in_specs=placed,
        out_specs=(
            P(CHAN, "slab", None, None),
            P(None, CHAN, "slab", None, None),
            P(CHAN, "slab", None),
            P(),
        ),
        check_vma=False,
    )
```

```python
import functools
import itertools
import math

import jax
import jax.numpy as jnp
from jax import lax
from jax.experimental import pallas as pl
from jax.experimental.pallas import tpu as pltpu
from jax.sharding import Mesh
from jax.sharding import PartitionSpec as P

SWEEPS = 6
CHAN = ("x", "y", "zfar", "znear")
SHARE = ("x", "y", "znear")
FAR = "zfar"
LANES = 128

index_pairs = ((0, 0), (1, 1), (2, 2), (0, 1), (0, 2), (1, 2))
entry_of = {pair: k for k, pair in enumerate(index_pairs)}
sweep_order = ((0, 1), (0, 2), (1, 2))
own_pairs = ((0, 0), (1, 1), (0, 1))

VMEM = pl.BlockSpec(memory_space=pltpu.VMEM)
SMEM = pl.BlockSpec(memory_space=pltpu.SMEM)
ANY = pl.BlockSpec(memory_space=pl.ANY)
SCRATCH = pltpu.CompilerParams(vmem_limit_bytes=6 * 2**20)


def near(array):
    return pltpu.with_memory_space_constraint(array, pltpu.VMEM)


def left_far(array):
    return pltpu.with_memory_space_constraint(array, pltpu.HBM)


def kept_near(shape):
    return pltpu.VMEM(shape, jnp.float32)


def by_distance(axes, first):
    sizes = [lax.axis_size(axis) for axis in axes]
    places = list(itertools.product(*map(range, sizes)))

    def away(place):
        return sum(min((a - b) % n, (b - a) % n) for a, b, n in zip(place, first, sizes))

    order = sorted(range(len(places)), key=lambda i: -away(places[i]))
    order.remove(places.index(first))
    return [places.index(first), *order]


def from_behind(block, axis, distance):
    devices = range(lax.axis_size(axis))
    route = [(i - distance, i) for i in devices if i - distance in devices]
    return lax.ppermute(block, axis, route)


def own_kernel(
    rate_ref,
    x_far,
    dual_far,
    projector_far,
    x_ref,
    cand_ref,
    sums_ref,
    projector_ref,
    arrived,
    projector_arrived,
):
    channels, rows, cols = x_ref.shape
    tiles = cols // LANES
    parts = arrived.shape[1]
    size = channels // parts
    copies = []
    for part in range(parts):
        some = pl.ds(part * size, size)
        copies.append(
            (
                pltpu.make_async_copy(x_far.at[some], x_ref.at[some], arrived.at[0, part]),
                pltpu.make_async_copy(
                    dual_far.at[:, some], cand_ref.at[:, some], arrived.at[1, part]
                ),
            )
        )
        for copy in copies[-1]:
            copy.start()
    projector_copies = []
    pieces = projector_arrived.shape[0]
    size_in = projector_ref.shape[0] // pieces
    for piece in range(pieces):
        some = pl.ds(piece * size_in, size_in)
        projector_copies.append(
            pltpu.make_async_copy(
                projector_far.at[some], projector_ref.at[some], projector_arrived.at[piece]
            )
        )
    for copy in projector_copies:
        copy.start()
    rate = rate_ref[0]
    inner_row = lax.broadcasted_iota(jnp.int32, (rows, LANES), 0) < rows - 1
    edge_lane = lax.broadcasted_iota(jnp.int32, (rows, LANES), 1) == LANES - 1
    for part in range(parts):
        for copy in copies[part]:
            copy.wait()
        for j in range(tiles):
            here = pl.ds(j * LANES, LANES)
            if part:
                sums = [sums_ref[k, :, here] for k in range(len(own_pairs))]
            else:
                sums = [jnp.zeros((rows, LANES), jnp.float32) for _ in own_pairs]
            for c in range(part * size, part * size + size):
                x = x_ref[c, :, here]
                below = pltpu.roll(x, rows - 1, 0)
                right = pltpu.roll(x, LANES - 1, 1)
                if j + 1 < tiles:
                    after = pltpu.roll(x_ref[c, :, pl.ds((j + 1) * LANES, LANES)], LANES - 1, 1)
                else:
                    after = x
                steps = (
                    jnp.where(inner_row, below - x, 0.0),
                    jnp.where(edge_lane, after, right) - x,
                )
                cand = [cand_ref[a, c, :, here] + rate * steps[a] for a in range(2)]
                for a in range(2):
                    cand_ref[a, c, :, here] = cand[a]
                sums = [s + cand[a] * cand[b] for s, (a, b) in zip(sums, own_pairs)]
            for k, s in enumerate(sums):
                sums_ref[k, :, here] = s
    for copy in projector_copies:
        copy.wait()


def gram_kernel(
    rate_ref, keep_ref, next_ref, sums_ref, x_ref, dual_ref, x_same, cand_ref, out_far, out_ref, left
):
    channels, rows, cols = x_ref.shape
    tiles = cols // LANES
    per_row = len(index_pairs) * tiles
    rate = rate_ref[0]
    keep = keep_ref[0]
    parts = left.shape[0]
    size = rows // parts
    copies = []
    for part in range(parts):
        these = pl.ds(part * size, size)
        for j in range(tiles):
            here = pl.ds(j * LANES, LANES)
            sums = {pair: sums_ref[k, these, here] for k, pair in enumerate(own_pairs)}
            for b in range(3):
                sums[b, 2] = jnp.zeros((size, LANES), jnp.float32)
            for c in range(channels):
                step = (next_ref[c, these, here] - x_ref[c, these, here]) * keep
                cand = dual_ref[2, c, these, here] + rate * step
                for b in range(2):
                    sums[b, 2] = sums[b, 2] + dual_ref[b, c, these, here] * cand
                sums[2, 2] = sums[2, 2] + cand * cand
                cand_ref[2, c, these, here] = cand
            for k, pair in enumerate(index_pairs):
                start = part * size * per_row + k * tiles + j
                out_ref[pl.ds(start, size, stride=per_row), :] = sums[pair]
        done = pl.ds(part * size * per_row, size * per_row)
        copies.append(pltpu.make_async_copy(out_ref.at[done], out_far.at[done], left.at[part]))
        copies[-1].start()
    for copy in copies:
        copy.wait()


def pass_on_kernel(weight_ref, parts_ref, residual_ref, back_ref, out_ref, back_same):
    peers, per_row, _ = parts_ref.shape
    copies, pairs, two, _ = out_ref.shape
    total = parts_ref[0]
    for p in range(1, peers):
        total = total + parts_ref[p]
    squares = jnp.zeros((8, LANES), jnp.float32)
    for c in range(residual_ref.shape[0]):
        for start in range(0, residual_ref.shape[1], 8):
            some = residual_ref[c, pl.ds(start, 8), :]
            squares = squares + some * some
    misfit = sum(squares[k : k + two] for k in range(0, 8, two))
    for k in range(pairs):
        pair = total[two * k : two * k + two] if k < per_row // two else misfit
        for p in range(copies):
            out_ref[p, k] = pair


def rotate(entry, vectors, p, q):
    k = 3 - p - q
    pq, kp, kq = (entry_of[tuple(sorted(s))] for s in ((p, q), (k, p), (k, q)))
    across, twice = entry[q] - entry[p], 2.0 * entry[pq]
    square = across * across + twice * twice
    still = square == 0.0
    inverse = lax.rsqrt(jnp.where(still, 1.0, square))
    length = square * inverse
    half = jnp.where(still, 1.0, 0.5 + 0.5 * jnp.abs(across) * inverse)
    root = lax.rsqrt(half)
    large, small = half * root, 0.5 * jnp.abs(twice) * inverse * root
    ahead = across >= 0.0
    cosine = jnp.where(ahead, large, small)
    sine = jnp.where(ahead, small, large)
    sine = jnp.where(twice < 0.0, -sine, sine)
    middle = entry[p] + entry[q]
    entry, vectors = list(entry), [list(row) for row in vectors]
    entry[p], entry[q] = 0.5 * (middle - length), 0.5 * (middle + length)
    entry[pq] = jnp.where(still, entry[pq], 0.0)
    entry[kp], entry[kq] = (
        cosine * entry[kp] - sine * entry[kq],
        sine * entry[kp] + cosine * entry[kq],
    )
    for row in vectors:
        row[p], row[q] = cosine * row[p] - sine * row[q], sine * row[p] + cosine * row[q]
    return entry, vectors


def factor_kernel(channels, weight_ref, parts_ref, out_ref, sums_ref):
    peers, pairs, two, _ = parts_ref.shape
    entries = len(index_pairs)
    tiles = out_ref.shape[1] // (entries + 2)
    for k in range(pairs):
        pair = parts_ref[0, k]
        for p in range(1, peers):
            pair = pair + parts_ref[p, k]
        sums_ref[pl.ds(two * k, two), :] = pair
    radius = weight_ref[0] * math.sqrt(channels)
    entry = [sums_ref[pl.ds(k * tiles, tiles), :] for k in range(entries)]
    one, zero = jnp.ones_like(entry[0]), jnp.zeros_like(entry[0])
    vectors = [[one if r == c else zero for c in range(3)] for r in range(3)]
    for _ in range(SWEEPS):
        for p, q in sweep_order:
            entry, vectors = rotate(entry, vectors, p, q)
    roots = [jnp.sqrt(jnp.maximum(entry[d], 0.0)) for d in range(3)]
    scales = [radius / jnp.maximum(root, radius) for root in roots]
    excess = sum(jnp.maximum(root - radius, 0.0) for root in roots) / radius
    misfit = sums_ref[pl.ds(entries * tiles, two), :]
    rows = [
        sum(vectors[a][d] * scales[d] * vectors[b][d] for d in range(3)) for a, b in index_pairs
    ]
    for p in range(out_ref.shape[0]):
        for k, row in enumerate(rows):
            out_ref[p, pl.ds(k * tiles, tiles), :] = row
        out_ref[p, pl.ds(entries * tiles, two), :] = misfit
        for start in range(entries * tiles + two, (entries + 1) * tiles, two):
            out_ref[p, pl.ds(start, two), :] = jnp.zeros_like(misfit)
        out_ref[p, pl.ds((entries + 1) * tiles, tiles), :] = excess


def factor_image(factor_ref, rows, tiles):
    per_row = factor_ref.shape[0] // rows

    def image(k, j):
        return factor_ref[pl.ds(k * tiles + j, rows, stride=per_row), :]

    return image


def entry_at(a, b):
    return entry_of[tuple(sorted((a, b)))]


def slice_kernel(factor_ref, cand_ref, new_ref, sums_far, sums_ref, left):
    _, channels, rows, cols = cand_ref.shape
    tiles = cols // LANES
    image = factor_image(factor_ref, rows, tiles)
    per_row = factor_ref.shape[0] // rows
    slabs, count, _ = sums_ref.shape
    size = count * tiles
    total = sum(
        factor_ref[pl.ds(r * per_row + per_row - size, size), :] for r in range(rows)
    )
    for k in range(count):
        row = jnp.sum(total[k * tiles : (k + 1) * tiles], axis=0, keepdims=True)
        for p in range(slabs):
            sums_ref[p, pl.ds(k, 1), :] = row
    copy = pltpu.make_async_copy(sums_ref, sums_far, left)
    copy.start()
    for j in range(tiles):
        here = pl.ds(j * LANES, LANES)
        factor = [image(entry_at(b, 2), j) for b in range(3)]
        for c in range(channels):
            new_ref[c, :, here] = sum(cand_ref[b, c, :, here] * factor[b] for b in range(3))
    copy.wait()


def rest_kernel(
    rate_ref,
    keep_ref,
    factor_ref,
    cand_ref,
    slice_ref,
    volume_ref,
    back_ref,
    data_ref,
    new_ref,
    ready_ref,
    data_out,
):
    _, channels, rows, cols = cand_ref.shape
    tiles = cols // LANES
    rate = rate_ref[0]
    keep = keep_ref[0]
    image = factor_image(factor_ref, rows, tiles)
    data_out[...] = data_ref[...]
    row_id = lax.broadcasted_iota(jnp.int32, (rows, LANES), 0)
    lane_id = lax.broadcasted_iota(jnp.int32, (rows, LANES), 1)
    before = [None] * channels
    for j in range(tiles):
        here = pl.ds(j * LANES, LANES)
        factor = [[image(entry_at(b, a), j) for b in range(3)] for a in range(2)]
        for c in range(channels):
            cand = [cand_ref[b, c, :, here] for b in range(3)]
            new = [sum(cand[b] * factor[a][b] for b in range(3)) for a in range(2)]
            along = slice_ref[c, :, here]
            for a in range(2):
                new_ref[a, c, :, here] = new[a]
            new_ref[2, c, :, here] = along
            kept = jnp.where(row_id < rows - 1, new[0], 0.0)
            spread = kept - jnp.where(row_id > 0, pltpu.roll(new[0], 1, 0), 0.0)
            left = pltpu.roll(new[1], 1, 1)
            earlier = jnp.where(lane_id > 0, left, 0.0 if j == 0 else before[c])
            before[c] = left
            kept = new[1] if j + 1 < tiles else jnp.where(lane_id < LANES - 1, new[1], 0.0)
            spread = spread + (kept - earlier) + keep * along
            ready_ref[c, :, here] = volume_ref[c, :, here] - rate * (back_ref[c, :, here] - spread)


def finish_kernel(rate_ref, ready_ref, prior_ref, updated_ref):
    rate = rate_ref[0]
    for c in range(ready_ref.shape[0]):
        updated_ref[c] = jnp.maximum(ready_ref[c] - rate * prior_ref[c], 0.0)


def totals_kernel(counts, sums_ref, updated_far, totals_ref):
    total = sums_ref[0]
    for p in range(1, sums_ref.shape[0]):
        total = total + sums_ref[p]
    across = jnp.sum(total, axis=1, keepdims=True)
    for k, count in enumerate(counts):
        totals_ref[k] = across[k, 0] * (1.0 / count)


def picked_blocks(blocks, where, count):
    chosen = (where[:, None] == jnp.arange(count, dtype=jnp.int32)[None, :]).astype(jnp.bfloat16)
    return jnp.einsum("tc,bcj->tbj", chosen, blocks, preferred_element_type=jnp.float32).astype(
        jnp.bfloat16
    )


def gathered_products(products, where, count):
    chosen = (where[:, None] == jnp.arange(count, dtype=jnp.int32)[None, :]).astype(jnp.float32)
    return jnp.einsum("tc,tbj->bcj", chosen, products, precision=lax.Precision.HIGHEST)


def on_device(
    volume_now,
    extrapolated,
    dual_grad,
    dual_data,
    measured,
    projector,
    tile_rows,
    tile_cols,
    dual_step,
    primal_step,
    reg_weight,
):
    f32 = jnp.float32
    dual_rate = dual_step[0]
    channels, slices, row_count, col_count = volume_now.shape
    pixels = row_count * col_count
    rays = dual_data.shape[2]
    edge = projector.shape[1]
    share_count, far_count = lax.axis_size(SHARE), lax.axis_size(FAR)
    slab_count = lax.axis_size("slab")
    total_channels = channels * share_count * far_count
    tiles = col_count // LANES
    held = len(index_pairs) * tiles
    last_slice = lax.axis_index("slab") == slab_count - 1
    images = (channels, row_count, col_count)

    keep = jnp.where(last_slice, 0.0, 1.0).reshape(1)
    image_form = jax.ShapeDtypeStruct(images, f32)

    following = from_behind(extrapolated, "slab", -1)
    sinogram = (channels, rays // edge, edge)
    x_near, duals, own_sums, projector_near = pl.pallas_call(
        own_kernel,
        out_shape=(
            kept_near(images),
            kept_near((3, *images)),
            kept_near((len(own_pairs), row_count, col_count)),
            pltpu.VMEM(projector.shape, projector.dtype),
        ),
        in_specs=[SMEM] + [ANY] * 3,
        out_specs=(VMEM,) * 4,
        scratch_shapes=[pltpu.SemaphoreType.DMA(n) for n in ((2, 4), (8,))],
        compiler_params=SCRATCH,
        name="own",
    )(
        dual_step,
        left_far(extrapolated.reshape(images)),
        left_far(dual_grad.reshape(3, *images)),
        left_far(projector),
    )
    x_near, candidate, partial_gram = pl.pallas_call(
        gram_kernel,
        out_shape=(
            kept_near(images),
            kept_near((3, *images)),
            pltpu.HBM((row_count * held, LANES), f32),
        ),
        in_specs=[SMEM, SMEM, VMEM, VMEM, VMEM, VMEM],
        out_specs=(VMEM, VMEM, ANY),
        scratch_shapes=[
            pltpu.VMEM((row_count * held, LANES), f32),
            pltpu.SemaphoreType.DMA((2,)),
        ],
        input_output_aliases={4: 0, 5: 1},
        compiler_params=SCRATCH,
        name="gram",
    )(
        dual_step,
        keep,
        near(following.reshape(images)),
        near(own_sums),
        near(x_near),
        near(duals),
    )
    share_order = [by_distance(SHARE, (2, 1, 1))]
    far_order = [by_distance((FAR,), (far_count // 2 + 1,))]
    gram_parts = lax.all_to_all(
        partial_gram.reshape(share_count, held, LANES),
        SHARE,
        0,
        0,
        axis_index_groups=share_order,
        tiled=True,
    )

    rounded = x_near.reshape(channels, pixels // edge, edge).astype(jnp.bfloat16)
    picked = picked_blocks(rounded, tile_cols, pixels // edge)
    products = jnp.einsum("tij,tbj->tbi", projector_near, picked, preferred_element_type=f32)
    projected = gathered_products(products, tile_rows, rays // edge)
    residual = projected - measured.reshape(sinogram)
    data_new = (dual_data.reshape(sinogram) + dual_rate * residual) / (1.0 + dual_rate)

    data_low = data_new.astype(jnp.bfloat16)
    picked_back = picked_blocks(data_low, tile_rows, rays // edge)
    products_back = jnp.einsum("tij,tbi->tbj", projector_near, picked_back, preferred_element_type=f32)
    back_proj = gathered_products(products_back, tile_cols, pixels // edge).reshape(
        volume_now.shape
    )
    to_far, back_proj = pl.pallas_call(
        pass_on_kernel,
        out_shape=(
            jax.ShapeDtypeStruct((far_count, held // 2 + 1, 2, LANES), f32),
            kept_near(images),
        ),
        in_specs=[SMEM, VMEM, VMEM, VMEM],
        out_specs=(VMEM, VMEM),
        input_output_aliases={3: 1},
        compiler_params=SCRATCH,
        name="pass_on",
    )(reg_weight, near(gram_parts), near(residual), near(back_proj.reshape(images)))
    far_parts = lax.all_to_all(to_far, FAR, 0, 0, axis_index_groups=far_order, tiled=True)

    to_share = pl.pallas_call(
        functools.partial(factor_kernel, total_channels),
        out_shape=kept_near((share_count, held + 2 * tiles, LANES)),
        in_specs=[SMEM, VMEM],
        out_specs=VMEM,
        scratch_shapes=[pltpu.VMEM((held + 2, LANES), f32)],
        compiler_params=SCRATCH,
        name="factor",
    )(reg_weight, near(far_parts))
    factor_rows = lax.all_to_all(
        to_share, SHARE, 0, 0, axis_index_groups=share_order, tiled=True
    )
    factor_near = near(factor_rows.reshape(-1, LANES))

    new_slice, sums = pl.pallas_call(
        slice_kernel,
        out_shape=(kept_near(images), pltpu.HBM((slab_count, 2, LANES), f32)),
        in_specs=[VMEM, VMEM],
        out_specs=(VMEM, ANY),
        scratch_shapes=[
            pltpu.VMEM((slab_count, 2, LANES), f32),
            pltpu.SemaphoreType.DMA(()),
        ],
        compiler_params=SCRATCH,
        name="slice",
    )(factor_near, near(candidate))
    prior_layer = from_behind(new_slice, "slab", 1)
    slab_order = [[0, *range(slab_count // 2, slab_count), *range(1, slab_count // 2)]]
    all_sums = lax.all_to_all(sums, "slab", 0, 0, axis_index_groups=slab_order, tiled=True)
    grad_new, ready, data_out = pl.pallas_call(
        rest_kernel,
        out_shape=(
            jax.ShapeDtypeStruct((3, *images), f32),
            kept_near(images),
            jax.ShapeDtypeStruct(sinogram, f32),
        ),
        in_specs=[SMEM, SMEM] + [VMEM] * 6,
        out_specs=(VMEM, VMEM, VMEM),
        compiler_params=SCRATCH,
        name="rest",
    )(
        primal_step,
        keep,
        factor_near,
        near(candidate),
        near(new_slice),
        near(volume_now.reshape(images)),
        near(back_proj),
        near(data_new),
    )
    counts = (total_channels * slab_count * slices * rays, slab_count * slices * pixels)
    updated = pl.pallas_call(
        finish_kernel,
        out_shape=image_form,
        in_specs=[SMEM, VMEM, VMEM],
        out_specs=VMEM,
        compiler_params=SCRATCH,
        name="finish",
    )(primal_step, near(ready), near(prior_layer))
    totals = pl.pallas_call(
        functools.partial(totals_kernel, counts),
        out_shape=jax.ShapeDtypeStruct((2,), f32),
        in_specs=[VMEM, ANY],
        out_specs=SMEM,
        compiler_params=SCRATCH,
        name="totals",
    )(near(all_sums), left_far(updated))
    return (
        updated.reshape(volume_now.shape),
        grad_new.reshape(dual_grad.shape),
        data_out.reshape(dual_data.shape),
        totals,
    )


def solution(mesh):
    torus = Mesh(
        mesh.devices.reshape(4, 2, 8, 2, mesh.shape["slab"]), ("x", "y", "zfar", "znear", "slab")
    )
    placed = (
        P(CHAN, "slab", None, None),
        P(CHAN, "slab", None, None),
        P(None, CHAN, "slab", None, None),
        P(CHAN, "slab", None),
        P(CHAN, "slab", None),
        P(),
        P(),
        P(),
        P(),
        P(),
        P(),
    )
    return jax.shard_map(
        on_device,
        mesh=torus,
        in_specs=placed,
        out_specs=(
            P(CHAN, "slab", None, None),
            P(None, CHAN, "slab", None, None),
            P(CHAN, "slab", None),
            P(),
        ),
        check_vma=False,
    )
```

```python
import functools
import itertools
import math

import jax
import jax.numpy as jnp
from jax import lax
from jax.experimental import pallas as pl
from jax.experimental.pallas import tpu as pltpu
from jax.sharding import Mesh
from jax.sharding import PartitionSpec as P

SWEEPS = 6
CHAN = ("x", "y", "zfar", "znear")
SHARE = ("x", "y", "znear")
FAR = "zfar"
LANES = 128

index_pairs = ((0, 0), (1, 1), (2, 2), (0, 1), (0, 2), (1, 2))
entry_of = {pair: k for k, pair in enumerate(index_pairs)}
sweep_order = ((0, 1), (0, 2), (1, 2))
own_pairs = ((0, 0), (1, 1), (0, 1))

VMEM = pl.BlockSpec(memory_space=pltpu.VMEM)
SMEM = pl.BlockSpec(memory_space=pltpu.SMEM)
ANY = pl.BlockSpec(memory_space=pl.ANY)
SCRATCH = pltpu.CompilerParams(vmem_limit_bytes=6 * 2**20)


def near(array):
    return pltpu.with_memory_space_constraint(array, pltpu.VMEM)


def left_far(array):
    return pltpu.with_memory_space_constraint(array, pltpu.HBM)


def kept_near(shape):
    return pltpu.VMEM(shape, jnp.float32)


def by_distance(axes, first):
    sizes = [lax.axis_size(axis) for axis in axes]
    places = list(itertools.product(*map(range, sizes)))

    def away(place):
        return sum(min((a - b) % n, (b - a) % n) for a, b, n in zip(place, first, sizes))

    order = sorted(range(len(places)), key=lambda i: -away(places[i]))
    order.remove(places.index(first))
    return [places.index(first), *order]


def from_behind(block, axis, distance):
    devices = range(lax.axis_size(axis))
    route = [(i - distance, i) for i in devices if i - distance in devices]
    return lax.ppermute(block, axis, route)


def own_kernel(
    rate_ref,
    x_far,
    dual_far,
    projector_far,
    x_ref,
    cand_ref,
    sums_ref,
    projector_ref,
    arrived,
    projector_arrived,
):
    channels, rows, cols = x_ref.shape
    tiles = cols // LANES
    parts = arrived.shape[1]
    size = channels // parts
    copies = []
    for part in range(parts):
        some = pl.ds(part * size, size)
        copies.append(
            (
                pltpu.make_async_copy(x_far.at[some], x_ref.at[some], arrived.at[0, part]),
                pltpu.make_async_copy(
                    dual_far.at[:, some], cand_ref.at[:, some], arrived.at[1, part]
                ),
            )
        )
        for copy in copies[-1]:
            copy.start()
    projector_copies = []
    pieces = projector_arrived.shape[0]
    size_in = projector_ref.shape[0] // pieces
    for piece in range(pieces):
        some = pl.ds(piece * size_in, size_in)
        projector_copies.append(
            pltpu.make_async_copy(
                projector_far.at[some], projector_ref.at[some], projector_arrived.at[piece]
            )
        )
    for copy in projector_copies:
        copy.start()
    rate = rate_ref[0]
    inner_row = lax.broadcasted_iota(jnp.int32, (rows, LANES), 0) < rows - 1
    edge_lane = lax.broadcasted_iota(jnp.int32, (rows, LANES), 1) == LANES - 1
    for part in range(parts):
        for copy in copies[part]:
            copy.wait()
        for j in range(tiles):
            here = pl.ds(j * LANES, LANES)
            if part:
                sums = [sums_ref[k, :, here] for k in range(len(own_pairs))]
            else:
                sums = [jnp.zeros((rows, LANES), jnp.float32) for _ in own_pairs]
            for c in range(part * size, part * size + size):
                x = x_ref[c, :, here]
                below = pltpu.roll(x, rows - 1, 0)
                right = pltpu.roll(x, LANES - 1, 1)
                if j + 1 < tiles:
                    after = pltpu.roll(x_ref[c, :, pl.ds((j + 1) * LANES, LANES)], LANES - 1, 1)
                else:
                    after = x
                steps = (
                    jnp.where(inner_row, below - x, 0.0),
                    jnp.where(edge_lane, after, right) - x,
                )
                cand = [cand_ref[a, c, :, here] + rate * steps[a] for a in range(2)]
                for a in range(2):
                    cand_ref[a, c, :, here] = cand[a]
                sums = [s + cand[a] * cand[b] for s, (a, b) in zip(sums, own_pairs)]
            for k, s in enumerate(sums):
                sums_ref[k, :, here] = s
    for copy in projector_copies:
        copy.wait()


def gram_kernel(
    rate_ref, keep_ref, next_ref, sums_ref, x_ref, dual_ref, x_same, cand_ref, out_far, out_ref, left
):
    channels, rows, cols = x_ref.shape
    tiles = cols // LANES
    per_row = len(index_pairs) * tiles
    rate = rate_ref[0]
    keep = keep_ref[0]
    parts = left.shape[0]
    size = rows // parts
    copies = []
    for part in range(parts):
        these = pl.ds(part * size, size)
        for j in range(tiles):
            here = pl.ds(j * LANES, LANES)
            sums = {pair: sums_ref[k, these, here] for k, pair in enumerate(own_pairs)}
            for b in range(3):
                sums[b, 2] = jnp.zeros((size, LANES), jnp.float32)
            for c in range(channels):
                step = (next_ref[c, these, here] - x_ref[c, these, here]) * keep
                cand = dual_ref[2, c, these, here] + rate * step
                for b in range(2):
                    sums[b, 2] = sums[b, 2] + dual_ref[b, c, these, here] * cand
                sums[2, 2] = sums[2, 2] + cand * cand
                cand_ref[2, c, these, here] = cand
            for k, pair in enumerate(index_pairs):
                start = part * size * per_row + k * tiles + j
                out_ref[pl.ds(start, size, stride=per_row), :] = sums[pair]
        done = pl.ds(part * size * per_row, size * per_row)
        copies.append(pltpu.make_async_copy(out_ref.at[done], out_far.at[done], left.at[part]))
        copies[-1].start()
    for copy in copies:
        copy.wait()


def pass_on_kernel(weight_ref, parts_ref, residual_ref, back_ref, out_ref, back_same):
    peers, per_row, _ = parts_ref.shape
    copies, pairs, two, _ = out_ref.shape
    total = parts_ref[0]
    for p in range(1, peers):
        total = total + parts_ref[p]
    squares = jnp.zeros((8, LANES), jnp.float32)
    for c in range(residual_ref.shape[0]):
        for start in range(0, residual_ref.shape[1], 8):
            some = residual_ref[c, pl.ds(start, 8), :]
            squares = squares + some * some
    misfit = sum(squares[k : k + two] for k in range(0, 8, two))
    for k in range(pairs):
        pair = total[two * k : two * k + two] if k < per_row // two else misfit
        for p in range(copies):
            out_ref[p, k] = pair


def rotate(entry, vectors, p, q):
    k = 3 - p - q
    pq, kp, kq = (entry_of[tuple(sorted(s))] for s in ((p, q), (k, p), (k, q)))
    across, twice = entry[q] - entry[p], 2.0 * entry[pq]
    square = across * across + twice * twice
    still = square == 0.0
    inverse = lax.rsqrt(jnp.where(still, 1.0, square))
    length = square * inverse
    half = jnp.where(still, 1.0, 0.5 + 0.5 * jnp.abs(across) * inverse)
    root = lax.rsqrt(half)
    large, small = half * root, 0.5 * jnp.abs(twice) * inverse * root
    ahead = across >= 0.0
    cosine = jnp.where(ahead, large, small)
    sine = jnp.where(ahead, small, large)
    sine = jnp.where(twice < 0.0, -sine, sine)
    middle = entry[p] + entry[q]
    entry, vectors = list(entry), [list(row) for row in vectors]
    entry[p], entry[q] = 0.5 * (middle - length), 0.5 * (middle + length)
    entry[pq] = jnp.where(still, entry[pq], 0.0)
    entry[kp], entry[kq] = (
        cosine * entry[kp] - sine * entry[kq],
        sine * entry[kp] + cosine * entry[kq],
    )
    for row in vectors:
        row[p], row[q] = cosine * row[p] - sine * row[q], sine * row[p] + cosine * row[q]
    return entry, vectors


def factor_kernel(channels, weight_ref, parts_ref, out_ref, sums_ref):
    peers, pairs, two, _ = parts_ref.shape
    entries = len(index_pairs)
    tiles = two * (pairs - 1) // entries
    for k in range(pairs):
        pair = parts_ref[0, k]
        for p in range(1, peers):
            pair = pair + parts_ref[p, k]
        sums_ref[pl.ds(two * k, two), :] = pair
    radius = weight_ref[0] * math.sqrt(channels)
    entry = [sums_ref[pl.ds(k * tiles, tiles), :] for k in range(entries)]
    one, zero = jnp.ones_like(entry[0]), jnp.zeros_like(entry[0])
    vectors = [[one if r == c else zero for c in range(3)] for r in range(3)]
    for _ in range(SWEEPS):
        for p, q in sweep_order:
            entry, vectors = rotate(entry, vectors, p, q)
    roots = [jnp.sqrt(jnp.maximum(entry[d], 0.0)) for d in range(3)]
    scales = [radius / jnp.maximum(root, radius) for root in roots]
    excess = sum(jnp.maximum(root - radius, 0.0) for root in roots) / radius
    misfit = sums_ref[pl.ds(entries * tiles, two), :]
    rows = [
        sum(vectors[a][d] * scales[d] * vectors[b][d] for d in range(3)) for a, b in index_pairs
    ]
    last = jnp.concatenate([jnp.sum(part, axis=0, keepdims=True) for part in (misfit, excess)])
    for k in range(pairs):
        row, start = rows[two * k // tiles] if k + 1 < pairs else last, two * k % tiles
        for p in range(out_ref.shape[0]):
            out_ref[p, k] = row[start : start + two]


def factor_image(factor_ref, rows, tiles):
    per_row = factor_ref.shape[0] // rows

    def image(k, j):
        return factor_ref[pl.ds(k * tiles + j, rows, stride=per_row), :]

    return image


def entry_at(a, b):
    return entry_of[tuple(sorted((a, b)))]


def slice_kernel(parts_ref, cand_ref, new_ref, factor_ref, sums_far, sums_ref, left):
    _, channels, rows, cols = cand_ref.shape
    tiles = cols // LANES
    peers, pairs, two, _ = parts_ref.shape
    total = parts_ref[0, pairs - 1]
    for p in range(1, peers):
        total = total + parts_ref[p, pairs - 1]
    for slab in range(sums_ref.shape[0]):
        sums_ref[slab] = total
    copy = pltpu.make_async_copy(sums_ref, sums_far, left)
    copy.start()
    per_row = factor_ref.shape[0] // rows
    for p in range(peers):
        for k in range(pairs - 1):
            factor_ref[pl.ds(p * per_row + two * k, two), :] = parts_ref[p, k]
    image = factor_image(factor_ref, rows, tiles)
    for j in range(tiles):
        here = pl.ds(j * LANES, LANES)
        factor = [image(entry_at(b, 2), j) for b in range(3)]
        for c in range(channels):
            new_ref[c, :, here] = sum(cand_ref[b, c, :, here] * factor[b] for b in range(3))
    copy.wait()


def rest_kernel(
    rate_ref,
    keep_ref,
    factor_ref,
    cand_ref,
    slice_ref,
    volume_ref,
    back_ref,
    data_ref,
    new_ref,
    ready_ref,
    data_out,
):
    _, channels, rows, cols = cand_ref.shape
    tiles = cols // LANES
    rate = rate_ref[0]
    keep = keep_ref[0]
    image = factor_image(factor_ref, rows, tiles)
    data_out[...] = data_ref[...]
    row_id = lax.broadcasted_iota(jnp.int32, (rows, LANES), 0)
    lane_id = lax.broadcasted_iota(jnp.int32, (rows, LANES), 1)
    before = [None] * channels
    for j in range(tiles):
        here = pl.ds(j * LANES, LANES)
        factor = [[image(entry_at(b, a), j) for b in range(3)] for a in range(2)]
        for c in range(channels):
            cand = [cand_ref[b, c, :, here] for b in range(3)]
            new = [sum(cand[b] * factor[a][b] for b in range(3)) for a in range(2)]
            along = slice_ref[c, :, here]
            for a in range(2):
                new_ref[a, c, :, here] = new[a]
            new_ref[2, c, :, here] = along
            kept = jnp.where(row_id < rows - 1, new[0], 0.0)
            spread = kept - jnp.where(row_id > 0, pltpu.roll(new[0], 1, 0), 0.0)
            left = pltpu.roll(new[1], 1, 1)
            earlier = jnp.where(lane_id > 0, left, 0.0 if j == 0 else before[c])
            before[c] = left
            kept = new[1] if j + 1 < tiles else jnp.where(lane_id < LANES - 1, new[1], 0.0)
            spread = spread + (kept - earlier) + keep * along
            ready_ref[c, :, here] = volume_ref[c, :, here] - rate * (back_ref[c, :, here] - spread)


def finish_kernel(rate_ref, ready_ref, prior_ref, updated_ref):
    rate = rate_ref[0]
    for c in range(ready_ref.shape[0]):
        updated_ref[c] = jnp.maximum(ready_ref[c] - rate * prior_ref[c], 0.0)


def totals_kernel(counts, sums_ref, updated_far, totals_ref):
    total = sums_ref[0]
    for p in range(1, sums_ref.shape[0]):
        total = total + sums_ref[p]
    across = jnp.sum(total, axis=1, keepdims=True)
    for k, count in enumerate(counts):
        totals_ref[k] = across[k, 0] * (1.0 / count)


def picked_blocks(blocks, where, count):
    chosen = (where[:, None] == jnp.arange(count, dtype=jnp.int32)[None, :]).astype(jnp.bfloat16)
    return jnp.einsum("tc,bcj->tbj", chosen, blocks, preferred_element_type=jnp.float32).astype(
        jnp.bfloat16
    )


def gathered_products(products, where, count):
    chosen = (where[:, None] == jnp.arange(count, dtype=jnp.int32)[None, :]).astype(jnp.float32)
    return jnp.einsum("tc,tbj->bcj", chosen, products, precision=lax.Precision.HIGHEST)


def on_device(
    volume_now,
    extrapolated,
    dual_grad,
    dual_data,
    measured,
    projector,
    tile_rows,
    tile_cols,
    dual_step,
    primal_step,
    reg_weight,
):
    f32 = jnp.float32
    dual_rate = dual_step[0]
    channels, slices, row_count, col_count = volume_now.shape
    pixels = row_count * col_count
    rays = dual_data.shape[2]
    edge = projector.shape[1]
    share_count, far_count = lax.axis_size(SHARE), lax.axis_size(FAR)
    slab_count = lax.axis_size("slab")
    total_channels = channels * share_count * far_count
    tiles = col_count // LANES
    held = len(index_pairs) * tiles
    last_slice = lax.axis_index("slab") == slab_count - 1
    images = (channels, row_count, col_count)

    keep = jnp.where(last_slice, 0.0, 1.0).reshape(1)
    image_form = jax.ShapeDtypeStruct(images, f32)

    following = from_behind(extrapolated, "slab", -1)
    sinogram = (channels, rays // edge, edge)
    x_near, duals, own_sums, projector_near = pl.pallas_call(
        own_kernel,
        out_shape=(
            kept_near(images),
            kept_near((3, *images)),
            kept_near((len(own_pairs), row_count, col_count)),
            pltpu.VMEM(projector.shape, projector.dtype),
        ),
        in_specs=[SMEM] + [ANY] * 3,
        out_specs=(VMEM,) * 4,
        scratch_shapes=[pltpu.SemaphoreType.DMA(n) for n in ((2, 4), (8,))],
        compiler_params=SCRATCH,
        name="own",
    )(
        dual_step,
        left_far(extrapolated.reshape(images)),
        left_far(dual_grad.reshape(3, *images)),
        left_far(projector),
    )
    x_near, candidate, partial_gram = pl.pallas_call(
        gram_kernel,
        out_shape=(
            kept_near(images),
            kept_near((3, *images)),
            pltpu.HBM((row_count * held, LANES), f32),
        ),
        in_specs=[SMEM, SMEM, VMEM, VMEM, VMEM, VMEM],
        out_specs=(VMEM, VMEM, ANY),
        scratch_shapes=[
            pltpu.VMEM((row_count * held, LANES), f32),
            pltpu.SemaphoreType.DMA((2,)),
        ],
        input_output_aliases={4: 0, 5: 1},
        compiler_params=SCRATCH,
        name="gram",
    )(
        dual_step,
        keep,
        near(following.reshape(images)),
        near(own_sums),
        near(x_near),
        near(duals),
    )
    share_order = [by_distance(SHARE, (2, 1, 1))]
    far_order = [by_distance((FAR,), (far_count // 2 + 1,))]
    gram_parts = lax.all_to_all(
        partial_gram.reshape(share_count, held, LANES),
        SHARE,
        0,
        0,
        axis_index_groups=share_order,
        tiled=True,
    )

    rounded = x_near.reshape(channels, pixels // edge, edge).astype(jnp.bfloat16)
    picked = picked_blocks(rounded, tile_cols, pixels // edge)
    products = jnp.einsum("tij,tbj->tbi", projector_near, picked, preferred_element_type=f32)
    projected = gathered_products(products, tile_rows, rays // edge)
    residual = projected - measured.reshape(sinogram)
    data_new = (dual_data.reshape(sinogram) + dual_rate * residual) / (1.0 + dual_rate)

    data_low = data_new.astype(jnp.bfloat16)
    picked_back = picked_blocks(data_low, tile_rows, rays // edge)
    products_back = jnp.einsum("tij,tbi->tbj", projector_near, picked_back, preferred_element_type=f32)
    back_proj = gathered_products(products_back, tile_cols, pixels // edge).reshape(
        volume_now.shape
    )
    to_far, back_proj = pl.pallas_call(
        pass_on_kernel,
        out_shape=(
            jax.ShapeDtypeStruct((far_count, held // 2 + 1, 2, LANES), f32),
            kept_near(images),
        ),
        in_specs=[SMEM, VMEM, VMEM, VMEM],
        out_specs=(VMEM, VMEM),
        input_output_aliases={3: 1},
        compiler_params=SCRATCH,
        name="pass_on",
    )(reg_weight, near(gram_parts), near(residual), near(back_proj.reshape(images)))
    far_parts = lax.all_to_all(to_far, FAR, 0, 0, axis_index_groups=far_order, tiled=True)

    to_share = pl.pallas_call(
        functools.partial(factor_kernel, total_channels),
        out_shape=kept_near((share_count, held // 2 + 1, 2, LANES)),
        in_specs=[SMEM, VMEM],
        out_specs=VMEM,
        scratch_shapes=[pltpu.VMEM((held + 2, LANES), f32)],
        compiler_params=SCRATCH,
        name="factor",
    )(reg_weight, near(far_parts))
    factor_rows = lax.all_to_all(
        to_share, SHARE, 0, 0, axis_index_groups=share_order, tiled=True
    )

    new_slice, factor_image_rows, sums = pl.pallas_call(
        slice_kernel,
        out_shape=(
            kept_near(images),
            kept_near((row_count * held, LANES)),
            pltpu.HBM((slab_count, 2, LANES), f32),
        ),
        in_specs=[VMEM, VMEM],
        out_specs=(VMEM, VMEM, ANY),
        scratch_shapes=[
            pltpu.VMEM((slab_count, 2, LANES), f32),
            pltpu.SemaphoreType.DMA(()),
        ],
        compiler_params=SCRATCH,
        name="slice",
    )(near(factor_rows), near(candidate))
    prior_layer = from_behind(new_slice, "slab", 1)
    slab_order = [[0, *range(slab_count // 2, slab_count), *range(1, slab_count // 2)]]
    all_sums = lax.all_to_all(sums, "slab", 0, 0, axis_index_groups=slab_order, tiled=True)
    grad_new, ready, data_out = pl.pallas_call(
        rest_kernel,
        out_shape=(
            jax.ShapeDtypeStruct((3, *images), f32),
            kept_near(images),
            jax.ShapeDtypeStruct(sinogram, f32),
        ),
        in_specs=[SMEM, SMEM] + [VMEM] * 6,
        out_specs=(VMEM, VMEM, VMEM),
        compiler_params=SCRATCH,
        name="rest",
    )(
        primal_step,
        keep,
        near(factor_image_rows),
        near(candidate),
        near(new_slice),
        near(volume_now.reshape(images)),
        near(back_proj),
        near(data_new),
    )
    counts = (total_channels * slab_count * slices * rays, slab_count * slices * pixels)
    updated = pl.pallas_call(
        finish_kernel,
        out_shape=image_form,
        in_specs=[SMEM, VMEM, VMEM],
        out_specs=VMEM,
        compiler_params=SCRATCH,
        name="finish",
    )(primal_step, near(ready), near(prior_layer))
    totals = pl.pallas_call(
        functools.partial(totals_kernel, counts),
        out_shape=jax.ShapeDtypeStruct((2,), f32),
        in_specs=[VMEM, ANY],
        out_specs=SMEM,
        compiler_params=SCRATCH,
        name="totals",
    )(near(all_sums), left_far(updated))
    return (
        updated.reshape(volume_now.shape),
        grad_new.reshape(dual_grad.shape),
        data_out.reshape(dual_data.shape),
        totals,
    )


def solution(mesh):
    torus = Mesh(
        mesh.devices.reshape(4, 2, 8, 2, mesh.shape["slab"]), ("x", "y", "zfar", "znear", "slab")
    )
    placed = (
        P(CHAN, "slab", None, None),
        P(CHAN, "slab", None, None),
        P(None, CHAN, "slab", None, None),
        P(CHAN, "slab", None),
        P(CHAN, "slab", None),
        P(),
        P(),
        P(),
        P(),
        P(),
        P(),
    )
    return jax.shard_map(
        on_device,
        mesh=torus,
        in_specs=placed,
        out_specs=(
            P(CHAN, "slab", None, None),
            P(None, CHAN, "slab", None, None),
            P(CHAN, "slab", None),
            P(),
        ),
        check_vma=False,
    )
```

```python
import functools
import itertools
import math

import jax
import jax.numpy as jnp
from jax import lax
from jax.experimental import pallas as pl
from jax.experimental.pallas import tpu as pltpu
from jax.sharding import Mesh
from jax.sharding import PartitionSpec as P

SWEEPS = 6
CHAN = ("x", "y", "zfar", "znear")
SHARE = ("x", "y", "znear")
FAR = "zfar"
LANES = 128

index_pairs = ((0, 0), (1, 1), (2, 2), (0, 1), (0, 2), (1, 2))
entry_of = {pair: k for k, pair in enumerate(index_pairs)}
sweep_order = ((0, 1), (0, 2), (1, 2))
own_pairs = ((0, 0), (1, 1), (0, 1))

VMEM = pl.BlockSpec(memory_space=pltpu.VMEM)
SMEM = pl.BlockSpec(memory_space=pltpu.SMEM)
ANY = pl.BlockSpec(memory_space=pl.ANY)
SCRATCH = pltpu.CompilerParams(vmem_limit_bytes=6 * 2**20)


def near(array):
    return pltpu.with_memory_space_constraint(array, pltpu.VMEM)


def left_far(array):
    return pltpu.with_memory_space_constraint(array, pltpu.HBM)


def kept_near(shape):
    return pltpu.VMEM(shape, jnp.float32)


def by_distance(axes, first):
    sizes = [lax.axis_size(axis) for axis in axes]
    places = list(itertools.product(*map(range, sizes)))

    def away(place):
        return sum(min((a - b) % n, (b - a) % n) for a, b, n in zip(place, first, sizes))

    order = sorted(range(len(places)), key=lambda i: -away(places[i]))
    order.remove(places.index(first))
    return [places.index(first), *order]


def from_behind(block, axis, distance):
    devices = range(lax.axis_size(axis))
    route = [(i - distance, i) for i in devices if i - distance in devices]
    return lax.ppermute(block, axis, route)


def own_kernel(
    rate_ref,
    x_far,
    dual_far,
    projector_far,
    x_ref,
    cand_ref,
    sums_ref,
    projector_ref,
    arrived,
    projector_arrived,
):
    channels, rows, cols = x_ref.shape
    tiles = cols // LANES
    parts = arrived.shape[1]
    size = channels // parts
    copies = []
    for part in range(parts):
        some = pl.ds(part * size, size)
        copies.append(
            (
                pltpu.make_async_copy(x_far.at[some], x_ref.at[some], arrived.at[0, part]),
                pltpu.make_async_copy(
                    dual_far.at[:, some], cand_ref.at[:, some], arrived.at[1, part]
                ),
            )
        )
        for copy in copies[-1]:
            copy.start()
    projector_copies = []
    pieces = projector_arrived.shape[0]
    size_in = projector_ref.shape[0] // pieces
    for piece in range(pieces):
        some = pl.ds(piece * size_in, size_in)
        projector_copies.append(
            pltpu.make_async_copy(
                projector_far.at[some], projector_ref.at[some], projector_arrived.at[piece]
            )
        )
    for copy in projector_copies:
        copy.start()
    rate = rate_ref[0]
    inner_row = lax.broadcasted_iota(jnp.int32, (rows, LANES), 0) < rows - 1
    edge_lane = lax.broadcasted_iota(jnp.int32, (rows, LANES), 1) == LANES - 1
    for part in range(parts):
        for copy in copies[part]:
            copy.wait()
        for j in range(tiles):
            here = pl.ds(j * LANES, LANES)
            if part:
                sums = [sums_ref[k, :, here] for k in range(len(own_pairs))]
            else:
                sums = [jnp.zeros((rows, LANES), jnp.float32) for _ in own_pairs]
            for c in range(part * size, part * size + size):
                x = x_ref[c, :, here]
                below = pltpu.roll(x, rows - 1, 0)
                right = pltpu.roll(x, LANES - 1, 1)
                if j + 1 < tiles:
                    after = pltpu.roll(x_ref[c, :, pl.ds((j + 1) * LANES, LANES)], LANES - 1, 1)
                else:
                    after = x
                steps = (
                    jnp.where(inner_row, below - x, 0.0),
                    jnp.where(edge_lane, after, right) - x,
                )
                cand = [cand_ref[a, c, :, here] + rate * steps[a] for a in range(2)]
                for a in range(2):
                    cand_ref[a, c, :, here] = cand[a]
                sums = [s + cand[a] * cand[b] for s, (a, b) in zip(sums, own_pairs)]
            for k, s in enumerate(sums):
                sums_ref[k, :, here] = s
    for copy in projector_copies:
        copy.wait()


def gram_kernel(
    rate_ref, keep_ref, next_ref, sums_ref, x_ref, dual_ref, x_same, cand_ref, out_far, out_ref, left
):
    channels, rows, cols = x_ref.shape
    tiles = cols // LANES
    per_row = len(index_pairs) * tiles
    rate = rate_ref[0]
    keep = keep_ref[0]
    parts = left.shape[0]
    size = rows // parts
    copies = []
    for part in range(parts):
        these = pl.ds(part * size, size)
        for j in range(tiles):
            here = pl.ds(j * LANES, LANES)
            sums = {pair: sums_ref[k, these, here] for k, pair in enumerate(own_pairs)}
            for b in range(3):
                sums[b, 2] = jnp.zeros((size, LANES), jnp.float32)
            for c in range(channels):
                step = (next_ref[c, these, here] - x_ref[c, these, here]) * keep
                cand = dual_ref[2, c, these, here] + rate * step
                for b in range(2):
                    sums[b, 2] = sums[b, 2] + dual_ref[b, c, these, here] * cand
                sums[2, 2] = sums[2, 2] + cand * cand
                cand_ref[2, c, these, here] = cand
            for k, pair in enumerate(index_pairs):
                start = part * size * per_row + k * tiles + j
                out_ref[pl.ds(start, size, stride=per_row), :] = sums[pair]
        done = pl.ds(part * size * per_row, size * per_row)
        copies.append(pltpu.make_async_copy(out_ref.at[done], out_far.at[done], left.at[part]))
        copies[-1].start()
    for copy in copies:
        copy.wait()


def pass_on_kernel(weight_ref, parts_ref, residual_ref, back_ref, out_ref, back_same):
    peers, per_row, _ = parts_ref.shape
    copies, pairs, two, _ = out_ref.shape
    total = parts_ref[0]
    for p in range(1, peers):
        total = total + parts_ref[p]
    squares = jnp.zeros((8, LANES), jnp.float32)
    for c in range(residual_ref.shape[0]):
        for start in range(0, residual_ref.shape[1], 8):
            some = residual_ref[c, pl.ds(start, 8), :]
            squares = squares + some * some
    misfit = sum(squares[k : k + two] for k in range(0, 8, two))
    for k in range(pairs):
        pair = total[two * k : two * k + two] if k < per_row // two else misfit
        for p in range(copies):
            out_ref[p, k] = pair


def rotate(entry, vectors, p, q):
    k = 3 - p - q
    pq, kp, kq = (entry_of[tuple(sorted(s))] for s in ((p, q), (k, p), (k, q)))
    across, twice = entry[q] - entry[p], 2.0 * entry[pq]
    square = across * across + twice * twice
    still = square == 0.0
    inverse = lax.rsqrt(jnp.where(still, 1.0, square))
    length = square * inverse
    half = jnp.where(still, 1.0, 0.5 + 0.5 * jnp.abs(across) * inverse)
    root = lax.rsqrt(half)
    large, small = half * root, 0.5 * jnp.abs(twice) * inverse * root
    ahead = across >= 0.0
    cosine = jnp.where(ahead, large, small)
    sine = jnp.where(ahead, small, large)
    sine = jnp.where(twice < 0.0, -sine, sine)
    middle = entry[p] + entry[q]
    entry, vectors = list(entry), [list(row) for row in vectors]
    entry[p], entry[q] = 0.5 * (middle - length), 0.5 * (middle + length)
    entry[pq] = jnp.where(still, entry[pq], 0.0)
    entry[kp], entry[kq] = (
        cosine * entry[kp] - sine * entry[kq],
        sine * entry[kp] + cosine * entry[kq],
    )
    for row in vectors:
        row[p], row[q] = cosine * row[p] - sine * row[q], sine * row[p] + cosine * row[q]
    return entry, vectors


def factor_kernel(channels, weight_ref, parts_ref, out_ref, sums_ref):
    peers, pairs, two, _ = parts_ref.shape
    entries = len(index_pairs)
    tiles = two * (pairs - 1) // entries
    for k in range(pairs):
        pair = parts_ref[0, k]
        for p in range(1, peers):
            pair = pair + parts_ref[p, k]
        sums_ref[pl.ds(two * k, two), :] = pair
    radius = weight_ref[0] * math.sqrt(channels)
    entry = [sums_ref[pl.ds(k * tiles, tiles), :] for k in range(entries)]
    one, zero = jnp.ones_like(entry[0]), jnp.zeros_like(entry[0])
    vectors = [[one if r == c else zero for c in range(3)] for r in range(3)]
    for _ in range(SWEEPS):
        for p, q in sweep_order:
            entry, vectors = rotate(entry, vectors, p, q)
    roots = [jnp.sqrt(jnp.maximum(entry[d], 0.0)) for d in range(3)]
    scales = [radius / jnp.maximum(root, radius) for root in roots]
    excess = sum(jnp.maximum(root - radius, 0.0) for root in roots) / radius
    misfit = sums_ref[pl.ds(entries * tiles, two), :]
    rows = [
        sum(vectors[a][d] * scales[d] * vectors[b][d] for d in range(3)) for a, b in index_pairs
    ]
    last = jnp.concatenate([jnp.sum(part, axis=0, keepdims=True) for part in (misfit, excess)])
    for k in range(pairs):
        row, start = rows[two * k // tiles] if k + 1 < pairs else last, two * k % tiles
        for p in range(out_ref.shape[0]):
            out_ref[p, k] = row[start : start + two]


def factor_image(factor_ref, rows, tiles):
    per_row = factor_ref.shape[0] // rows

    def image(k, j):
        return factor_ref[pl.ds(k * tiles + j, rows, stride=per_row), :]

    return image


def entry_at(a, b):
    return entry_of[tuple(sorted((a, b)))]


def slice_kernel(parts_ref, cand_ref, new_ref, factor_ref, sums_far, sums_ref, left):
    _, channels, rows, cols = cand_ref.shape
    tiles = cols // LANES
    peers, pairs, two, _ = parts_ref.shape
    total = parts_ref[0, pairs - 1]
    for p in range(1, peers):
        total = total + parts_ref[p, pairs - 1]
    for slab in range(sums_ref.shape[0]):
        sums_ref[slab] = total
    copy = pltpu.make_async_copy(sums_ref, sums_far, left)
    copy.start()
    per_row = factor_ref.shape[0] // rows
    for p in range(peers):
        for k in range(pairs - 1):
            factor_ref[pl.ds(p * per_row + two * k, two), :] = parts_ref[p, k]
    image = factor_image(factor_ref, rows, tiles)
    for j in range(tiles):
        here = pl.ds(j * LANES, LANES)
        factor = [image(entry_at(b, 2), j) for b in range(3)]
        for c in range(channels):
            new_ref[c, :, here] = sum(cand_ref[b, c, :, here] * factor[b] for b in range(3))
    copy.wait()


def rest_kernel(
    rate_ref,
    keep_ref,
    factor_ref,
    cand_ref,
    slice_ref,
    volume_ref,
    back_ref,
    data_ref,
    new_ref,
    ready_ref,
    data_out,
):
    _, channels, rows, cols = cand_ref.shape
    tiles = cols // LANES
    rate = rate_ref[0]
    keep = keep_ref[0]
    image = factor_image(factor_ref, rows, tiles)
    data_out[...] = data_ref[...]
    row_id = lax.broadcasted_iota(jnp.int32, (rows, LANES), 0)
    lane_id = lax.broadcasted_iota(jnp.int32, (rows, LANES), 1)
    before = [None] * channels
    for j in range(tiles):
        here = pl.ds(j * LANES, LANES)
        factor = [[image(entry_at(b, a), j) for b in range(3)] for a in range(2)]
        for c in range(channels):
            cand = [cand_ref[b, c, :, here] for b in range(3)]
            new = [sum(cand[b] * factor[a][b] for b in range(3)) for a in range(2)]
            along = slice_ref[c, :, here]
            for a in range(2):
                new_ref[a, c, :, here] = new[a]
            new_ref[2, c, :, here] = along
            kept = jnp.where(row_id < rows - 1, new[0], 0.0)
            spread = kept - jnp.where(row_id > 0, pltpu.roll(new[0], 1, 0), 0.0)
            left = pltpu.roll(new[1], 1, 1)
            earlier = jnp.where(lane_id > 0, left, 0.0 if j == 0 else before[c])
            before[c] = left
            kept = new[1] if j + 1 < tiles else jnp.where(lane_id < LANES - 1, new[1], 0.0)
            spread = spread + (kept - earlier) + keep * along
            ready_ref[c, :, here] = volume_ref[c, :, here] - rate * (back_ref[c, :, here] - spread)


def finish_kernel(rate_ref, ready_ref, prior_ref, updated_ref):
    rate = rate_ref[0]
    for c in range(ready_ref.shape[0]):
        updated_ref[c] = jnp.maximum(ready_ref[c] - rate * prior_ref[c], 0.0)


def totals_kernel(counts, sums_ref, updated_far, totals_ref):
    total = sums_ref[0]
    for p in range(1, sums_ref.shape[0]):
        total = total + sums_ref[p]
    across = jnp.sum(total, axis=1, keepdims=True)
    for k, count in enumerate(counts):
        totals_ref[k] = across[k, 0] * (1.0 / count)


def picked_blocks(blocks, where, count):
    chosen = (where[:, None] == jnp.arange(count, dtype=jnp.int32)[None, :]).astype(jnp.bfloat16)
    return jnp.einsum("tc,bcj->tbj", chosen, blocks, preferred_element_type=jnp.float32).astype(
        jnp.bfloat16
    )


def gathered_products(products, where, count):
    chosen = (where[:, None] == jnp.arange(count, dtype=jnp.int32)[None, :]).astype(jnp.float32)
    return jnp.einsum("tc,tbj->bcj", chosen, products, precision=lax.Precision.HIGHEST)


def on_device(
    volume_now,
    extrapolated,
    dual_grad,
    dual_data,
    measured,
    projector,
    tile_rows,
    tile_cols,
    dual_step,
    primal_step,
    reg_weight,
):
    f32 = jnp.float32
    dual_rate = dual_step[0]
    channels, slices, row_count, col_count = volume_now.shape
    pixels = row_count * col_count
    rays = dual_data.shape[2]
    edge = projector.shape[1]
    share_count, far_count = lax.axis_size(SHARE), lax.axis_size(FAR)
    slab_count = lax.axis_size("slab")
    total_channels = channels * share_count * far_count
    tiles = col_count // LANES
    held = len(index_pairs) * tiles
    last_slice = lax.axis_index("slab") == slab_count - 1
    images = (channels, row_count, col_count)

    keep = jnp.where(last_slice, 0.0, 1.0).reshape(1)
    image_form = jax.ShapeDtypeStruct(images, f32)

    following = from_behind(extrapolated, "slab", -1)
    sinogram = (channels, rays // edge, edge)
    x_near, duals, own_sums, projector_near = pl.pallas_call(
        own_kernel,
        out_shape=(
            kept_near(images),
            kept_near((3, *images)),
            kept_near((len(own_pairs), row_count, col_count)),
            pltpu.VMEM(projector.shape, projector.dtype),
        ),
        in_specs=[SMEM] + [ANY] * 3,
        out_specs=(VMEM,) * 4,
        scratch_shapes=[pltpu.SemaphoreType.DMA(n) for n in ((2, 4), (8,))],
        compiler_params=SCRATCH,
        name="own",
    )(
        dual_step,
        left_far(extrapolated.reshape(images)),
        left_far(dual_grad.reshape(3, *images)),
        left_far(projector),
    )
    x_near, candidate, partial_gram = pl.pallas_call(
        gram_kernel,
        out_shape=(
            kept_near(images),
            kept_near((3, *images)),
            pltpu.HBM((row_count * held, LANES), f32),
        ),
        in_specs=[SMEM, SMEM, VMEM, VMEM, VMEM, VMEM],
        out_specs=(VMEM, VMEM, ANY),
        scratch_shapes=[
            pltpu.VMEM((row_count * held, LANES), f32),
            pltpu.SemaphoreType.DMA((2,)),
        ],
        input_output_aliases={4: 0, 5: 1},
        compiler_params=SCRATCH,
        name="gram",
    )(
        dual_step,
        keep,
        near(following.reshape(images)),
        near(own_sums),
        near(x_near),
        near(duals),
    )
    share_order = [by_distance(SHARE, (2, 1, 1))]
    far_order = [by_distance((FAR,), (far_count // 2 + 2,))]
    gram_parts = lax.all_to_all(
        partial_gram.reshape(share_count, held, LANES),
        SHARE,
        0,
        0,
        axis_index_groups=share_order,
        tiled=True,
    )

    rounded = x_near.reshape(channels, pixels // edge, edge).astype(jnp.bfloat16)
    picked = picked_blocks(rounded, tile_cols, pixels // edge)
    products = jnp.einsum("tij,tbj->tbi", projector_near, picked, preferred_element_type=f32)
    projected = gathered_products(products, tile_rows, rays // edge)
    residual = projected - measured.reshape(sinogram)
    data_new = (dual_data.reshape(sinogram) + dual_rate * residual) / (1.0 + dual_rate)

    data_low = data_new.astype(jnp.bfloat16)
    picked_back = picked_blocks(data_low, tile_rows, rays // edge)
    products_back = jnp.einsum("tij,tbi->tbj", projector_near, picked_back, preferred_element_type=f32)
    back_proj = gathered_products(products_back, tile_cols, pixels // edge).reshape(
        volume_now.shape
    )
    to_far, back_proj = pl.pallas_call(
        pass_on_kernel,
        out_shape=(
            jax.ShapeDtypeStruct((far_count, held // 2 + 1, 2, LANES), f32),
            kept_near(images),
        ),
        in_specs=[SMEM, VMEM, VMEM, VMEM],
        out_specs=(VMEM, VMEM),
        input_output_aliases={3: 1},
        compiler_params=SCRATCH,
        name="pass_on",
    )(reg_weight, near(gram_parts), near(residual), near(back_proj.reshape(images)))
    far_parts = lax.all_to_all(to_far, FAR, 0, 0, axis_index_groups=far_order, tiled=True)

    to_share = pl.pallas_call(
        functools.partial(factor_kernel, total_channels),
        out_shape=kept_near((share_count, held // 2 + 1, 2, LANES)),
        in_specs=[SMEM, VMEM],
        out_specs=VMEM,
        scratch_shapes=[pltpu.VMEM((held + 2, LANES), f32)],
        compiler_params=SCRATCH,
        name="factor",
    )(reg_weight, near(far_parts))
    factor_rows = lax.all_to_all(
        to_share, SHARE, 0, 0, axis_index_groups=share_order, tiled=True
    )

    new_slice, factor_image_rows, sums = pl.pallas_call(
        slice_kernel,
        out_shape=(
            kept_near(images),
            kept_near((row_count * held, LANES)),
            pltpu.HBM((slab_count, 2, LANES), f32),
        ),
        in_specs=[VMEM, VMEM],
        out_specs=(VMEM, VMEM, ANY),
        scratch_shapes=[
            pltpu.VMEM((slab_count, 2, LANES), f32),
            pltpu.SemaphoreType.DMA(()),
        ],
        compiler_params=SCRATCH,
        name="slice",
    )(near(factor_rows), near(candidate))
    prior_layer = from_behind(new_slice, "slab", 1)
    slab_order = [[0, *range(slab_count // 2, slab_count), *range(1, slab_count // 2)]]
    all_sums = lax.all_to_all(sums, "slab", 0, 0, axis_index_groups=slab_order, tiled=True)
    grad_new, ready, data_out = pl.pallas_call(
        rest_kernel,
        out_shape=(
            jax.ShapeDtypeStruct((3, *images), f32),
            kept_near(images),
            jax.ShapeDtypeStruct(sinogram, f32),
        ),
        in_specs=[SMEM, SMEM] + [VMEM] * 6,
        out_specs=(VMEM, VMEM, VMEM),
        compiler_params=SCRATCH,
        name="rest",
    )(
        primal_step,
        keep,
        near(factor_image_rows),
        near(candidate),
        near(new_slice),
        near(volume_now.reshape(images)),
        near(back_proj),
        near(data_new),
    )
    counts = (total_channels * slab_count * slices * rays, slab_count * slices * pixels)
    updated = pl.pallas_call(
        finish_kernel,
        out_shape=image_form,
        in_specs=[SMEM, VMEM, VMEM],
        out_specs=VMEM,
        compiler_params=SCRATCH,
        name="finish",
    )(primal_step, near(ready), near(prior_layer))
    totals = pl.pallas_call(
        functools.partial(totals_kernel, counts),
        out_shape=jax.ShapeDtypeStruct((2,), f32),
        in_specs=[VMEM, ANY],
        out_specs=SMEM,
        compiler_params=SCRATCH,
        name="totals",
    )(near(all_sums), left_far(updated))
    return (
        updated.reshape(volume_now.shape),
        grad_new.reshape(dual_grad.shape),
        data_out.reshape(dual_data.shape),
        totals,
    )


def solution(mesh):
    torus = Mesh(
        mesh.devices.reshape(4, 2, 8, 2, mesh.shape["slab"]), ("x", "y", "zfar", "znear", "slab")
    )
    placed = (
        P(CHAN, "slab", None, None),
        P(CHAN, "slab", None, None),
        P(None, CHAN, "slab", None, None),
        P(CHAN, "slab", None),
        P(CHAN, "slab", None),
        P(),
        P(),
        P(),
        P(),
        P(),
        P(),
    )
    return jax.shard_map(
        on_device,
        mesh=torus,
        in_specs=placed,
        out_specs=(
            P(CHAN, "slab", None, None),
            P(None, CHAN, "slab", None, None),
            P(CHAN, "slab", None),
            P(),
        ),
        check_vma=False,
    )
```

```python
import functools
import itertools
import math

import jax
import jax.numpy as jnp
from jax import lax
from jax.experimental import pallas as pl
from jax.experimental.pallas import tpu as pltpu
from jax.sharding import Mesh
from jax.sharding import PartitionSpec as P

SWEEPS = 6
CHAN = ("x", "y", "zfar", "znear")
SHARE = ("x", "y", "znear")
FAR = "zfar"
LANES = 128

index_pairs = ((0, 0), (1, 1), (2, 2), (0, 1), (0, 2), (1, 2))
entry_of = {pair: k for k, pair in enumerate(index_pairs)}
sweep_order = ((0, 1), (0, 2), (1, 2))
own_pairs = ((0, 0), (1, 1), (0, 1))

VMEM = pl.BlockSpec(memory_space=pltpu.VMEM)
SMEM = pl.BlockSpec(memory_space=pltpu.SMEM)
ANY = pl.BlockSpec(memory_space=pl.ANY)
SCRATCH = pltpu.CompilerParams(vmem_limit_bytes=6 * 2**20)


def near(array):
    return pltpu.with_memory_space_constraint(array, pltpu.VMEM)


def left_far(array):
    return pltpu.with_memory_space_constraint(array, pltpu.HBM)


def kept_near(shape):
    return pltpu.VMEM(shape, jnp.float32)


def by_distance(axes, first):
    sizes = [lax.axis_size(axis) for axis in axes]
    places = list(itertools.product(*map(range, sizes)))

    def away(place):
        return sum(min((a - b) % n, (b - a) % n) for a, b, n in zip(place, first, sizes))

    order = sorted(range(len(places)), key=lambda i: -away(places[i]))
    order.remove(places.index(first))
    return [places.index(first), *order]


def from_behind(block, axis, distance):
    devices = range(lax.axis_size(axis))
    route = [(i - distance, i) for i in devices if i - distance in devices]
    return lax.ppermute(block, axis, route)


def own_kernel(
    rate_ref,
    x_far,
    dual_far,
    projector_far,
    x_ref,
    cand_ref,
    sums_ref,
    projector_ref,
    arrived,
    projector_arrived,
):
    channels, rows, cols = x_ref.shape
    tiles = cols // LANES
    parts = arrived.shape[1]
    size = channels // parts
    copies = []
    for part in range(parts):
        some = pl.ds(part * size, size)
        copies.append(
            (
                pltpu.make_async_copy(x_far.at[some], x_ref.at[some], arrived.at[0, part]),
                pltpu.make_async_copy(
                    dual_far.at[:, some], cand_ref.at[:, some], arrived.at[1, part]
                ),
            )
        )
        for copy in copies[-1]:
            copy.start()
    projector_copies = []
    pieces = projector_arrived.shape[0]
    size_in = projector_ref.shape[0] // pieces
    for piece in range(pieces):
        some = pl.ds(piece * size_in, size_in)
        projector_copies.append(
            pltpu.make_async_copy(
                projector_far.at[some], projector_ref.at[some], projector_arrived.at[piece]
            )
        )
    for copy in projector_copies:
        copy.start()
    rate = rate_ref[0]
    inner_row = lax.broadcasted_iota(jnp.int32, (rows, LANES), 0) < rows - 1
    edge_lane = lax.broadcasted_iota(jnp.int32, (rows, LANES), 1) == LANES - 1
    for part in range(parts):
        for copy in copies[part]:
            copy.wait()
        for j in range(tiles):
            here = pl.ds(j * LANES, LANES)
            if part:
                sums = [sums_ref[k, :, here] for k in range(len(own_pairs))]
            else:
                sums = [jnp.zeros((rows, LANES), jnp.float32) for _ in own_pairs]
            for c in range(part * size, part * size + size):
                x = x_ref[c, :, here]
                below = pltpu.roll(x, rows - 1, 0)
                right = pltpu.roll(x, LANES - 1, 1)
                if j + 1 < tiles:
                    after = pltpu.roll(x_ref[c, :, pl.ds((j + 1) * LANES, LANES)], LANES - 1, 1)
                else:
                    after = x
                steps = (
                    jnp.where(inner_row, below - x, 0.0),
                    jnp.where(edge_lane, after, right) - x,
                )
                cand = [cand_ref[a, c, :, here] + rate * steps[a] for a in range(2)]
                for a in range(2):
                    cand_ref[a, c, :, here] = cand[a]
                sums = [s + cand[a] * cand[b] for s, (a, b) in zip(sums, own_pairs)]
            for k, s in enumerate(sums):
                sums_ref[k, :, here] = s
    for copy in projector_copies:
        copy.wait()


def gram_kernel(
    rate_ref, keep_ref, next_ref, sums_ref, x_ref, dual_ref, x_same, cand_ref, out_far, out_ref, left
):
    channels, rows, cols = x_ref.shape
    tiles = cols // LANES
    per_row = len(index_pairs) * tiles
    rate = rate_ref[0]
    keep = keep_ref[0]
    parts = left.shape[0]
    size = rows // parts
    copies = []
    for part in range(parts):
        these = pl.ds(part * size, size)
        for j in range(tiles):
            here = pl.ds(j * LANES, LANES)
            sums = {pair: sums_ref[k, these, here] for k, pair in enumerate(own_pairs)}
            for b in range(3):
                sums[b, 2] = jnp.zeros((size, LANES), jnp.float32)
            for c in range(channels):
                step = (next_ref[c, these, here] - x_ref[c, these, here]) * keep
                cand = dual_ref[2, c, these, here] + rate * step
                for b in range(2):
                    sums[b, 2] = sums[b, 2] + dual_ref[b, c, these, here] * cand
                sums[2, 2] = sums[2, 2] + cand * cand
                cand_ref[2, c, these, here] = cand
            for k, pair in enumerate(index_pairs):
                start = part * size * per_row + k * tiles + j
                out_ref[pl.ds(start, size, stride=per_row), :] = sums[pair]
        done = pl.ds(part * size * per_row, size * per_row)
        copies.append(pltpu.make_async_copy(out_ref.at[done], out_far.at[done], left.at[part]))
        copies[-1].start()
    for copy in copies:
        copy.wait()


def pass_on_kernel(weight_ref, parts_ref, residual_ref, back_ref, out_ref, back_same):
    peers, per_row, _ = parts_ref.shape
    copies, pairs, two, _ = out_ref.shape
    total = parts_ref[0]
    for p in range(1, peers):
        total = total + parts_ref[p]
    squares = jnp.zeros((8, LANES), jnp.float32)
    for c in range(residual_ref.shape[0]):
        for start in range(0, residual_ref.shape[1], 8):
            some = residual_ref[c, pl.ds(start, 8), :]
            squares = squares + some * some
    misfit = sum(squares[k : k + two] for k in range(0, 8, two))
    for k in range(pairs):
        pair = total[two * k : two * k + two] if k < per_row // two else misfit
        for p in range(copies):
            out_ref[p, k] = pair


def rotate(entry, vectors, p, q):
    k = 3 - p - q
    pq, kp, kq = (entry_of[tuple(sorted(s))] for s in ((p, q), (k, p), (k, q)))
    across, twice = entry[q] - entry[p], 2.0 * entry[pq]
    square = across * across + twice * twice
    still = square == 0.0
    inverse = lax.rsqrt(jnp.where(still, 1.0, square))
    length = square * inverse
    half = jnp.where(still, 1.0, 0.5 + 0.5 * jnp.abs(across) * inverse)
    root = lax.rsqrt(half)
    large, small = half * root, 0.5 * jnp.abs(twice) * inverse * root
    ahead = across >= 0.0
    cosine = jnp.where(ahead, large, small)
    sine = jnp.where(ahead, small, large)
    sine = jnp.where(twice < 0.0, -sine, sine)
    middle = entry[p] + entry[q]
    entry, vectors = list(entry), [list(row) for row in vectors]
    entry[p], entry[q] = 0.5 * (middle - length), 0.5 * (middle + length)
    entry[pq] = jnp.where(still, entry[pq], 0.0)
    entry[kp], entry[kq] = (
        cosine * entry[kp] - sine * entry[kq],
        sine * entry[kp] + cosine * entry[kq],
    )
    for row in vectors:
        row[p], row[q] = cosine * row[p] - sine * row[q], sine * row[p] + cosine * row[q]
    return entry, vectors


def factor_kernel(channels, weight_ref, parts_ref, out_ref, sums_ref):
    peers, pairs, two, _ = parts_ref.shape
    entries = len(index_pairs)
    tiles = two * (pairs - 1) // entries
    for k in range(pairs):
        pair = parts_ref[0, k]
        for p in range(1, peers):
            pair = pair + parts_ref[p, k]
        sums_ref[pl.ds(two * k, two), :] = pair
    radius = weight_ref[0] * math.sqrt(channels)
    entry = [sums_ref[pl.ds(k * tiles, tiles), :] for k in range(entries)]
    one, zero = jnp.ones_like(entry[0]), jnp.zeros_like(entry[0])
    vectors = [[one if r == c else zero for c in range(3)] for r in range(3)]
    for _ in range(SWEEPS):
        for p, q in sweep_order:
            entry, vectors = rotate(entry, vectors, p, q)
    roots = [jnp.sqrt(jnp.maximum(entry[d], 0.0)) for d in range(3)]
    scales = [radius / jnp.maximum(root, radius) for root in roots]
    excess = sum(jnp.maximum(root - radius, 0.0) for root in roots) / radius
    misfit = sums_ref[pl.ds(entries * tiles, two), :]
    rows = [
        sum(vectors[a][d] * scales[d] * vectors[b][d] for d in range(3)) for a, b in index_pairs
    ]
    last = jnp.concatenate([jnp.sum(part, axis=0, keepdims=True) for part in (misfit, excess)])
    for k in range(pairs):
        row, start = rows[two * k // tiles] if k + 1 < pairs else last, two * k % tiles
        for p in range(out_ref.shape[0]):
            out_ref[p, k] = row[start : start + two]


def factor_image(factor_ref, rows, tiles):
    per_row = factor_ref.shape[0] // rows

    def image(k, j):
        return factor_ref[pl.ds(k * tiles + j, rows, stride=per_row), :]

    return image


def entry_at(a, b):
    return entry_of[tuple(sorted((a, b)))]


def slice_kernel(parts_ref, cand_ref, new_ref, factor_ref, sums_far, sums_ref, left):
    _, channels, rows, cols = cand_ref.shape
    tiles = cols // LANES
    peers, pairs, two, _ = parts_ref.shape
    total = parts_ref[0, pairs - 1]
    for p in range(1, peers):
        total = total + parts_ref[p, pairs - 1]
    for slab in range(sums_ref.shape[0]):
        sums_ref[slab] = total
    copy = pltpu.make_async_copy(sums_ref, sums_far, left)
    copy.start()
    per_row = factor_ref.shape[0] // rows
    for p in range(peers):
        for k in range(pairs - 1):
            factor_ref[pl.ds(p * per_row + two * k, two), :] = parts_ref[p, k]
    image = factor_image(factor_ref, rows, tiles)
    for j in range(tiles):
        here = pl.ds(j * LANES, LANES)
        factor = [image(entry_at(b, 2), j) for b in range(3)]
        for c in range(channels):
            new_ref[c, :, here] = sum(cand_ref[b, c, :, here] * factor[b] for b in range(3))
    copy.wait()


def rest_kernel(
    rate_ref,
    keep_ref,
    factor_ref,
    cand_ref,
    slice_ref,
    volume_ref,
    back_ref,
    data_ref,
    new_ref,
    ready_ref,
    data_out,
):
    _, channels, rows, cols = cand_ref.shape
    tiles = cols // LANES
    rate = rate_ref[0]
    keep = keep_ref[0]
    image = factor_image(factor_ref, rows, tiles)
    data_out[...] = data_ref[...]
    row_id = lax.broadcasted_iota(jnp.int32, (rows, LANES), 0)
    lane_id = lax.broadcasted_iota(jnp.int32, (rows, LANES), 1)
    before = [None] * channels
    for j in range(tiles):
        here = pl.ds(j * LANES, LANES)
        factor = [[image(entry_at(b, a), j) for b in range(3)] for a in range(2)]
        for c in range(channels):
            cand = [cand_ref[b, c, :, here] for b in range(3)]
            new = [sum(cand[b] * factor[a][b] for b in range(3)) for a in range(2)]
            along = slice_ref[c, :, here]
            for a in range(2):
                new_ref[a, c, :, here] = new[a]
            new_ref[2, c, :, here] = along
            kept = jnp.where(row_id < rows - 1, new[0], 0.0)
            spread = kept - jnp.where(row_id > 0, pltpu.roll(new[0], 1, 0), 0.0)
            left = pltpu.roll(new[1], 1, 1)
            earlier = jnp.where(lane_id > 0, left, 0.0 if j == 0 else before[c])
            before[c] = left
            kept = new[1] if j + 1 < tiles else jnp.where(lane_id < LANES - 1, new[1], 0.0)
            spread = spread + (kept - earlier) + keep * along
            ready_ref[c, :, here] = volume_ref[c, :, here] - rate * (back_ref[c, :, here] - spread)


def finish_kernel(rate_ref, ready_ref, prior_ref, updated_ref):
    rate = rate_ref[0]
    for c in range(ready_ref.shape[0]):
        updated_ref[c] = jnp.maximum(ready_ref[c] - rate * prior_ref[c], 0.0)


def totals_kernel(counts, sums_ref, updated_far, totals_ref):
    total = sums_ref[0]
    for p in range(1, sums_ref.shape[0]):
        total = total + sums_ref[p]
    across = jnp.sum(total, axis=1, keepdims=True)
    for k, count in enumerate(counts):
        totals_ref[k] = across[k, 0] * (1.0 / count)


def picked_blocks(blocks, where, count):
    chosen = (where[:, None] == jnp.arange(count, dtype=jnp.int32)[None, :]).astype(jnp.bfloat16)
    return jnp.einsum("tc,bcj->tbj", chosen, blocks, preferred_element_type=jnp.float32).astype(
        jnp.bfloat16
    )


def gathered_products(products, where, count):
    chosen = (where[:, None] == jnp.arange(count, dtype=jnp.int32)[None, :]).astype(jnp.float32)
    return jnp.einsum("tc,tbj->bcj", chosen, products, precision=lax.Precision.HIGHEST)


def on_device(
    volume_now,
    extrapolated,
    dual_grad,
    dual_data,
    measured,
    projector,
    tile_rows,
    tile_cols,
    dual_step,
    primal_step,
    reg_weight,
):
    f32 = jnp.float32
    dual_rate = dual_step[0]
    channels, slices, row_count, col_count = volume_now.shape
    pixels = row_count * col_count
    rays = dual_data.shape[2]
    edge = projector.shape[1]
    share_count, far_count = lax.axis_size(SHARE), lax.axis_size(FAR)
    slab_count = lax.axis_size("slab")
    total_channels = channels * share_count * far_count
    tiles = col_count // LANES
    held = len(index_pairs) * tiles
    last_slice = lax.axis_index("slab") == slab_count - 1
    images = (channels, row_count, col_count)

    keep = jnp.where(last_slice, 0.0, 1.0).reshape(1)
    image_form = jax.ShapeDtypeStruct(images, f32)

    following = from_behind(extrapolated, "slab", -1)
    sinogram = (channels, rays // edge, edge)
    x_near, duals, own_sums, projector_near = pl.pallas_call(
        own_kernel,
        out_shape=(
            kept_near(images),
            kept_near((3, *images)),
            kept_near((len(own_pairs), row_count, col_count)),
            pltpu.VMEM(projector.shape, projector.dtype),
        ),
        in_specs=[SMEM] + [ANY] * 3,
        out_specs=(VMEM,) * 4,
        scratch_shapes=[pltpu.SemaphoreType.DMA(n) for n in ((2, 4), (8,))],
        compiler_params=SCRATCH,
        name="own",
    )(
        dual_step,
        left_far(extrapolated.reshape(images)),
        left_far(dual_grad.reshape(3, *images)),
        left_far(projector),
    )
    x_near, candidate, partial_gram = pl.pallas_call(
        gram_kernel,
        out_shape=(
            kept_near(images),
            kept_near((3, *images)),
            pltpu.HBM((row_count * held, LANES), f32),
        ),
        in_specs=[SMEM, SMEM, VMEM, VMEM, VMEM, VMEM],
        out_specs=(VMEM, VMEM, ANY),
        scratch_shapes=[
            pltpu.VMEM((row_count * held, LANES), f32),
            pltpu.SemaphoreType.DMA((2,)),
        ],
        input_output_aliases={4: 0, 5: 1},
        compiler_params=SCRATCH,
        name="gram",
    )(
        dual_step,
        keep,
        near(following.reshape(images)),
        near(own_sums),
        near(x_near),
        near(duals),
    )
    share_order = [by_distance(SHARE, (2, 1, 1))]
    far_order = [by_distance((FAR,), (far_count // 2,))]
    gram_parts = lax.all_to_all(
        partial_gram.reshape(share_count, held, LANES),
        SHARE,
        0,
        0,
        axis_index_groups=share_order,
        tiled=True,
    )

    rounded = x_near.reshape(channels, pixels // edge, edge).astype(jnp.bfloat16)
    picked = picked_blocks(rounded, tile_cols, pixels // edge)
    products = jnp.einsum("tij,tbj->tbi", projector_near, picked, preferred_element_type=f32)
    projected = gathered_products(products, tile_rows, rays // edge)
    residual = projected - measured.reshape(sinogram)
    data_new = (dual_data.reshape(sinogram) + dual_rate * residual) / (1.0 + dual_rate)

    data_low = data_new.astype(jnp.bfloat16)
    picked_back = picked_blocks(data_low, tile_rows, rays // edge)
    products_back = jnp.einsum("tij,tbi->tbj", projector_near, picked_back, preferred_element_type=f32)
    back_proj = gathered_products(products_back, tile_cols, pixels // edge).reshape(
        volume_now.shape
    )
    to_far, back_proj = pl.pallas_call(
        pass_on_kernel,
        out_shape=(
            jax.ShapeDtypeStruct((far_count, held // 2 + 1, 2, LANES), f32),
            kept_near(images),
        ),
        in_specs=[SMEM, VMEM, VMEM, VMEM],
        out_specs=(VMEM, VMEM),
        input_output_aliases={3: 1},
        compiler_params=SCRATCH,
        name="pass_on",
    )(reg_weight, near(gram_parts), near(residual), near(back_proj.reshape(images)))
    far_parts = lax.all_to_all(to_far, FAR, 0, 0, axis_index_groups=far_order, tiled=True)

    to_share = pl.pallas_call(
        functools.partial(factor_kernel, total_channels),
        out_shape=kept_near((share_count, held // 2 + 1, 2, LANES)),
        in_specs=[SMEM, VMEM],
        out_specs=VMEM,
        scratch_shapes=[pltpu.VMEM((held + 2, LANES), f32)],
        compiler_params=SCRATCH,
        name="factor",
    )(reg_weight, near(far_parts))
    factor_rows = lax.all_to_all(
        to_share, SHARE, 0, 0, axis_index_groups=share_order, tiled=True
    )

    new_slice, factor_image_rows, sums = pl.pallas_call(
        slice_kernel,
        out_shape=(
            kept_near(images),
            kept_near((row_count * held, LANES)),
            pltpu.HBM((slab_count, 2, LANES), f32),
        ),
        in_specs=[VMEM, VMEM],
        out_specs=(VMEM, VMEM, ANY),
        scratch_shapes=[
            pltpu.VMEM((slab_count, 2, LANES), f32),
            pltpu.SemaphoreType.DMA(()),
        ],
        compiler_params=SCRATCH,
        name="slice",
    )(near(factor_rows), near(candidate))
    prior_layer = from_behind(new_slice, "slab", 1)
    slab_order = [[0, *range(slab_count // 2, slab_count), *range(1, slab_count // 2)]]
    all_sums = lax.all_to_all(sums, "slab", 0, 0, axis_index_groups=slab_order, tiled=True)
    grad_new, ready, data_out = pl.pallas_call(
        rest_kernel,
        out_shape=(
            jax.ShapeDtypeStruct((3, *images), f32),
            kept_near(images),
            jax.ShapeDtypeStruct(sinogram, f32),
        ),
        in_specs=[SMEM, SMEM] + [VMEM] * 6,
        out_specs=(VMEM, VMEM, VMEM),
        compiler_params=SCRATCH,
        name="rest",
    )(
        primal_step,
        keep,
        near(factor_image_rows),
        near(candidate),
        near(new_slice),
        near(volume_now.reshape(images)),
        near(back_proj),
        near(data_new),
    )
    counts = (total_channels * slab_count * slices * rays, slab_count * slices * pixels)
    updated = pl.pallas_call(
        finish_kernel,
        out_shape=image_form,
        in_specs=[SMEM, VMEM, VMEM],
        out_specs=VMEM,
        compiler_params=SCRATCH,
        name="finish",
    )(primal_step, near(ready), near(prior_layer))
    totals = pl.pallas_call(
        functools.partial(totals_kernel, counts),
        out_shape=jax.ShapeDtypeStruct((2,), f32),
        in_specs=[VMEM, ANY],
        out_specs=SMEM,
        compiler_params=SCRATCH,
        name="totals",
    )(near(all_sums), left_far(updated))
    return (
        updated.reshape(volume_now.shape),
        grad_new.reshape(dual_grad.shape),
        data_out.reshape(dual_data.shape),
        totals,
    )


def solution(mesh):
    torus = Mesh(
        mesh.devices.reshape(4, 2, 8, 2, mesh.shape["slab"]), ("x", "y", "zfar", "znear", "slab")
    )
    placed = (
        P(CHAN, "slab", None, None),
        P(CHAN, "slab", None, None),
        P(None, CHAN, "slab", None, None),
        P(CHAN, "slab", None),
        P(CHAN, "slab", None),
        P(),
        P(),
        P(),
        P(),
        P(),
        P(),
    )
    return jax.shard_map(
        on_device,
        mesh=torus,
        in_specs=placed,
        out_specs=(
            P(CHAN, "slab", None, None),
            P(None, CHAN, "slab", None, None),
            P(CHAN, "slab", None),
            P(),
        ),
        check_vma=False,
    )
```

```python
import functools
import itertools
import math

import jax
import jax.numpy as jnp
from jax import lax
from jax.experimental import pallas as pl
from jax.experimental.pallas import tpu as pltpu
from jax.sharding import Mesh
from jax.sharding import PartitionSpec as P

SWEEPS = 6
CHAN = ("x", "y", "zfar", "znear")
SHARE = ("x", "y", "znear")
FAR = "zfar"
LANES = 128

index_pairs = ((0, 0), (1, 1), (2, 2), (0, 1), (0, 2), (1, 2))
entry_of = {pair: k for k, pair in enumerate(index_pairs)}
sweep_order = ((0, 1), (0, 2), (1, 2))
own_pairs = ((0, 0), (1, 1), (0, 1))

VMEM = pl.BlockSpec(memory_space=pltpu.VMEM)
SMEM = pl.BlockSpec(memory_space=pltpu.SMEM)
ANY = pl.BlockSpec(memory_space=pl.ANY)
SCRATCH = pltpu.CompilerParams(vmem_limit_bytes=6 * 2**20)


def near(array):
    return pltpu.with_memory_space_constraint(array, pltpu.VMEM)


def left_far(array):
    return pltpu.with_memory_space_constraint(array, pltpu.HBM)


def kept_near(shape):
    return pltpu.VMEM(shape, jnp.float32)


def by_distance(axes, first):
    sizes = [lax.axis_size(axis) for axis in axes]
    places = list(itertools.product(*map(range, sizes)))

    def away(place):
        return sum(min((a - b) % n, (b - a) % n) for a, b, n in zip(place, first, sizes))

    order = sorted(range(len(places)), key=lambda i: -away(places[i]))
    order.remove(places.index(first))
    return [places.index(first), *order]


def from_behind(block, axis, distance):
    devices = range(lax.axis_size(axis))
    route = [(i - distance, i) for i in devices if i - distance in devices]
    return lax.ppermute(block, axis, route)


def own_kernel(
    rate_ref,
    x_far,
    dual_far,
    projector_far,
    x_ref,
    cand_ref,
    sums_ref,
    projector_ref,
    arrived,
    projector_arrived,
):
    channels, rows, cols = x_ref.shape
    tiles = cols // LANES
    parts = arrived.shape[1]
    size = channels // parts
    copies = []
    for part in range(parts):
        some = pl.ds(part * size, size)
        copies.append(
            (
                pltpu.make_async_copy(x_far.at[some], x_ref.at[some], arrived.at[0, part]),
                pltpu.make_async_copy(
                    dual_far.at[:, some], cand_ref.at[:, some], arrived.at[1, part]
                ),
            )
        )
        for copy in copies[-1]:
            copy.start()
    projector_copies = []
    pieces = projector_arrived.shape[0]
    size_in = projector_ref.shape[0] // pieces
    for piece in range(pieces):
        some = pl.ds(piece * size_in, size_in)
        projector_copies.append(
            pltpu.make_async_copy(
                projector_far.at[some], projector_ref.at[some], projector_arrived.at[piece]
            )
        )
    for copy in projector_copies:
        copy.start()
    rate = rate_ref[0]
    inner_row = lax.broadcasted_iota(jnp.int32, (rows, LANES), 0) < rows - 1
    edge_lane = lax.broadcasted_iota(jnp.int32, (rows, LANES), 1) == LANES - 1
    for part in range(parts):
        for copy in copies[part]:
            copy.wait()
        for j in range(tiles):
            here = pl.ds(j * LANES, LANES)
            if part:
                sums = [sums_ref[k, :, here] for k in range(len(own_pairs))]
            else:
                sums = [jnp.zeros((rows, LANES), jnp.float32) for _ in own_pairs]
            for c in range(part * size, part * size + size):
                x = x_ref[c, :, here]
                below = pltpu.roll(x, rows - 1, 0)
                right = pltpu.roll(x, LANES - 1, 1)
                if j + 1 < tiles:
                    after = pltpu.roll(x_ref[c, :, pl.ds((j + 1) * LANES, LANES)], LANES - 1, 1)
                else:
                    after = x
                steps = (
                    jnp.where(inner_row, below - x, 0.0),
                    jnp.where(edge_lane, after, right) - x,
                )
                cand = [cand_ref[a, c, :, here] + rate * steps[a] for a in range(2)]
                for a in range(2):
                    cand_ref[a, c, :, here] = cand[a]
                sums = [s + cand[a] * cand[b] for s, (a, b) in zip(sums, own_pairs)]
            for k, s in enumerate(sums):
                sums_ref[k, :, here] = s
    for copy in projector_copies:
        copy.wait()


def gram_kernel(
    rate_ref, keep_ref, next_ref, sums_ref, x_ref, dual_ref, x_same, cand_ref, out_far, out_ref, left
):
    channels, rows, cols = x_ref.shape
    tiles = cols // LANES
    per_row = len(index_pairs) * tiles
    rate = rate_ref[0]
    keep = keep_ref[0]
    parts = left.shape[0]
    size = rows // parts
    copies = []
    for part in range(parts):
        these = pl.ds(part * size, size)
        for j in range(tiles):
            here = pl.ds(j * LANES, LANES)
            sums = {pair: sums_ref[k, these, here] for k, pair in enumerate(own_pairs)}
            for b in range(3):
                sums[b, 2] = jnp.zeros((size, LANES), jnp.float32)
            for c in range(channels):
                step = (next_ref[c, these, here] - x_ref[c, these, here]) * keep
                cand = dual_ref[2, c, these, here] + rate * step
                for b in range(2):
                    sums[b, 2] = sums[b, 2] + dual_ref[b, c, these, here] * cand
                sums[2, 2] = sums[2, 2] + cand * cand
                cand_ref[2, c, these, here] = cand
            for k, pair in enumerate(index_pairs):
                start = part * size * per_row + k * tiles + j
                out_ref[pl.ds(start, size, stride=per_row), :] = sums[pair]
        done = pl.ds(part * size * per_row, size * per_row)
        copies.append(pltpu.make_async_copy(out_ref.at[done], out_far.at[done], left.at[part]))
        copies[-1].start()
    for copy in copies:
        copy.wait()


def pass_on_kernel(weight_ref, parts_ref, residual_ref, back_ref, out_ref, back_same):
    peers, per_row, _ = parts_ref.shape
    copies, pairs, two, _ = out_ref.shape
    total = parts_ref[0]
    for p in range(1, peers):
        total = total + parts_ref[p]
    squares = jnp.zeros((8, LANES), jnp.float32)
    for c in range(residual_ref.shape[0]):
        for start in range(0, residual_ref.shape[1], 8):
            some = residual_ref[c, pl.ds(start, 8), :]
            squares = squares + some * some
    misfit = sum(squares[k : k + two] for k in range(0, 8, two))
    for k in range(pairs):
        pair = total[two * k : two * k + two] if k < per_row // two else misfit
        for p in range(copies):
            out_ref[p, k] = pair


def rotate(entry, vectors, p, q):
    k = 3 - p - q
    pq, kp, kq = (entry_of[tuple(sorted(s))] for s in ((p, q), (k, p), (k, q)))
    across, twice = entry[q] - entry[p], 2.0 * entry[pq]
    square = across * across + twice * twice
    still = square == 0.0
    inverse = lax.rsqrt(jnp.where(still, 1.0, square))
    length = square * inverse
    half = jnp.where(still, 1.0, 0.5 + 0.5 * jnp.abs(across) * inverse)
    root = lax.rsqrt(half)
    large, small = half * root, 0.5 * jnp.abs(twice) * inverse * root
    ahead = across >= 0.0
    cosine = jnp.where(ahead, large, small)
    sine = jnp.where(ahead, small, large)
    sine = jnp.where(twice < 0.0, -sine, sine)
    middle = entry[p] + entry[q]
    entry, vectors = list(entry), [list(row) for row in vectors]
    entry[p], entry[q] = 0.5 * (middle - length), 0.5 * (middle + length)
    entry[pq] = jnp.where(still, entry[pq], 0.0)
    entry[kp], entry[kq] = (
        cosine * entry[kp] - sine * entry[kq],
        sine * entry[kp] + cosine * entry[kq],
    )
    for row in vectors:
        row[p], row[q] = cosine * row[p] - sine * row[q], sine * row[p] + cosine * row[q]
    return entry, vectors


def factor_kernel(channels, weight_ref, parts_ref, out_ref, sums_ref):
    peers, pairs, two, _ = parts_ref.shape
    entries = len(index_pairs)
    tiles = two * (pairs - 1) // entries
    for k in range(pairs):
        pair = parts_ref[0, k]
        for p in range(1, peers):
            pair = pair + parts_ref[p, k]
        sums_ref[pl.ds(two * k, two), :] = pair
    radius = weight_ref[0] * math.sqrt(channels)
    entry = [sums_ref[pl.ds(k * tiles, tiles), :] for k in range(entries)]
    one, zero = jnp.ones_like(entry[0]), jnp.zeros_like(entry[0])
    vectors = [[one if r == c else zero for c in range(3)] for r in range(3)]
    for _ in range(SWEEPS):
        for p, q in sweep_order:
            entry, vectors = rotate(entry, vectors, p, q)
    roots = [jnp.sqrt(jnp.maximum(entry[d], 0.0)) for d in range(3)]
    scales = [radius / jnp.maximum(root, radius) for root in roots]
    excess = sum(jnp.maximum(root - radius, 0.0) for root in roots) / radius
    misfit = sums_ref[pl.ds(entries * tiles, two), :]
    rows = [
        sum(vectors[a][d] * scales[d] * vectors[b][d] for d in range(3)) for a, b in index_pairs
    ]
    last = jnp.concatenate([jnp.sum(part, axis=0, keepdims=True) for part in (misfit, excess)])
    for k in range(pairs):
        row, start = rows[two * k // tiles] if k + 1 < pairs else last, two * k % tiles
        for p in range(out_ref.shape[0]):
            out_ref[p, k] = row[start : start + two]


def factor_image(factor_ref, rows, tiles):
    per_row = factor_ref.shape[0] // rows

    def image(k, j):
        return factor_ref[pl.ds(k * tiles + j, rows, stride=per_row), :]

    return image


def entry_at(a, b):
    return entry_of[tuple(sorted((a, b)))]


def slice_kernel(parts_ref, cand_ref, new_ref, factor_ref, sums_far, sums_ref, left):
    _, channels, rows, cols = cand_ref.shape
    tiles = cols // LANES
    peers, pairs, two, _ = parts_ref.shape
    total = parts_ref[0, pairs - 1]
    for p in range(1, peers):
        total = total + parts_ref[p, pairs - 1]
    for slab in range(sums_ref.shape[0]):
        sums_ref[slab] = total
    copy = pltpu.make_async_copy(sums_ref, sums_far, left)
    copy.start()
    per_row = factor_ref.shape[0] // rows
    for p in range(peers):
        for k in range(pairs - 1):
            factor_ref[pl.ds(p * per_row + two * k, two), :] = parts_ref[p, k]
    image = factor_image(factor_ref, rows, tiles)
    for j in range(tiles):
        here = pl.ds(j * LANES, LANES)
        factor = [image(entry_at(b, 2), j) for b in range(3)]
        for c in range(channels):
            new_ref[c, :, here] = sum(cand_ref[b, c, :, here] * factor[b] for b in range(3))
    copy.wait()


def rest_kernel(
    rate_ref,
    keep_ref,
    factor_ref,
    cand_ref,
    slice_ref,
    volume_ref,
    back_ref,
    data_ref,
    new_ref,
    ready_ref,
    data_out,
):
    _, channels, rows, cols = cand_ref.shape
    tiles = cols // LANES
    rate = rate_ref[0]
    keep = keep_ref[0]
    image = factor_image(factor_ref, rows, tiles)
    data_out[...] = data_ref[...]
    row_id = lax.broadcasted_iota(jnp.int32, (rows, LANES), 0)
    lane_id = lax.broadcasted_iota(jnp.int32, (rows, LANES), 1)
    before = [None] * channels
    for j in range(tiles):
        here = pl.ds(j * LANES, LANES)
        factor = [[image(entry_at(b, a), j) for b in range(3)] for a in range(2)]
        for c in range(channels):
            cand = [cand_ref[b, c, :, here] for b in range(3)]
            new = [sum(cand[b] * factor[a][b] for b in range(3)) for a in range(2)]
            along = slice_ref[c, :, here]
            for a in range(2):
                new_ref[a, c, :, here] = new[a]
            new_ref[2, c, :, here] = along
            kept = jnp.where(row_id < rows - 1, new[0], 0.0)
            spread = kept - jnp.where(row_id > 0, pltpu.roll(new[0], 1, 0), 0.0)
            left = pltpu.roll(new[1], 1, 1)
            earlier = jnp.where(lane_id > 0, left, 0.0 if j == 0 else before[c])
            before[c] = left
            kept = new[1] if j + 1 < tiles else jnp.where(lane_id < LANES - 1, new[1], 0.0)
            spread = spread + (kept - earlier) + keep * along
            ready_ref[c, :, here] = volume_ref[c, :, here] - rate * (back_ref[c, :, here] - spread)


def finish_kernel(rate_ref, ready_ref, prior_ref, updated_ref):
    rate = rate_ref[0]
    for c in range(ready_ref.shape[0]):
        updated_ref[c] = jnp.maximum(ready_ref[c] - rate * prior_ref[c], 0.0)


def totals_kernel(counts, sums_ref, updated_far, totals_ref):
    total = sums_ref[0]
    for p in range(1, sums_ref.shape[0]):
        total = total + sums_ref[p]
    across = jnp.sum(total, axis=1, keepdims=True)
    for k, count in enumerate(counts):
        totals_ref[k] = across[k, 0] * (1.0 / count)


def picked_blocks(blocks, where, count):
    chosen = (where[:, None] == jnp.arange(count, dtype=jnp.int32)[None, :]).astype(jnp.bfloat16)
    return jnp.einsum("tc,bcj->tbj", chosen, blocks, preferred_element_type=jnp.float32).astype(
        jnp.bfloat16
    )


def gathered_products(products, where, count):
    chosen = (where[:, None] == jnp.arange(count, dtype=jnp.int32)[None, :]).astype(jnp.float32)
    return jnp.einsum("tc,tbj->bcj", chosen, products, precision=lax.Precision.HIGHEST)


def on_device(
    volume_now,
    extrapolated,
    dual_grad,
    dual_data,
    measured,
    projector,
    tile_rows,
    tile_cols,
    dual_step,
    primal_step,
    reg_weight,
):
    f32 = jnp.float32
    dual_rate = dual_step[0]
    channels, slices, row_count, col_count = volume_now.shape
    pixels = row_count * col_count
    rays = dual_data.shape[2]
    edge = projector.shape[1]
    share_count, far_count = lax.axis_size(SHARE), lax.axis_size(FAR)
    slab_count = lax.axis_size("slab")
    total_channels = channels * share_count * far_count
    tiles = col_count // LANES
    held = len(index_pairs) * tiles
    last_slice = lax.axis_index("slab") == slab_count - 1
    images = (channels, row_count, col_count)

    keep = jnp.where(last_slice, 0.0, 1.0).reshape(1)
    image_form = jax.ShapeDtypeStruct(images, f32)

    following = from_behind(extrapolated, "slab", -1)
    sinogram = (channels, rays // edge, edge)
    x_near, duals, own_sums, projector_near = pl.pallas_call(
        own_kernel,
        out_shape=(
            kept_near(images),
            kept_near((3, *images)),
            kept_near((len(own_pairs), row_count, col_count)),
            pltpu.VMEM(projector.shape, projector.dtype),
        ),
        in_specs=[SMEM] + [ANY] * 3,
        out_specs=(VMEM,) * 4,
        scratch_shapes=[pltpu.SemaphoreType.DMA(n) for n in ((2, 4), (8,))],
        compiler_params=SCRATCH,
        name="own",
    )(
        dual_step,
        left_far(extrapolated.reshape(images)),
        left_far(dual_grad.reshape(3, *images)),
        left_far(projector),
    )
    x_near, candidate, partial_gram = pl.pallas_call(
        gram_kernel,
        out_shape=(
            kept_near(images),
            kept_near((3, *images)),
            pltpu.HBM((row_count * held, LANES), f32),
        ),
        in_specs=[SMEM, SMEM, VMEM, VMEM, VMEM, VMEM],
        out_specs=(VMEM, VMEM, ANY),
        scratch_shapes=[
            pltpu.VMEM((row_count * held, LANES), f32),
            pltpu.SemaphoreType.DMA((2,)),
        ],
        input_output_aliases={4: 0, 5: 1},
        compiler_params=SCRATCH,
        name="gram",
    )(
        dual_step,
        keep,
        near(following.reshape(images)),
        near(own_sums),
        near(x_near),
        near(duals),
    )
    share_order = [by_distance(SHARE, (2, 1, 1))]
    far_order = [[(far_count // 2 + 1 + i) % far_count for i in range(far_count)]]
    gram_parts = lax.all_to_all(
        partial_gram.reshape(share_count, held, LANES),
        SHARE,
        0,
        0,
        axis_index_groups=share_order,
        tiled=True,
    )

    rounded = x_near.reshape(channels, pixels // edge, edge).astype(jnp.bfloat16)
    picked = picked_blocks(rounded, tile_cols, pixels // edge)
    products = jnp.einsum("tij,tbj->tbi", projector_near, picked, preferred_element_type=f32)
    projected = gathered_products(products, tile_rows, rays // edge)
    residual = projected - measured.reshape(sinogram)
    data_new = (dual_data.reshape(sinogram) + dual_rate * residual) / (1.0 + dual_rate)

    data_low = data_new.astype(jnp.bfloat16)
    picked_back = picked_blocks(data_low, tile_rows, rays // edge)
    products_back = jnp.einsum("tij,tbi->tbj", projector_near, picked_back, preferred_element_type=f32)
    back_proj = gathered_products(products_back, tile_cols, pixels // edge).reshape(
        volume_now.shape
    )
    to_far, back_proj = pl.pallas_call(
        pass_on_kernel,
        out_shape=(
            jax.ShapeDtypeStruct((far_count, held // 2 + 1, 2, LANES), f32),
            kept_near(images),
        ),
        in_specs=[SMEM, VMEM, VMEM, VMEM],
        out_specs=(VMEM, VMEM),
        input_output_aliases={3: 1},
        compiler_params=SCRATCH,
        name="pass_on",
    )(reg_weight, near(gram_parts), near(residual), near(back_proj.reshape(images)))
    far_parts = lax.all_to_all(to_far, FAR, 0, 0, axis_index_groups=far_order, tiled=True)

    to_share = pl.pallas_call(
        functools.partial(factor_kernel, total_channels),
        out_shape=kept_near((share_count, held // 2 + 1, 2, LANES)),
        in_specs=[SMEM, VMEM],
        out_specs=VMEM,
        scratch_shapes=[pltpu.VMEM((held + 2, LANES), f32)],
        compiler_params=SCRATCH,
        name="factor",
    )(reg_weight, near(far_parts))
    factor_rows = lax.all_to_all(
        to_share, SHARE, 0, 0, axis_index_groups=share_order, tiled=True
    )

    new_slice, factor_image_rows, sums = pl.pallas_call(
        slice_kernel,
        out_shape=(
            kept_near(images),
            kept_near((row_count * held, LANES)),
            pltpu.HBM((slab_count, 2, LANES), f32),
        ),
        in_specs=[VMEM, VMEM],
        out_specs=(VMEM, VMEM, ANY),
        scratch_shapes=[
            pltpu.VMEM((slab_count, 2, LANES), f32),
            pltpu.SemaphoreType.DMA(()),
        ],
        compiler_params=SCRATCH,
        name="slice",
    )(near(factor_rows), near(candidate))
    prior_layer = from_behind(new_slice, "slab", 1)
    slab_order = [[0, *range(slab_count // 2, slab_count), *range(1, slab_count // 2)]]
    all_sums = lax.all_to_all(sums, "slab", 0, 0, axis_index_groups=slab_order, tiled=True)
    grad_new, ready, data_out = pl.pallas_call(
        rest_kernel,
        out_shape=(
            jax.ShapeDtypeStruct((3, *images), f32),
            kept_near(images),
            jax.ShapeDtypeStruct(sinogram, f32),
        ),
        in_specs=[SMEM, SMEM] + [VMEM] * 6,
        out_specs=(VMEM, VMEM, VMEM),
        compiler_params=SCRATCH,
        name="rest",
    )(
        primal_step,
        keep,
        near(factor_image_rows),
        near(candidate),
        near(new_slice),
        near(volume_now.reshape(images)),
        near(back_proj),
        near(data_new),
    )
    counts = (total_channels * slab_count * slices * rays, slab_count * slices * pixels)
    updated = pl.pallas_call(
        finish_kernel,
        out_shape=image_form,
        in_specs=[SMEM, VMEM, VMEM],
        out_specs=VMEM,
        compiler_params=SCRATCH,
        name="finish",
    )(primal_step, near(ready), near(prior_layer))
    totals = pl.pallas_call(
        functools.partial(totals_kernel, counts),
        out_shape=jax.ShapeDtypeStruct((2,), f32),
        in_specs=[VMEM, ANY],
        out_specs=SMEM,
        compiler_params=SCRATCH,
        name="totals",
    )(near(all_sums), left_far(updated))
    return (
        updated.reshape(volume_now.shape),
        grad_new.reshape(dual_grad.shape),
        data_out.reshape(dual_data.shape),
        totals,
    )


def solution(mesh):
    torus = Mesh(
        mesh.devices.reshape(4, 2, 8, 2, mesh.shape["slab"]), ("x", "y", "zfar", "znear", "slab")
    )
    placed = (
        P(CHAN, "slab", None, None),
        P(CHAN, "slab", None, None),
        P(None, CHAN, "slab", None, None),
        P(CHAN, "slab", None),
        P(CHAN, "slab", None),
        P(),
        P(),
        P(),
        P(),
        P(),
        P(),
    )
    return jax.shard_map(
        on_device,
        mesh=torus,
        in_specs=placed,
        out_specs=(
            P(CHAN, "slab", None, None),
            P(None, CHAN, "slab", None, None),
            P(CHAN, "slab", None),
            P(),
        ),
        check_vma=False,
    )
```
